32 devices in a mesh: rep: 2 (over core), ctx: 4 (over z), tp: 4 (over y, x).
Axes of the slice: x: 2, y: 2, z: 4, core: 2. Of those that a mesh axis runs over, the one named last changes fastest.
Arguments:
- q_mr: bfloat16 [2048, 8192], P(('rep', 'ctx'), 'tp'), parts along dimension 0, may hold values from -6 to 6
- k_mr: bfloat16 [2048, 8192], P(('rep', 'ctx'), 'tp'), parts along dimension 0, may hold values from -6 to 6
- v_mr: bfloat16 [2048, 8192], P(('rep', 'ctx'), 'tp'), parts along dimension 0, may hold values from -6 to 6
- q_li: bfloat16 [2048, 8192], P(('rep', 'ctx'), 'tp'), parts along dimension 0, may hold values from -6 to 6
- k_li: bfloat16 [2048, 8192], P(('rep', 'ctx'), 'tp'), parts along dimension 0, may hold values from -6 to 6
- mr_taps: bfloat16 [512, 128], P('tp'), may hold values from -0.5 to 0.5
- li_rate: float32 [512, 16], P('tp'), may hold values from 0 to 0.0625, as said below
- li_residue: float32 [512, 16], P('tp'), may hold values from -1.5 to 1.5
Outputs:
- mr_out: bfloat16 [2048, 8192], P(('rep', 'ctx'), 'tp'), parts along dimension 0
- li_out: bfloat16 [2048, 8192], P(('rep', 'ctx'), 'tp'), parts along dimension 0
The draws below stay inside these ranges and needn't reach their ends.
There are 2 independent parts, one for each index of `rep`. The reference program is written for one: setup_inputs(seed, part) draws one part's arguments, and reference() takes and returns one part's arrays. A program takes and returns all parts, laid end to end along the dimension named above; an argument that names none is the same for every part. Nothing has to cross between parts.
Inputs may be any that keep to these rules, and one draw needn't show every extreme that they name: `li_rate`: positive decay rates per position.
All inputs are finite; a program needn't handle non-finite values.
Results may differ from the reference program's by a relative error of at most 0.013.
Values may be sent and summed in bfloat16 or wider, within the bound.
No kernel may reach another device: no remote copies, remote signals or barrier semaphores. Data moves between devices by JAX's collectives and lax.ppermute only.
A program may use at most 128 MiB of HBM per device.

```python
import jax
import jax.numpy as jnp
from jax import lax

D = 8192
GROUPS = 512
POLES = 16
MR_LEN = 128
TOK_DEV = 256
SEQ = 1024
N_CTX = 4


def draw_li_rate(key, part):
    key_mix, key_slow, key_fast = jax.random.split(jax.random.fold_in(key, 17), 3)
    chooser = jax.random.randint(key_mix, (GROUPS, POLES), 0, 10)
    slow_u = jax.random.uniform(key_slow, (GROUPS, POLES), jnp.float32)
    fast_u = jax.random.uniform(key_fast, (GROUPS, POLES), jnp.float32)
    edge_rate = 2.3 / SEQ
    low_rate = 0.3 / SEQ
    cut_level = 5
    slow_rate = low_rate * jnp.exp(slow_u * jnp.log(edge_rate / low_rate))
    fast_rate = edge_rate * jnp.exp(fast_u * jnp.log(0.0625 / edge_rate))
    return jnp.where(chooser < cut_level, slow_rate, fast_rate).astype(jnp.float32)


def level_of(stream_key, extent, cuts, low, largest):
    def one(axis_at, parts):
        steps = jax.random.uniform(jax.random.fold_in(jax.random.fold_in(stream_key, 6), axis_at), (parts,), jnp.float32, low / len(cuts), largest / len(cuts))
        return jnp.repeat(jnp.exp(steps), extent[axis_at] // parts).reshape((-1,) + (1,) * (len(extent) - axis_at - 1))

    factor_of = one(*cuts[0])
    for cut in cuts[1:]:
        factor_of = factor_of * one(*cut)
    return factor_of


def centred(own_key, dims, spread, reach, cuts=(), held_as=jnp.bfloat16):
    entries = jax.random.normal(own_key, dims, jnp.float32) * spread
    if len(cuts) > 0:
        entries = level_of(own_key, dims, cuts, -0.22, 0.18) * entries
    return jnp.clip(entries, min=-reach, max=reach).astype(held_as)


def setup_inputs(seed: int = 0, part: int = 0) -> dict:
    splits = jax.random.split(jax.random.key(seed), 9)
    own_keys = jax.random.split(jax.random.fold_in(splits[8], part), 9)
    q_mr = centred(own_keys[0], (SEQ, D), 1.0, 6.0, ((0, 4), (1, 4)))
    k_mr = centred(own_keys[1], (SEQ, D), 1.0, 6.0, ((0, 4), (1, 4)))
    v_mr = centred(own_keys[2], (SEQ, D), 1.0, 6.0, ((0, 4), (1, 4)))
    q_li = centred(own_keys[3], (SEQ, D), 1.0, 6.0, ((0, 4), (1, 4)))
    k_li = centred(own_keys[4], (SEQ, D), 1.0, 6.0, ((0, 4), (1, 4)))
    mr_taps = centred(splits[5], (GROUPS, MR_LEN), MR_LEN ** -0.5, 0.5, ((0, 4),))
    li_rate = draw_li_rate(jax.random.fold_in(splits[8], 71), part)
    li_residue = centred(splits[7], (GROUPS, POLES), 0.25, 1.5, ((0, 4),), jnp.float32)
    return dict(q_mr=q_mr, k_mr=k_mr, v_mr=v_mr, q_li=q_li, k_li=k_li, mr_taps=mr_taps, li_rate=li_rate, li_residue=li_residue)


highest = lax.Precision.HIGHEST

def modal_tables(li_rate, li_residue, block_len):
    positions = jnp.arange(block_len).astype(jnp.float32)
    rate_col = li_rate[:, :, None]
    res_scale = li_residue * jnp.sqrt(-jnp.expm1(-2.0 * li_rate))
    li_taps = jnp.einsum('gp,gpt->gt', res_scale, jnp.exp(-rate_col * positions), precision=highest)
    end_w = jnp.exp(-rate_col * (block_len - 1.0 - positions))
    carry_w = res_scale[:, :, None] * jnp.exp(-rate_col * (positions + 1.0))
    block_decay = jnp.exp(-li_rate * block_len)
    return (li_taps, end_w, carry_w, block_decay)

def lower_toeplitz(li_taps):
    tap_len = li_taps.shape[1]
    lag_index = jnp.arange(tap_len)[:, None] - jnp.arange(tap_len)[None, :]
    gathered = li_taps[:, jnp.clip(lag_index, 0, tap_len - 1)]
    return jnp.where(lag_index >= 0, gathered, jnp.zeros_like(gathered))

def reference(q_mr, k_mr, v_mr, q_li, k_li, mr_taps, li_rate, li_residue):
    group_width = D // GROUPS
    block_len = TOK_DEV
    u_mr = (k_mr * v_mr).astype(jnp.bfloat16)
    padded = jnp.concatenate([jnp.zeros((MR_LEN - 1, D), jnp.bfloat16), u_mr], axis=0)
    lag_index = jnp.arange(block_len)[:, None] + (MR_LEN - 1) - jnp.arange(block_len + MR_LEN - 1)[None, :]
    tap_values = mr_taps.astype(jnp.float32)[:, jnp.clip(lag_index, 0, MR_LEN - 1)]
    inside = (lag_index >= 0) & (lag_index < MR_LEN)
    mr_table = jnp.where(inside, tap_values, jnp.zeros_like(tap_values))

    def mr_block(block_index):
        start_row = (block_index * block_len).astype(jnp.int32)
        block_rows = lax.dynamic_slice_in_dim(padded, start_row, block_len + MR_LEN - 1, 0)
        block_rows = block_rows.astype(jnp.float32).reshape(block_len + MR_LEN - 1, GROUPS, group_width)
        return jnp.einsum('gts,sgc->tgc', mr_table, block_rows, precision=highest).reshape(block_len, D)
    conv_mr = lax.map(mr_block, jnp.arange(N_CTX).astype(jnp.int32)).reshape(SEQ, D)
    mr_out = (q_mr * conv_mr).astype(jnp.bfloat16)
    u_li = (k_li * mr_out).astype(jnp.bfloat16)
    li_taps, end_w, carry_w, block_decay = modal_tables(li_rate, li_residue, block_len)
    li_table = lower_toeplitz(li_taps)
    blocked = u_li.reshape(N_CTX, block_len, GROUPS, group_width)

    def li_step(carried, block_rows):
        block_rows = block_rows.astype(jnp.float32)
        near_part = jnp.einsum('gts,sgc->tgc', li_table, block_rows, precision=highest)
        far_part = jnp.einsum('gpt,gpc->tgc', carry_w, carried, precision=highest)
        local_state = jnp.einsum('gps,sgc->gpc', end_w, block_rows, precision=highest)
        updated = block_decay[:, :, None] * carried + local_state
        return (updated, (near_part + far_part).reshape(block_len, D))
    initial = jnp.zeros((GROUPS, POLES, group_width), jnp.float32)
    _, conv_li = lax.scan(li_step, initial, blocked)
    li_out = (q_li * conv_li.reshape(SEQ, D)).astype(jnp.bfloat16)
    return (mr_out, li_out)
```

```python
import functools

import jax
import jax.numpy as jnp
from jax import lax
from jax.experimental import pallas as pl
from jax.experimental.pallas import tpu as pltpu
from jax.sharding import PartitionSpec as P

F32 = jnp.float32
BF16 = jnp.bfloat16
WIDE = 256


def shifted(array, axis, by):
    peers = lax.axis_size(axis)
    pairs = [(i, i + by) for i in range(peers) if 0 <= i + by < peers]
    return lax.ppermute(array, axis, pairs)


def iota(shape, dim):
    return lax.broadcasted_iota(jnp.int32, shape, dim)


def dot(a, b):
    return jnp.dot(a, b, preferred_element_type=F32)


def same_group(width, dtype):
    rows, cols = iota((WIDE, WIDE), 0), iota((WIDE, WIDE), 1)
    return jnp.where(rows // width == cols // width, 1.0, 0.0).astype(F32).astype(dtype)


def spread(compact, mask):
    copies = WIDE // compact.shape[0]
    return jnp.concatenate([compact] * copies, axis=0) * mask


def split(array):
    upper = array.astype(BF16)
    return upper, (array - upper.astype(F32)).astype(BF16)


def one_minus_exp(x):
    series = 1.0 - x / 7.0
    for n in (6.0, 5.0, 4.0, 3.0, 2.0):
        series = 1.0 - x / n * series
    return jnp.where(x < 0.25, x * series, 1.0 - jnp.exp(-x))


def expand_groups(per_group, width):
    groups = per_group.shape[0]
    pick = (iota((groups, WIDE), 1) // width == iota((groups, WIDE), 0)).astype(F32)
    return lax.dot_general(
        per_group.astype(F32),
        pick,
        (((0,), (0,)), ((), ())),
        precision=lax.Precision.HIGHEST,
        preferred_element_type=F32,
    )


def local_kernel(
    q_ref, k_ref, v_ref, kli_ref, taps_ref, rate_ref, residue_ref,
    mr_ref, part_ref, near_ref, state_ref, taptab_ref, litab_ref, powers_ref, rates_ref, scale_ref,
    mask_ref, acc_ref,
):
    rows = k_ref.shape[0]
    groups, tap_count = taps_ref.shape
    width = WIDE // groups
    half = tap_count

    @pl.when(pl.program_id(0) == 0)
    def _():
        mask_ref[...] = same_group(width, BF16)

    mask = mask_ref[...]
    lane_item = iota((tap_count + width, WIDE), 1) % width

    table = expand_groups(taps_ref[...], width)
    table = jnp.concatenate([table, jnp.zeros((width, WIDE), F32)], axis=0)
    step = 1
    while step < width:
        table = jnp.where((lane_item & step) != 0, pltpu.roll(table, step, 0), table)
        step *= 2
    table = table.astype(BF16)
    taptab_ref[...] = table

    rates = expand_groups(rate_ref[...], width)
    scale = expand_groups(residue_ref[...], width) * jnp.sqrt(one_minus_exp(2.0 * rates))
    rates_ref[...] = rates
    scale_ref[...] = scale
    poles = rates.shape[0]
    item = (iota((poles, WIDE), 1) % width).astype(F32)
    rate_row = jnp.sum(jnp.where(iota((poles, WIDE), 0) == iota((poles, WIDE), 1) % width, rates, 0.0), axis=0, keepdims=True)
    times = iota((half, WIDE), 0).astype(F32)
    powers_ref[...] = jnp.exp(-rate_row * (times + 1.0)).astype(BF16)
    power_hi, power_lo = split(jnp.exp(-rate_row * times))
    lift_hi, lift_lo = split(scale * jnp.exp(rates * item))
    lift_hi, lift_lo = spread(lift_hi, mask), spread(lift_lo, mask)
    li_taps = dot(power_hi, lift_hi) + dot(power_hi, lift_lo) + dot(power_lo, lift_hi)
    li_taps = jnp.where(iota((half, WIDE), 0) >= iota((half, WIDE), 1) % width, li_taps, 0.0)
    ends = jnp.exp(-rates * (width - 1.0 - item))
    li_table = jnp.concatenate([ends, li_taps], axis=0).astype(BF16)
    litab_ref[...] = li_table

    u = k_ref[...] * v_ref[...]
    acc_ref[...] = jnp.zeros_like(acc_ref)
    for first in range(0, rows, width):
        count = min(tap_count + width, rows - first)
        acc_ref[pl.ds(first, count), :] += dot(table[:count], spread(u[first : first + width], mask))
    part_ref[...] = acc_ref[:half, :]
    mr = (q_ref[half:, :].astype(F32) * acc_ref[half:, :]).astype(BF16)
    mr_ref[...] = mr
    near, state = near_block(mr * kli_ref[...], li_table, rates, mask, width, acc_ref)
    near_ref[...] = near
    state_ref[...] = state


def near_block(u, li_table, rates, mask, width, acc_ref):
    rows = u.shape[0]
    poles = rates.shape[0]
    chunk_decay = jnp.exp(-rates * width)
    state = jnp.zeros((poles, WIDE), F32)
    acc_ref[:rows, :] = jnp.zeros((rows, WIDE), F32)
    for first in range(0, rows, width):
        got = dot(li_table[: poles + rows - first], spread(u[first : first + width], mask))
        state = state * chunk_decay + got[:poles]
        acc_ref[pl.ds(first, rows - first), :] += got[poles:]
    return acc_ref[:rows, :], state


def rim_kernel(
    rim_ref, part_ref, q_ref, kli_ref, taptab_ref, litab_ref, rates_ref, late_ref, mr_in_ref,
    mr_ref, near_ref, early_ref, total_ref,
    mask_ref, acc_ref,
):
    del mr_in_ref
    half = rim_ref.shape[0]
    width = taptab_ref.shape[0] - half

    @pl.when(pl.program_id(0) == 0)
    def _():
        mask_ref[...] = same_group(width, BF16)

    mask = mask_ref[...]
    rates = rates_ref[...]
    rim = rim_ref[...]
    acc_ref[...] = part_ref[...]
    for first in range(0, half, width):
        acc_ref[: first + width, :] += dot(taptab_ref[half - first :, :], spread(rim[first : first + width], mask))
    mr = (q_ref[...].astype(F32) * acc_ref[...]).astype(BF16)
    mr_ref[...] = mr
    near, state = near_block(mr * kli_ref[...], litab_ref[...], rates, mask, width, acc_ref)
    near_ref[...] = near
    early_ref[...] = state
    total_ref[...] = (late_ref[...] + state * jnp.exp(-rates * half)).astype(BF16)


def far_kernel(
    n_arrived, *refs,
):
    arrived = refs[:n_arrived]
    q_ref, near_early_ref, near_late_ref, early_ref, powers_ref, rates_ref, scale_ref, out_ref, mask_ref = refs[n_arrived:]
    half = near_early_ref.shape[0]
    width = WIDE * early_ref.shape[0] // WIDE

    @pl.when(pl.program_id(0) == 0)
    def _():
        mask_ref[...] = same_group(width, BF16)

    mask = mask_ref[...]
    rates = rates_ref[...]
    block_decay = jnp.exp(-rates * (2.0 * half))
    entering = arrived[-1][...].astype(F32)
    for ref in arrived[-2::-1]:
        entering = entering * block_decay + ref[...].astype(F32)
    middle = entering * jnp.exp(-rates * half) + early_ref[...]
    powers = powers_ref[...]
    for at, state, near_ref in ((0, entering, near_early_ref), (half, middle, near_late_ref)):
        far = dot(powers, spread((state * scale_ref[...]).astype(BF16), mask))
        out_ref[at : at + half, :] = (q_ref[at : at + half, :].astype(F32) * (near_ref[...] + far)).astype(BF16)


def columns(rows, at=0):
    return pl.BlockSpec((rows, WIDE), lambda i: (at, i))


def body(q_mr, k_mr, v_mr, q_li, k_li, mr_taps, li_rate, li_residue):
    rows, channels = q_mr.shape
    groups, tap_count = mr_taps.shape
    poles = li_rate.shape[1]
    width = channels // groups
    half = tap_count
    assert rows == 2 * half and poles == width
    steps = channels // WIDE
    wide_groups = WIDE // width
    shape = jax.ShapeDtypeStruct
    params = pltpu.CompilerParams(vmem_limit_bytes=32 * 1024 * 1024)

    rim = shifted(k_mr[half:] * v_mr[half:], "ctx", 1)

    per_group = lambda n: pl.BlockSpec((wide_groups, n), lambda i: (i, 0))
    mr_out, part, near_late, late, taptab, litab, powers, rates, scale = pl.pallas_call(
        local_kernel,
        grid=(steps,),
        in_specs=[
            columns(rows), columns(rows), columns(rows), columns(half, 1),
            per_group(tap_count), per_group(poles), per_group(poles),
        ],
        out_specs=[
            columns(half, 1), columns(half), columns(half), columns(poles),
            columns(half + width), columns(half + poles), columns(half), columns(poles), columns(poles),
        ],
        out_shape=[
            shape((rows, channels), BF16), shape((half, channels), F32), shape((half, channels), F32),
            shape((poles, channels), F32), shape((half + width, channels), BF16), shape((half + poles, channels), BF16),
            shape((half, channels), BF16), shape((poles, channels), F32), shape((poles, channels), F32),
        ],
        scratch_shapes=[pltpu.VMEM((WIDE, WIDE), BF16), pltpu.VMEM((rows, WIDE), F32)],
        cost_estimate=pl.CostEstimate(flops=4 * 10**9, bytes_accessed=10 * 2**20, transcendentals=10**6),
        compiler_params=params,
        name="local_rows",
    )(q_mr, k_mr, v_mr, k_li, mr_taps, li_rate, li_residue)

    mr_out, near_early, early, total = pl.pallas_call(
        rim_kernel,
        grid=(steps,),
        in_specs=[
            columns(half), columns(half), columns(half), columns(half),
            columns(half + width), columns(half + poles), columns(poles), columns(poles), pl.BlockSpec(memory_space=pl.ANY),
        ],
        out_specs=[columns(half), columns(half), columns(poles), columns(poles)],
        out_shape=[
            shape((rows, channels), BF16), shape((half, channels), F32),
            shape((poles, channels), F32), shape((poles, channels), BF16),
        ],
        scratch_shapes=[pltpu.VMEM((WIDE, WIDE), BF16), pltpu.VMEM((half, WIDE), F32)],
        input_output_aliases={8: 0},
        cost_estimate=pl.CostEstimate(flops=2 * 10**9, bytes_accessed=4 * 2**20, transcendentals=10**4),
        compiler_params=params,
        name="rim_rows",
    )(rim, part, q_mr, k_li, taptab, litab, rates, late, mr_out)

    peers = lax.axis_size("ctx")
    reach = min(3, max(peers - 1, 1))
    arrived = [shifted(total, "ctx", by) for by in range(1, reach + 1)]
    while reach < peers - 1:
        decay = jnp.exp(-rates * rows)
        window = arrived[-1].astype(F32)
        for piece in arrived[-2::-1]:
            window = window * decay + piece.astype(F32)
        merged = window
        for times in (1, 2, 3):
            if times * reach < peers:
                far = shifted(window, "ctx", times * reach)
                merged = merged + far * jnp.exp(-rates * (rows * reach * times))
        arrived = [merged]
        reach *= 4

    li_out = pl.pallas_call(
        functools.partial(far_kernel, len(arrived)),
        grid=(steps,),
        in_specs=[columns(poles)] * len(arrived) + [
            columns(rows), columns(half), columns(half), columns(poles), columns(half), columns(poles), columns(poles),
        ],
        out_specs=columns(rows),
        out_shape=shape((rows, channels), BF16),
        scratch_shapes=[pltpu.VMEM((WIDE, WIDE), BF16)],
        cost_estimate=pl.CostEstimate(flops=10**9, bytes_accessed=5 * 2**20, transcendentals=10**4),
        compiler_params=params,
        name="far_rows",
    )(*arrived, q_li, near_early, near_late, early, powers, rates, scale)
    return (mr_out, li_out)


def solution(mesh):
    seq = P(("rep", "ctx"), "tp")
    in_specs = (seq, seq, seq, seq, seq, P("tp", None), P("tp", None), P("tp", None))
    return jax.shard_map(body, mesh=mesh, in_specs=in_specs, out_specs=(seq, seq), check_vma=False)
```

```python
import functools

import jax
import jax.numpy as jnp
from jax import lax
from jax.experimental import pallas as pl
from jax.experimental.pallas import tpu as pltpu
from jax.sharding import PartitionSpec as P

F32 = jnp.float32
BF16 = jnp.bfloat16
WIDE = 256


def shifted(array, axis, by):
    peers = lax.axis_size(axis)
    pairs = [(i, i + by) for i in range(peers) if 0 <= i + by < peers]
    return lax.ppermute(array, axis, pairs)


def iota(shape, dim):
    return lax.broadcasted_iota(jnp.int32, shape, dim)


def dot(a, b):
    return jnp.dot(a, b, preferred_element_type=F32)


def same_group(width, dtype):
    rows, cols = iota((WIDE, WIDE), 0), iota((WIDE, WIDE), 1)
    return jnp.where(rows // width == cols // width, 1.0, 0.0).astype(F32).astype(dtype)


def spread(compact, mask):
    copies = WIDE // compact.shape[0]
    return jnp.concatenate([compact] * copies, axis=0) * mask


def split(array):
    upper = array.astype(BF16)
    return upper, (array - upper.astype(F32)).astype(BF16)


def one_minus_exp(x):
    series = 1.0 - x / 7.0
    for n in (6.0, 5.0, 4.0, 3.0, 2.0):
        series = 1.0 - x / n * series
    return jnp.where(x < 0.25, x * series, 1.0 - jnp.exp(-x))


def expand_groups(per_group, width):
    groups = per_group.shape[0]
    pick = (iota((groups, WIDE), 1) // width == iota((groups, WIDE), 0)).astype(F32)
    return lax.dot_general(
        per_group.astype(F32),
        pick,
        (((0,), (0,)), ((), ())),
        precision=lax.Precision.HIGHEST,
        preferred_element_type=F32,
    )


def cols(i):
    return pl.ds(pl.multiple_of(i * WIDE, WIDE), WIDE)


def local_kernel(
    q_hbm, k_hbm, v_hbm, kli_hbm, qli_hbm, taps_ref, rate_ref, residue_ref,
    mr_hbm, part_ref, near_ref, state_ref, taptab_ref, litab_ref, powers_ref, rates_ref, scale_ref,
    qe_ref, klie_ref, qli_ref,
    k_ref, v_ref, q_ref, kli_ref, mr_ref, mask_ref, acc_ref, in_sem, side_sem, out_sem,
):
    rows, channels = k_hbm.shape
    groups, tap_count = taps_ref.shape
    steps = channels // WIDE
    width = channels // groups
    wide_groups = WIDE // width
    poles = rate_ref.shape[1]
    half = tap_count

    def fetch(i):
        at = cols(i)
        late = pl.ds(half, rows - half)
        return (
            pltpu.make_async_copy(k_hbm.at[:, at], k_ref.at[:, at], in_sem.at[0, i]),
            pltpu.make_async_copy(v_hbm.at[:, at], v_ref.at[:, at], in_sem.at[1, i]),
            pltpu.make_async_copy(q_hbm.at[late, at], q_ref.at[:, at], in_sem.at[2, i]),
            pltpu.make_async_copy(kli_hbm.at[late, at], kli_ref.at[:, at], in_sem.at[3, i]),
        )

    def put(i):
        return pltpu.make_async_copy(mr_ref.at[:, cols(i)], mr_hbm.at[pl.ds(half, rows - half), cols(i)], out_sem.at[i])

    side = (
        pltpu.make_async_copy(q_hbm.at[pl.ds(0, half)], qe_ref, side_sem.at[0]),
        pltpu.make_async_copy(kli_hbm.at[pl.ds(0, half)], klie_ref, side_sem.at[1]),
        pltpu.make_async_copy(qli_hbm, qli_ref, side_sem.at[2]),
    )
    for i in range(steps):
        for copy in fetch(i):
            copy.start()
    for copy in side:
        copy.start()

    mask_ref[...] = same_group(width, BF16)
    lane_item = iota((tap_count + width, WIDE), 1) % width
    item = (iota((poles, WIDE), 1) % width).astype(F32)
    times = iota((half, WIDE), 0).astype(F32)

    @pl.loop(0, steps)
    def _(i):
        at = cols(i)
        mask = mask_ref[...]
        own = pl.ds(pl.multiple_of(i * wide_groups, wide_groups), wide_groups)

        table = expand_groups(taps_ref[own, :], width)
        table = jnp.concatenate([table, jnp.zeros((width, WIDE), F32)], axis=0)
        step = 1
        while step < width:
            table = jnp.where((lane_item & step) != 0, pltpu.roll(table, step, 0), table)
            step *= 2
        table = table.astype(BF16)
        taptab_ref[:, at] = table

        rates = expand_groups(rate_ref[own, :], width)
        scale = expand_groups(residue_ref[own, :], width) * jnp.sqrt(one_minus_exp(2.0 * rates))
        rates_ref[:, at] = rates
        scale_ref[:, at] = scale
        on_diagonal = iota((poles, WIDE), 0) == iota((poles, WIDE), 1) % width
        rate_row = jnp.sum(jnp.where(on_diagonal, rates, 0.0), axis=0, keepdims=True)
        power = jnp.exp(-rate_row * times)
        powers_ref[:, at] = (power * jnp.exp(-rate_row)).astype(BF16)
        power_hi, power_lo = split(power)
        lift_hi, lift_lo = split(scale * jnp.exp(rates * item))
        lift_hi, lift_lo = spread(lift_hi, mask), spread(lift_lo, mask)
        li_taps = dot(power_hi, lift_hi) + dot(power_hi, lift_lo) + dot(power_lo, lift_hi)
        li_taps = jnp.where(iota((half, WIDE), 0) >= iota((half, WIDE), 1) % width, li_taps, 0.0)
        ends = jnp.exp(-rates * (width - 1.0 - item))
        li_table = jnp.concatenate([ends, li_taps], axis=0).astype(BF16)
        litab_ref[:, at] = li_table

        for copy in fetch(i):
            copy.wait()
        u = k_ref[:, at] * v_ref[:, at]
        acc_ref[...] = jnp.zeros_like(acc_ref)
        for first in range(0, rows, width):
            count = min(tap_count + width, rows - first)
            acc_ref[pl.ds(first, count), :] += dot(table[:count], spread(u[first : first + width], mask))
        part_ref[:, at] = acc_ref[:half, :]
        mr = (q_ref[:, at].astype(F32) * acc_ref[half:, :]).astype(BF16)
        mr_ref[:, at] = mr
        put(i).start()
        near, state = near_block(mr * kli_ref[:, at], li_table, rates, mask, width, acc_ref)
        near_ref[:, at] = near
        state_ref[:, at] = state

    for copy in side:
        copy.wait()
    for i in range(steps):
        put(i).wait()


def near_block(u, li_table, rates, mask, width, acc_ref):
    rows = u.shape[0]
    poles = rates.shape[0]
    chunk_decay = jnp.exp(-rates * width)
    state = jnp.zeros((poles, WIDE), F32)
    acc_ref[:rows, :] = jnp.zeros((rows, WIDE), F32)
    for first in range(0, rows, width):
        got = dot(li_table[: poles + rows - first], spread(u[first : first + width], mask))
        state = state * chunk_decay + got[:poles]
        acc_ref[pl.ds(first, rows - first), :] += got[poles:]
    return acc_ref[:rows, :], state


def rim_kernel(
    rim_ref, part_ref, q_ref, kli_ref, taptab_ref, litab_ref, rates_ref, late_ref, mr_in_hbm,
    mr_hbm, near_ref, early_ref, total_ref,
    mr_ref, mask_ref, acc_ref, out_sem,
):
    del mr_in_hbm
    half, channels = rim_ref.shape
    width = taptab_ref.shape[0] - half
    steps = channels // WIDE

    def put(i):
        return pltpu.make_async_copy(mr_ref.at[:, cols(i)], mr_hbm.at[pl.ds(0, half), cols(i)], out_sem.at[i])

    mask_ref[...] = same_group(width, BF16)

    @pl.loop(0, steps)
    def _(i):
        at = cols(i)
        mask = mask_ref[...]
        rates = rates_ref[:, at]
        rim = rim_ref[:, at]
        acc_ref[...] = part_ref[:, at]
        for first in range(0, half, width):
            acc_ref[: first + width, :] += dot(taptab_ref[half - first :, at], spread(rim[first : first + width], mask))
        mr = (q_ref[:, at].astype(F32) * acc_ref[...]).astype(BF16)
        mr_ref[:, at] = mr
        put(i).start()
        near, state = near_block(mr * kli_ref[:, at], litab_ref[:, at], rates, mask, width, acc_ref)
        near_ref[:, at] = near
        early_ref[:, at] = state
        total_ref[:, at] = (late_ref[:, at] + state * jnp.exp(-rates * half)).astype(BF16)

    for i in range(steps):
        put(i).wait()


def far_kernel(n_arrived, *refs):
    arrived = refs[:n_arrived]
    (
        q_ref, near_early_ref, near_late_ref, early_ref, powers_ref, rates_ref, scale_ref,
        out_hbm, out_ref, mask_ref, out_sem,
    ) = refs[n_arrived:]
    half, channels = near_early_ref.shape
    width = early_ref.shape[0]
    steps = channels // WIDE

    def put(i):
        return pltpu.make_async_copy(out_ref.at[:, cols(i)], out_hbm.at[:, cols(i)], out_sem.at[i])

    mask_ref[...] = same_group(width, BF16)

    @pl.loop(0, steps)
    def _(i):
        at = cols(i)
        mask = mask_ref[...]
        rates = rates_ref[:, at]
        scale = scale_ref[:, at]
        block_decay = jnp.exp(-rates * (2.0 * half))
        entering = arrived[-1][:, at].astype(F32)
        for ref in arrived[-2::-1]:
            entering = entering * block_decay + ref[:, at].astype(F32)
        middle = entering * jnp.exp(-rates * half) + early_ref[:, at]
        powers = powers_ref[:, at]
        for first, state, near_ref in ((0, entering, near_early_ref), (half, middle, near_late_ref)):
            far = dot(powers, spread((state * scale).astype(BF16), mask))
            gate = q_ref[first : first + half, at].astype(F32)
            out_ref[first : first + half, at] = (gate * (near_ref[:, at] + far)).astype(BF16)
        put(i).start()

    for i in range(steps):
        put(i).wait()


def body(q_mr, k_mr, v_mr, q_li, k_li, mr_taps, li_rate, li_residue):
    rows, channels = q_mr.shape
    groups, tap_count = mr_taps.shape
    poles = li_rate.shape[1]
    width = channels // groups
    half = tap_count
    assert rows == 2 * half and poles == width
    steps = channels // WIDE
    params = pltpu.CompilerParams(vmem_limit_bytes=40 * 1024 * 1024)
    vmem, hbm = pl.BlockSpec(memory_space=pltpu.VMEM), pl.BlockSpec(memory_space=pl.ANY)
    in_hbm = lambda array: pltpu.with_memory_space_constraint(array, pltpu.HBM)
    dma = pltpu.SemaphoreType.DMA

    rim = shifted(k_mr[half:] * v_mr[half:], "ctx", 1)

    mr_out, part, near_late, late, taptab, litab, powers, rates, scale, q_early, kli_early, qli = pl.pallas_call(
        local_kernel,
        in_specs=[hbm] * 5 + [vmem] * 3,
        out_specs=[hbm] + [vmem] * 11,
        out_shape=[
            pltpu.HBM((rows, channels), BF16),
            pltpu.VMEM((half, channels), F32),
            pltpu.VMEM((half, channels), F32),
            pltpu.VMEM((poles, channels), F32),
            pltpu.VMEM((half + width, channels), BF16),
            pltpu.VMEM((half + poles, channels), BF16),
            pltpu.VMEM((half, channels), BF16),
            pltpu.VMEM((poles, channels), F32),
            pltpu.VMEM((poles, channels), F32),
            pltpu.VMEM((half, channels), BF16),
            pltpu.VMEM((half, channels), BF16),
            pltpu.VMEM((rows, channels), BF16),
        ],
        scratch_shapes=[
            pltpu.VMEM((rows, channels), BF16),
            pltpu.VMEM((rows, channels), BF16),
            pltpu.VMEM((half, channels), BF16),
            pltpu.VMEM((half, channels), BF16),
            pltpu.VMEM((half, channels), BF16),
            pltpu.VMEM((WIDE, WIDE), BF16),
            pltpu.VMEM((rows, WIDE), F32),
            dma((4, steps)),
            dma((3,)),
            dma((steps,)),
        ],
        cost_estimate=pl.CostEstimate(flops=4 * 10**9, bytes_accessed=10 * 2**20, transcendentals=10**6),
        compiler_params=params,
        name="local_rows",
    )(*map(in_hbm, (q_mr, k_mr, v_mr, k_li, q_li)), mr_taps, li_rate, li_residue)

    mr_out, near_early, early, total = pl.pallas_call(
        rim_kernel,
        in_specs=[vmem] * 8 + [hbm],
        out_specs=[hbm] + [vmem] * 3,
        out_shape=[
            pltpu.HBM((rows, channels), BF16),
            pltpu.VMEM((half, channels), F32),
            pltpu.VMEM((poles, channels), F32),
            pltpu.VMEM((poles, channels), BF16),
        ],
        scratch_shapes=[
            pltpu.VMEM((half, channels), BF16),
            pltpu.VMEM((WIDE, WIDE), BF16),
            pltpu.VMEM((half, WIDE), F32),
            dma((steps,)),
        ],
        input_output_aliases={8: 0},
        cost_estimate=pl.CostEstimate(flops=2 * 10**9, bytes_accessed=4 * 2**20, transcendentals=10**4),
        compiler_params=params,
        name="rim_rows",
    )(rim, part, q_early, kli_early, taptab, litab, rates, late, mr_out)

    peers = lax.axis_size("ctx")
    reach = min(3, max(peers - 1, 1))
    arrived = [shifted(total, "ctx", by) for by in range(1, reach + 1)]
    while reach < peers - 1:
        decay = jnp.exp(-rates * rows)
        window = arrived[-1].astype(F32)
        for piece in arrived[-2::-1]:
            window = window * decay + piece.astype(F32)
        merged = window
        for times in (1, 2, 3):
            if times * reach < peers:
                far = shifted(window, "ctx", times * reach)
                merged = merged + far * jnp.exp(-rates * (rows * reach * times))
        arrived = [merged]
        reach *= 4

    li_out = pl.pallas_call(
        functools.partial(far_kernel, len(arrived)),
        in_specs=[vmem] * (len(arrived) + 7),
        out_specs=hbm,
        out_shape=jax.ShapeDtypeStruct((rows, channels), BF16),
        scratch_shapes=[pltpu.VMEM((rows, channels), BF16), pltpu.VMEM((WIDE, WIDE), BF16), dma((steps,))],
        cost_estimate=pl.CostEstimate(flops=10**9, bytes_accessed=5 * 2**20, transcendentals=10**4),
        compiler_params=params,
        name="far_rows",
    )(*arrived, qli, near_early, near_late, early, powers, rates, scale)
    return (mr_out, li_out)


def solution(mesh):
    seq = P(("rep", "ctx"), "tp")
    in_specs = (seq, seq, seq, seq, seq, P("tp", None), P("tp", None), P("tp", None))
    return jax.shard_map(body, mesh=mesh, in_specs=in_specs, out_specs=(seq, seq), check_vma=False)
```

```python
import functools

import jax
import jax.numpy as jnp
from jax import lax
from jax.experimental import pallas as pl
from jax.experimental.pallas import tpu as pltpu
from jax.sharding import PartitionSpec as P

F32 = jnp.float32
BF16 = jnp.bfloat16
WIDE = 256
CHUNK = 16


def shifted(array, axis, by):
    peers = lax.axis_size(axis)
    pairs = [(i, i + by) for i in range(peers) if 0 <= i + by < peers]
    return lax.ppermute(array, axis, pairs)


def iota(shape, dim):
    return lax.broadcasted_iota(jnp.int32, shape, dim)


def dot(a, b):
    return jnp.dot(a, b, preferred_element_type=F32)


def same_group(width, dtype):
    rows, cols = iota((WIDE, WIDE), 0), iota((WIDE, WIDE), 1)
    return jnp.where(rows // width == cols // width, 1.0, 0.0).astype(F32).astype(dtype)


def spread(compact, mask):
    copies = WIDE // compact.shape[0]
    return jnp.concatenate([compact] * copies, axis=0) * mask


def split(array):
    upper = array.astype(BF16)
    return upper, (array - upper.astype(F32)).astype(BF16)


def one_minus_exp(x):
    series = 1.0 - x / 7.0
    for n in (6.0, 5.0, 4.0, 3.0, 2.0):
        series = 1.0 - x / n * series
    return jnp.where(x < 0.25, x * series, 1.0 - jnp.exp(-x))


def expand_groups(per_group, first_group, width, precision=None):
    groups = per_group.shape[1]
    pick = iota((groups, WIDE), 1) // width + first_group == iota((groups, WIDE), 0)
    return jnp.dot(per_group, pick.astype(F32).astype(per_group.dtype), precision=precision, preferred_element_type=F32)


def pipelined(steps, *stages):
    for turn in range(steps + len(stages) - 1):
        for lag, stage in enumerate(stages):
            if 0 <= turn - lag < steps:
                i = turn - lag
                stage(i, slice(i * WIDE, (i + 1) * WIDE))


def rates_along(rates, width):
    on_diagonal = iota(rates.shape, 0) == iota(rates.shape, 1) % width
    return jnp.sum(jnp.where(on_diagonal, rates, 0.0), axis=0, keepdims=True)


def pole_sums(ends, u, fold_ref, poles):
    every = dot(ends, u)
    parts = []
    lanes = 128
    for at in range(0, WIDE, lanes):
        own = every[at : at + lanes, at : at + lanes] * fold_ref[at : at + lanes, at : at + lanes]
        parts.append(functools.reduce(jnp.add, [own[p : p + poles] for p in range(0, lanes, poles)]))
    return jnp.concatenate(parts, axis=1)


def local_kernel(
    q_hbm, k_hbm, v_hbm, kli_hbm, taps_hbm, rate_hbm,
    mr_ref, part_ref, ulate_ref, late_ref, first_ref, taptab_ref, ends_ref, decay_ref, q_ref, kli_ref,
    k_ref, v_ref, taps_ref, rate_ref, mask_ref, fold_ref, acc_ref, in_sem, small_sem,
):
    rows, channels = k_hbm.shape
    groups, tap_count = taps_hbm.shape
    steps = channels // WIDE
    width = channels // groups
    wide_groups = WIDE // width
    poles = rate_hbm.shape[0]
    half = tap_count
    block = 2 * WIDE

    small = (
        pltpu.make_async_copy(taps_hbm, taps_ref, small_sem.at[0]),
        pltpu.make_async_copy(rate_hbm, rate_ref, small_sem.at[1]),
    )
    for copy in small:
        copy.start()

    def fetch(n):
        at = slice(n * block, (n + 1) * block)
        pairs = ((k_hbm, k_ref), (v_hbm, v_ref), (q_hbm, q_ref), (kli_hbm, kli_ref))
        return [pltpu.make_async_copy(a.at[:, at], b.at[:, at], in_sem.at[m, n]) for m, (a, b) in enumerate(pairs)]

    blocks = [fetch(n) for n in range(channels // block)]
    for copies in blocks:
        for copy in copies:
            copy.start()

    mask_ref[...] = same_group(width, BF16)
    fold_ref[...] = same_group(width, F32)
    for copy in small:
        copy.wait()

    def tables(i, at):
        lane_item = iota((tap_count + width, WIDE), 1) % width
        own = slice(i * wide_groups, (i + 1) * wide_groups)
        pick = (iota((wide_groups, WIDE), 1) // width == iota((wide_groups, WIDE), 0)).astype(F32).astype(BF16)
        table = lax.dot_general(taps_ref[own, :], pick, (((0,), (0,)), ((), ())), preferred_element_type=F32)
        table = jnp.concatenate([table, jnp.zeros((width, WIDE), F32)], axis=0)
        step = 1
        while step < width:
            table = jnp.where((lane_item & step) != 0, pltpu.roll(table, step, 0), table)
            step *= 2
        taptab_ref[:, at] = table.astype(BF16)
        rates = expand_groups(rate_ref[...], i * wide_groups, width, lax.Precision.HIGHEST)
        decay_ref[:, at] = jnp.exp(-rates * half)
        left = half - 1.0 - iota((half, WIDE), 0).astype(F32)
        ends_ref[at, :] = jnp.transpose(jnp.exp(-rates_along(rates, width) * left)).astype(BF16)

    def convolve(i, at):
        if i * WIDE % block == 0:
            for copy in blocks[i * WIDE // block]:
                copy.wait()
        mask = mask_ref[...]
        u = k_ref[:, at] * v_ref[:, at]
        acc_ref[:, at] = jnp.zeros((rows, WIDE), F32)
        for first in range(0, rows, width):
            count = min(tap_count + width, rows - first)
            acc_ref[first : first + count, at] += dot(taptab_ref[:count, at], spread(u[first : first + width], mask))

    def gate(i, at):
        early, late = acc_ref[:half, at], acc_ref[half:, at]
        part_ref[:, at] = early
        mr = (q_ref[half:, at].astype(F32) * late).astype(BF16)
        mr_ref[:, at] = mr
        u_late = mr * kli_ref[half:, at]
        ulate_ref[:, at] = u_late
        u_early = (q_ref[:half, at].astype(F32) * early).astype(BF16) * kli_ref[:half, at]
        ends = ends_ref[at, :]
        late_state = pole_sums(ends, u_late, fold_ref, poles)
        early_state = pole_sums(ends, u_early, fold_ref, poles)
        late_ref[:, at] = late_state
        first_ref[:, at] = (late_state + early_state * decay_ref[:, at]).astype(BF16)

    pipelined(steps, tables, convolve, gate)


def near_rows(u_ref, litab_ref, near_ref, mask_ref, width):
    half = u_ref.shape[0]

    def work(i, at):
        mask = mask_ref[...]
        near_ref[:, at] = jnp.zeros((half, WIDE), F32)
        u = u_ref[:, at]
        for first in range(0, half, width):
            near_ref[first:half, at] += dot(litab_ref[: half - first, at], spread(u[first : first + width], mask))

    return work


def filter_kernel(
    qli_hbm, rate_hbm, residue_hbm, ulate_ref,
    near_ref, litab_ref, powers_ref, decay_ref, scale_ref, qli_ref,
    rate_ref, residue_ref, mask_ref, sem,
):
    half, channels = ulate_ref.shape
    poles, groups = rate_hbm.shape
    steps = channels // WIDE
    width = channels // groups
    wide_groups = WIDE // width
    copies = (
        pltpu.make_async_copy(rate_hbm, rate_ref, sem.at[0]),
        pltpu.make_async_copy(residue_hbm, residue_ref, sem.at[1]),
        pltpu.make_async_copy(qli_hbm, qli_ref, sem.at[2]),
    )
    for copy in copies:
        copy.start()
    mask_ref[...] = same_group(width, BF16)
    for copy in copies[:2]:
        copy.wait()

    def tables(i, at):
        mask = mask_ref[...]
        rates = expand_groups(rate_ref[...], i * wide_groups, width, lax.Precision.HIGHEST)
        residue = expand_groups(residue_ref[...], i * wide_groups, width, lax.Precision.HIGHEST)
        scale = residue * jnp.sqrt(one_minus_exp(2.0 * rates))
        decay_ref[:, at] = jnp.exp(-rates * half)
        scale_ref[:, at] = scale
        item = (iota((poles, WIDE), 1) % width).astype(F32)
        times = iota((half, WIDE), 0).astype(F32)
        rate_row = rates_along(rates, width)
        power = jnp.exp(-rate_row * times)
        powers_ref[:, at] = (power * jnp.exp(-rate_row)).astype(BF16)
        power_hi, power_lo = split(power)
        lift_hi, lift_lo = split(scale * jnp.exp(rates * item))
        lift_hi, lift_lo = spread(lift_hi, mask), spread(lift_lo, mask)
        li_taps = dot(power_hi, lift_hi) + dot(power_hi, lift_lo) + dot(power_lo, lift_hi)
        causal = iota((half, WIDE), 0) >= iota((half, WIDE), 1) % width
        litab_ref[:, at] = jnp.where(causal, li_taps, 0.0).astype(BF16)

    pipelined(steps, tables, near_rows(ulate_ref, litab_ref, near_ref, mask_ref, width))
    copies[2].wait()


def rim_kernel(
    rim_ref, part_ref, q_ref, kli_ref, taptab_ref, ends_ref, decay_ref, late_ref, before_ref,
    mr_ref, u_ref, early_ref, total_ref,
    mask_ref, fold_ref, acc_ref,
):
    half, channels = rim_ref.shape
    width = taptab_ref.shape[0] - half
    poles = late_ref.shape[0]
    mask_ref[...] = same_group(width, BF16)
    fold_ref[...] = same_group(width, F32)

    def convolve(i, at):
        mask = mask_ref[...]
        rim = rim_ref[:, at]
        acc_ref[:, at] = part_ref[:, at]
        for first in range(0, half, width):
            acc_ref[: first + width, at] += dot(taptab_ref[half - first :, at], spread(rim[first : first + width], mask))

    def gate(i, at):
        decay = decay_ref[:, at]
        mr = (q_ref[:half, at].astype(F32) * acc_ref[:, at]).astype(BF16)
        mr_ref[:, at] = mr
        u = mr * kli_ref[:half, at]
        u_ref[:, at] = u
        state = pole_sums(ends_ref[at, :], u, fold_ref, poles)
        early_ref[:, at] = state
        entered = before_ref[:, at].astype(F32) * decay
        total_ref[:, at] = (late_ref[:, at] + (state + entered) * decay).astype(BF16)

    pipelined(channels // WIDE, convolve, gate)


def near_kernel(mr_early_ref, mr_late_ref, u_ref, litab_ref, mr_hbm, near_ref, mask_ref, sem):
    half, channels = u_ref.shape
    copies = (
        pltpu.make_async_copy(mr_early_ref, mr_hbm.at[:half], sem.at[0]),
        pltpu.make_async_copy(mr_late_ref, mr_hbm.at[half:], sem.at[1]),
    )
    for copy in copies:
        copy.start()
    mask_ref[...] = same_group(CHUNK, BF16)
    pipelined(channels // WIDE, near_rows(u_ref, litab_ref, near_ref, mask_ref, CHUNK))
    for copy in copies:
        copy.wait()


def far_kernel(one_before, *refs):
    (
        q_ref, near_early_ref, near_late_ref, early_ref, powers_ref, decay_ref, scale_ref,
        out_hbm, out_ref, mask_ref, out_sem,
    ) = refs[-11:]
    arrived = refs[one_before:-11]
    half, channels = powers_ref.shape
    steps = channels // WIDE

    def put(i, at):
        return pltpu.make_async_copy(out_ref.at[:, at], out_hbm.at[:, at], out_sem.at[i])

    mask_ref[...] = same_group(early_ref.shape[0], BF16)

    def work(i, at):
        mask = mask_ref[...]
        scale = scale_ref[:, at]
        decay = decay_ref[:, at]
        entering = arrived[-1][:, at].astype(F32)
        for ref in arrived[-2::-1]:
            entering = entering * (decay * decay) + ref[:, at].astype(F32)
        if one_before:
            entering = entering + refs[0][:, at].astype(F32)
        middle = entering * decay + early_ref[:, at]
        powers = powers_ref[:, at]
        for first, state, near_ref in ((0, entering, near_early_ref), (half, middle, near_late_ref)):
            far = dot(powers, spread((state * scale).astype(BF16), mask))
            gate = q_ref[first : first + half, at].astype(F32)
            out_ref[first : first + half, at] = (gate * (near_ref[:, at] + far)).astype(BF16)
        put(i, at).start()

    pipelined(steps, work)
    for i in range(steps):
        put(i, slice(i * WIDE, (i + 1) * WIDE)).wait()


def body(q_mr, k_mr, v_mr, q_li, k_li, mr_taps, li_rate, li_residue):
    rows, channels = q_mr.shape
    groups, tap_count = mr_taps.shape
    poles = li_rate.shape[1]
    width = channels // groups
    half = tap_count
    assert rows == 2 * half and poles == width == CHUNK
    steps = channels // WIDE
    params = pltpu.CompilerParams(vmem_limit_bytes=40 * 1024 * 1024)
    vmem, hbm = pl.BlockSpec(memory_space=pltpu.VMEM), pl.BlockSpec(memory_space=pl.ANY)
    in_hbm = lambda *arrays: [pltpu.with_memory_space_constraint(array, pltpu.HBM) for array in arrays]
    dma = pltpu.SemaphoreType.DMA
    mask, fold = pltpu.VMEM((WIDE, WIDE), BF16), pltpu.VMEM((WIDE, WIDE), F32)
    pole_sum, short, tall = (poles, channels), (half, channels), (rows, channels)

    def call(kernel, name, ins, outs, scratch, flops, *operands):
        return pl.pallas_call(
            kernel,
            in_specs=ins,
            out_specs=[hbm if isinstance(out, jax.ShapeDtypeStruct) else vmem for out in outs],
            out_shape=outs,
            scratch_shapes=scratch,
            cost_estimate=pl.CostEstimate(flops=flops, bytes_accessed=4 * 2**20, transcendentals=10**5),
            compiler_params=params,
            name=name,
        )(*operands)

    rim = shifted(k_mr[half:] * v_mr[half:], "ctx", 1)

    mr_late, part, u_late, late, first, taptab, ends, decay, q, kli = call(
        local_kernel,
        "local_rows",
        [hbm] * 6,
        [
            pltpu.VMEM(short, BF16),
            pltpu.VMEM(short, F32),
            pltpu.VMEM(short, BF16),
            pltpu.VMEM(pole_sum, F32),
            pltpu.VMEM(pole_sum, BF16),
            pltpu.VMEM((half + width, channels), BF16),
            pltpu.VMEM((channels, half), BF16),
            pltpu.VMEM(pole_sum, F32),
            pltpu.VMEM(tall, BF16),
            pltpu.VMEM(tall, BF16),
        ],
        [
            pltpu.VMEM(tall, BF16),
            pltpu.VMEM(tall, BF16),
            pltpu.VMEM((groups, tap_count), BF16),
            pltpu.VMEM((poles, groups), F32),
            mask,
            fold,
            pltpu.VMEM(tall, F32),
            dma((4, steps)),
            dma((2,)),
        ],
        4 * 10**9,
        *in_hbm(q_mr, k_mr, v_mr, k_li, mr_taps, li_rate.T),
    )

    peers = lax.axis_size("ctx")
    send = lambda array, pairs: lax.ppermute(array, "ctx", pairs)
    before = send(first, [(0, 1)]) if peers == 4 else jnp.zeros(pole_sum, BF16)

    near_late, litab, powers, decay, scale, qli = call(
        filter_kernel,
        "filter_tables",
        [hbm] * 3 + [vmem],
        [
            pltpu.VMEM(short, F32),
            pltpu.VMEM(short, BF16),
            pltpu.VMEM(short, BF16),
            pltpu.VMEM(pole_sum, F32),
            pltpu.VMEM(pole_sum, F32),
            pltpu.VMEM(tall, BF16),
        ],
        [pltpu.VMEM((poles, groups), F32), pltpu.VMEM((poles, groups), F32), mask, dma((3,))],
        2 * 10**9,
        *in_hbm(q_li, li_rate.T, li_residue.T),
        u_late,
    )

    mr_early, u_early, early, total = call(
        rim_kernel,
        "rim_rows",
        [vmem] * 9,
        [pltpu.VMEM(short, BF16), pltpu.VMEM(short, BF16), pltpu.VMEM(pole_sum, F32), pltpu.VMEM(pole_sum, BF16)],
        [mask, fold, pltpu.VMEM(short, F32)],
        2 * 10**9,
        rim, part, q, kli, taptab, ends, decay, late, before,
    )

    if peers == 4:
        next_but_one = send(total, [(1, 3)])
        arrived = [send(total, [(1, 2), (2, 3)]), next_but_one]
    else:
        reach = min(3, max(peers - 1, 1))
        arrived = [shifted(total, "ctx", by) for by in range(1, reach + 1)]
        rates = jnp.repeat(li_rate.T, width, axis=1)
        while reach < peers - 1:
            window = arrived[-1].astype(F32)
            for piece in arrived[-2::-1]:
                window = window * jnp.exp(-rates * rows) + piece.astype(F32)
            merged = window
            for times in (1, 2, 3):
                if times * reach < peers:
                    moved = shifted(window, "ctx", times * reach)
                    merged = merged + moved * jnp.exp(-rates * (rows * reach * times))
            arrived = [merged]
            reach *= 4

    mr_out, near_early = call(
        near_kernel,
        "near_part",
        [vmem] * 4,
        [jax.ShapeDtypeStruct(tall, BF16), pltpu.VMEM(short, F32)],
        [mask, dma((2,))],
        2 * 10**9,
        mr_early, mr_late, u_early, litab,
    )

    if peers == 4:
        arrived = [before] + arrived
    (li_out,) = call(
        functools.partial(far_kernel, peers == 4),
        "far_rows",
        [vmem] * (len(arrived) + 7),
        [jax.ShapeDtypeStruct(tall, BF16)],
        [pltpu.VMEM(tall, BF16), mask, dma((steps,))],
        10**9,
        *arrived, qli, near_early, near_late, early, powers, decay, scale,
    )
    return (mr_out, li_out)


def solution(mesh):
    seq = P(("rep", "ctx"), "tp")
    in_specs = (seq, seq, seq, seq, seq, P("tp", None), P("tp", None), P("tp", None))
    return jax.shard_map(body, mesh=mesh, in_specs=in_specs, out_specs=(seq, seq), check_vma=False)
```

```python
import functools

import jax
import jax.numpy as jnp
from jax import lax
from jax.experimental import pallas as pl
from jax.experimental.pallas import tpu as pltpu
from jax.sharding import PartitionSpec as P

F32 = jnp.float32
BF16 = jnp.bfloat16
WIDE = 256
CHUNK = 16


def shifted(array, axis, by):
    peers = lax.axis_size(axis)
    pairs = [(i, i + by) for i in range(peers) if 0 <= i + by < peers]
    return lax.ppermute(array, axis, pairs)


def iota(shape, dim):
    return lax.broadcasted_iota(jnp.int32, shape, dim)


def dot(a, b):
    return jnp.dot(a, b, preferred_element_type=F32)


def same_group(width, dtype):
    rows, cols = iota((WIDE, WIDE), 0), iota((WIDE, WIDE), 1)
    return jnp.where(rows // width == cols // width, 1.0, 0.0).astype(F32).astype(dtype)


def spread(compact, mask):
    copies = WIDE // compact.shape[0]
    return jnp.concatenate([compact] * copies, axis=0) * mask


def split(array):
    upper = array.astype(BF16)
    return upper, (array - upper.astype(F32)).astype(BF16)


def one_minus_exp(x):
    series = 1.0 - x / 7.0
    for n in (6.0, 5.0, 4.0, 3.0, 2.0):
        series = 1.0 - x / n * series
    return jnp.where(x < 0.25, x * series, 1.0 - jnp.exp(-x))


def expand_groups(per_group, first_group, width, precision=None):
    groups = per_group.shape[1]
    pick = iota((groups, WIDE), 1) // width + first_group == iota((groups, WIDE), 0)
    return jnp.dot(per_group, pick.astype(F32).astype(per_group.dtype), precision=precision, preferred_element_type=F32)


def pipelined(steps, *stages):
    for turn in range(steps + len(stages) - 1):
        for lag, stage in enumerate(stages):
            if 0 <= turn - lag < steps:
                i = turn - lag
                stage(i, slice(i * WIDE, (i + 1) * WIDE))


def rates_along(rates, width):
    on_diagonal = iota(rates.shape, 0) == iota(rates.shape, 1) % width
    return jnp.sum(jnp.where(on_diagonal, rates, 0.0), axis=0, keepdims=True)


def pole_sums(ends, u, fold_ref, poles):
    every = dot(ends, u)
    parts = []
    lanes = 128
    for at in range(0, WIDE, lanes):
        own = every[at : at + lanes, at : at + lanes] * fold_ref[at : at + lanes, at : at + lanes]
        parts.append(functools.reduce(jnp.add, [own[p : p + poles] for p in range(0, lanes, poles)]))
    return jnp.concatenate(parts, axis=1)


def local_kernel(
    tail_ref, q_hbm, k_hbm, v_hbm, kli_hbm, taps_hbm, rate_hbm,
    mr_ref, part_ref, ulate_ref, late_ref, first_ref, taptab_ref, ends_ref, decay_ref, q_ref, kli_ref,
    mr_early_ref, u_early_ref, early_ref,
    k_ref, v_ref, taps_ref, rate_ref, mask_ref, fold_ref, acc_ref, in_sem,
):
    rows, channels = k_hbm.shape
    groups, tap_count = taps_hbm.shape
    steps = channels // WIDE
    width = channels // groups
    wide_groups = WIDE // width
    poles = rate_hbm.shape[0]
    half = tap_count

    pairs = (
        (taps_hbm, taps_ref), (rate_hbm, rate_ref),
        (k_hbm.at[:half], k_ref), (v_hbm.at[:half], v_ref), (q_hbm, q_ref), (kli_hbm, kli_ref),
    )
    copies = [pltpu.make_async_copy(a, b, in_sem.at[n]) for n, (a, b) in enumerate(pairs)]
    for copy in copies:
        copy.start()

    mask_ref[...] = same_group(width, BF16)
    fold_ref[...] = same_group(width, F32)
    for copy in copies[:2]:
        copy.wait()

    def tables(i, at):
        lane_item = iota((tap_count + width, WIDE), 1) % width
        own = slice(i * wide_groups, (i + 1) * wide_groups)
        pick = (iota((wide_groups, WIDE), 1) // width == iota((wide_groups, WIDE), 0)).astype(F32).astype(BF16)
        table = lax.dot_general(taps_ref[own, :], pick, (((0,), (0,)), ((), ())), preferred_element_type=F32)
        table = jnp.concatenate([table, jnp.zeros((width, WIDE), F32)], axis=0)
        step = 1
        while step < width:
            table = jnp.where((lane_item & step) != 0, pltpu.roll(table, step, 0), table)
            step *= 2
        taptab_ref[:, at] = table.astype(BF16)
        rates = expand_groups(rate_ref[...], i * wide_groups, width, lax.Precision.HIGHEST)
        decay_ref[:, at] = jnp.exp(-rates * half)
        left = half - 1.0 - iota((half, WIDE), 0).astype(F32)
        ends_ref[at, :] = jnp.transpose(jnp.exp(-rates_along(rates, width) * left)).astype(BF16)

    def convolve_late(i, at):
        mask = mask_ref[...]
        acc_ref[half:, at] = jnp.zeros((rows - half, WIDE), F32)
        for first in range(half, rows, width):
            u = tail_ref[first - half : first - half + width, at]
            acc_ref[first:, at] += dot(taptab_ref[: rows - first, at], spread(u, mask))

    def convolve_early(i, at):
        mask = mask_ref[...]
        u = k_ref[:, at] * v_ref[:, at]
        acc_ref[:half, at] = jnp.zeros((half, WIDE), F32)
        for first in range(0, half, width):
            count = tap_count + width
            acc_ref[first : first + count, at] += dot(taptab_ref[:, at], spread(u[first : first + width], mask))

    def gate(i, at):
        early, late = acc_ref[:half, at], acc_ref[half:, at]
        part_ref[:, at] = early
        mr = (q_ref[half:, at].astype(F32) * late).astype(BF16)
        mr_ref[:, at] = mr
        u_late = mr * kli_ref[half:, at]
        ulate_ref[:, at] = u_late
        mr_early = (q_ref[:half, at].astype(F32) * early).astype(BF16)
        mr_early_ref[:, at] = mr_early
        u_early = mr_early * kli_ref[:half, at]
        u_early_ref[:, at] = u_early
        ends = ends_ref[at, :]
        late_state = pole_sums(ends, u_late, fold_ref, poles)
        early_state = pole_sums(ends, u_early, fold_ref, poles)
        late_ref[:, at] = late_state
        early_ref[:, at] = early_state
        first_ref[:, at] = (late_state + early_state * decay_ref[:, at]).astype(BF16)

    pipelined(steps, tables)
    pipelined(steps, convolve_late)
    for copy in copies[2:]:
        copy.wait()
    pipelined(steps, convolve_early, gate)


def near_rows(u_ref, litab_ref, near_ref, mask_ref, width):
    half = u_ref.shape[0]

    def work(i, at):
        mask = mask_ref[...]
        near_ref[:, at] = jnp.zeros((half, WIDE), F32)
        u = u_ref[:, at]
        for first in range(0, half, width):
            near_ref[first:half, at] += dot(litab_ref[: half - first, at], spread(u[first : first + width], mask))

    return work


def filter_kernel(
    qli_hbm, rate_hbm, residue_hbm,
    litab_ref, powers_ref, decay_ref, scale_ref, qli_ref,
    rate_ref, residue_ref, mask_ref, sem,
):
    half, channels = litab_ref.shape
    poles, groups = rate_hbm.shape
    steps = channels // WIDE
    width = channels // groups
    wide_groups = WIDE // width
    copies = (
        pltpu.make_async_copy(rate_hbm, rate_ref, sem.at[0]),
        pltpu.make_async_copy(residue_hbm, residue_ref, sem.at[1]),
        pltpu.make_async_copy(qli_hbm, qli_ref, sem.at[2]),
    )
    for copy in copies:
        copy.start()
    mask_ref[...] = same_group(width, BF16)
    for copy in copies[:2]:
        copy.wait()

    def tables(i, at):
        mask = mask_ref[...]
        rates = expand_groups(rate_ref[...], i * wide_groups, width, lax.Precision.HIGHEST)
        residue = expand_groups(residue_ref[...], i * wide_groups, width, lax.Precision.HIGHEST)
        scale = residue * jnp.sqrt(one_minus_exp(2.0 * rates))
        decay_ref[:, at] = jnp.exp(-rates * half)
        scale_ref[:, at] = scale
        item = (iota((poles, WIDE), 1) % width).astype(F32)
        times = iota((half, WIDE), 0).astype(F32)
        rate_row = rates_along(rates, width)
        power = jnp.exp(-rate_row * times)
        powers_ref[:, at] = (power * jnp.exp(-rate_row)).astype(BF16)
        power_hi, power_lo = split(power)
        lift_hi, lift_lo = split(scale * jnp.exp(rates * item))
        lift_hi, lift_lo = spread(lift_hi, mask), spread(lift_lo, mask)
        li_taps = dot(power_hi, lift_hi) + dot(power_hi, lift_lo) + dot(power_lo, lift_hi)
        causal = iota((half, WIDE), 0) >= iota((half, WIDE), 1) % width
        litab_ref[:, at] = jnp.where(causal, li_taps, 0.0).astype(BF16)

    pipelined(steps, tables)
    copies[2].wait()


def rim_rows(
    rim_ref, part_ref, q_ref, kli_ref, taptab_ref, ends_ref, mr_ref, u_ref, early_ref, mask_ref, fold_ref, acc_ref
):
    half, channels = rim_ref.shape
    width = taptab_ref.shape[0] - half
    poles = early_ref.shape[0]
    mask_ref[...] = same_group(width, BF16)
    fold_ref[...] = same_group(width, F32)

    def convolve(i, at):
        mask = mask_ref[...]
        rim = rim_ref[:, at]
        acc_ref[:, at] = part_ref[:, at]
        for first in range(0, half, width):
            acc_ref[: first + width, at] += dot(taptab_ref[half - first :, at], spread(rim[first : first + width], mask))

    def gate(i, at):
        mr = (q_ref[:half, at].astype(F32) * acc_ref[:, at]).astype(BF16)
        mr_ref[:, at] = mr
        u = mr * kli_ref[:half, at]
        u_ref[:, at] = u
        early_ref[:, at] = pole_sums(ends_ref[at, :], u, fold_ref, poles)

    pipelined(channels // WIDE, convolve, gate)


def inner(name):
    at = lax.axis_index(name)
    return jnp.logical_and(at > 0, at < lax.axis_size(name) - 1)


def rim_kernel(by_place, *refs):
    if by_place:
        pl.when(inner("ctx"))(lambda: rim_rows(*refs))
    else:
        rim_rows(*refs)


def near_kernel(
    by_place,
    rim_ref, part_ref, q_ref, kli_ref, taptab_ref, ends_ref,
    mr_first_ref, u_first_ref, early_first_ref, mr_rim_ref, u_rim_ref, early_rim_ref, mr_late_ref, ulate_ref, litab_ref,
    early_ref, near_early_ref, near_late_ref, mr_hbm,
    mr_ref, u_ref, mask_ref, fold_ref, acc_ref, sem,
):
    half, channels = u_ref.shape
    steps = channels // WIDE
    copies = (
        pltpu.make_async_copy(mr_late_ref, mr_hbm.at[half:], sem.at[0]),
        pltpu.make_async_copy(mr_ref, mr_hbm.at[:half], sem.at[1]),
    )
    copies[0].start()

    def take(*sources):
        for source, target in zip(sources, (mr_ref, u_ref, early_ref)):
            target[...] = source[...]

    if by_place:
        own = (rim_ref, part_ref, q_ref, kli_ref, taptab_ref, ends_ref, mr_ref, u_ref, early_ref, mask_ref, fold_ref, acc_ref)
        place = lax.axis_index("ctx")
        pl.when(place == 0)(lambda: take(mr_first_ref, u_first_ref, early_first_ref))
        pl.when(inner("ctx"))(lambda: take(mr_rim_ref, u_rim_ref, early_rim_ref))
        pl.when(place == lax.axis_size("ctx") - 1)(lambda: rim_rows(*own))
    else:
        take(mr_rim_ref, u_rim_ref, early_rim_ref)
    copies[1].start()
    mask_ref[...] = same_group(CHUNK, BF16)
    pipelined(steps, near_rows(ulate_ref, litab_ref, near_late_ref, mask_ref, CHUNK))
    pipelined(steps, near_rows(u_ref, litab_ref, near_early_ref, mask_ref, CHUNK))
    for copy in copies:
        copy.wait()


def far_kernel(one_before, *refs):
    (
        q_ref, near_early_ref, near_late_ref, early_ref, powers_ref, decay_ref, scale_ref,
        out_hbm, out_ref, mask_ref, out_sem,
    ) = refs[-11:]
    arrived = refs[one_before:-11]
    half, channels = powers_ref.shape
    steps = channels // WIDE

    def put(i, at):
        return pltpu.make_async_copy(out_ref.at[:, at], out_hbm.at[:, at], out_sem.at[i])

    mask_ref[...] = same_group(early_ref.shape[0], BF16)

    def work(i, at):
        mask = mask_ref[...]
        scale = scale_ref[:, at]
        decay = decay_ref[:, at]
        entering = arrived[-1][:, at].astype(F32)
        for ref in arrived[-2::-1]:
            entering = entering * (decay * decay) + ref[:, at].astype(F32)
        if one_before:
            entering = entering + refs[0][:, at].astype(F32)
        middle = entering * decay + early_ref[:, at]
        powers = powers_ref[:, at]
        for first, state, near_ref in ((0, entering, near_early_ref), (half, middle, near_late_ref)):
            far = dot(powers, spread((state * scale).astype(BF16), mask))
            gate = q_ref[first : first + half, at].astype(F32)
            out_ref[first : first + half, at] = (gate * (near_ref[:, at] + far)).astype(BF16)
        put(i, at).start()

    pipelined(steps, work)
    for i in range(steps):
        put(i, slice(i * WIDE, (i + 1) * WIDE)).wait()


def body(q_mr, k_mr, v_mr, q_li, k_li, mr_taps, li_rate, li_residue):
    rows, channels = q_mr.shape
    groups, tap_count = mr_taps.shape
    poles = li_rate.shape[1]
    width = channels // groups
    half = tap_count
    assert rows == 2 * half and poles == width == CHUNK
    steps = channels // WIDE
    params = pltpu.CompilerParams(vmem_limit_bytes=40 * 1024 * 1024)
    vmem, hbm = pl.BlockSpec(memory_space=pltpu.VMEM), pl.BlockSpec(memory_space=pl.ANY)
    in_hbm = lambda *arrays: [pltpu.with_memory_space_constraint(array, pltpu.HBM) for array in arrays]
    dma = pltpu.SemaphoreType.DMA
    mask, fold = pltpu.VMEM((WIDE, WIDE), BF16), pltpu.VMEM((WIDE, WIDE), F32)
    pole_sum, short, tall = (poles, channels), (half, channels), (rows, channels)

    def call(kernel, name, ins, outs, scratch, flops, *operands):
        return pl.pallas_call(
            kernel,
            in_specs=ins,
            out_specs=[hbm if isinstance(out, jax.ShapeDtypeStruct) else vmem for out in outs],
            out_shape=outs,
            scratch_shapes=scratch,
            cost_estimate=pl.CostEstimate(flops=flops, bytes_accessed=4 * 2**20, transcendentals=10**5),
            compiler_params=params,
            name=name,
        )(*operands)

    tail = k_mr[half:] * v_mr[half:]
    rim = shifted(tail, "ctx", 1)

    mr_late, part, u_late, late, first, taptab, ends, decay, q, kli, *without_rim = call(
        local_kernel,
        "local_rows",
        [vmem] + [hbm] * 6,
        [
            pltpu.VMEM(short, BF16),
            pltpu.VMEM(short, F32),
            pltpu.VMEM(short, BF16),
            pltpu.VMEM(pole_sum, F32),
            pltpu.VMEM(pole_sum, BF16),
            pltpu.VMEM((half + width, channels), BF16),
            pltpu.VMEM((channels, half), BF16),
            pltpu.VMEM(pole_sum, F32),
            pltpu.VMEM(tall, BF16),
            pltpu.VMEM(tall, BF16),
            pltpu.VMEM(short, BF16),
            pltpu.VMEM(short, BF16),
            pltpu.VMEM(pole_sum, F32),
        ],
        [
            pltpu.VMEM(short, BF16),
            pltpu.VMEM(short, BF16),
            pltpu.VMEM((groups, tap_count), BF16),
            pltpu.VMEM((poles, groups), F32),
            mask,
            fold,
            pltpu.VMEM(tall, F32),
            dma((6,)),
        ],
        4 * 10**9,
        tail,
        *in_hbm(q_mr, k_mr, v_mr, k_li, mr_taps, li_rate.T),
    )

    peers = lax.axis_size("ctx")
    send = lambda array, pairs: lax.ppermute(array, "ctx", pairs)
    before = send(first, [(0, 1)]) if peers == 4 else jnp.zeros(pole_sum, BF16)

    litab, powers, decay, scale, qli = call(
        filter_kernel,
        "filter_tables",
        [hbm] * 3,
        [
            pltpu.VMEM(short, BF16),
            pltpu.VMEM(short, BF16),
            pltpu.VMEM(pole_sum, F32),
            pltpu.VMEM(pole_sum, F32),
            pltpu.VMEM(tall, BF16),
        ],
        [pltpu.VMEM((poles, groups), F32), pltpu.VMEM((poles, groups), F32), mask, dma((3,))],
        2 * 10**9,
        *in_hbm(q_li, li_rate.T, li_residue.T),
    )

    by_place = peers == 4
    rows_of_rim = (rim, part, q, kli, taptab, ends)
    with_rim = call(
        functools.partial(rim_kernel, by_place),
        "rim_rows",
        [vmem] * 6,
        [pltpu.VMEM(short, BF16), pltpu.VMEM(short, BF16), pltpu.VMEM(pole_sum, F32)],
        [mask, fold, pltpu.VMEM(short, F32)],
        2 * 10**9,
        *rows_of_rim,
    )
    total = (late + (with_rim[2] + before.astype(F32) * decay) * decay).astype(BF16)

    if peers == 4:
        next_but_one = send(total, [(1, 3)])
        arrived = [send(total, [(1, 2), (2, 3)]), next_but_one]
    else:
        reach = min(3, max(peers - 1, 1))
        arrived = [shifted(total, "ctx", by) for by in range(1, reach + 1)]
        rates = jnp.repeat(li_rate.T, width, axis=1)
        while reach < peers - 1:
            window = arrived[-1].astype(F32)
            for piece in arrived[-2::-1]:
                window = window * jnp.exp(-rates * rows) + piece.astype(F32)
            merged = window
            for times in (1, 2, 3):
                if times * reach < peers:
                    moved = shifted(window, "ctx", times * reach)
                    merged = merged + moved * jnp.exp(-rates * (rows * reach * times))
            arrived = [merged]
            reach *= 4

    early, near_early, near_late, mr_out = call(
        functools.partial(near_kernel, by_place),
        "near_part",
        [vmem] * 15,
        [pltpu.VMEM(pole_sum, F32), pltpu.VMEM(short, F32), pltpu.VMEM(short, F32), jax.ShapeDtypeStruct(tall, BF16)],
        [pltpu.VMEM(short, BF16), pltpu.VMEM(short, BF16), mask, fold, pltpu.VMEM(short, F32), dma((2,))],
        2 * 10**9,
        *rows_of_rim, *without_rim, *with_rim, mr_late, u_late, litab,
    )

    if peers == 4:
        arrived = [before] + arrived
    (li_out,) = call(
        functools.partial(far_kernel, peers == 4),
        "far_rows",
        [vmem] * (len(arrived) + 7),
        [jax.ShapeDtypeStruct(tall, BF16)],
        [pltpu.VMEM(tall, BF16), mask, dma((steps,))],
        10**9,
        *arrived, qli, near_early, near_late, early, powers, decay, scale,
    )
    return (mr_out, li_out)


def solution(mesh):
    seq = P(("rep", "ctx"), "tp")
    in_specs = (seq, seq, seq, seq, seq, P("tp", None), P("tp", None), P("tp", None))
    return jax.shard_map(body, mesh=mesh, in_specs=in_specs, out_specs=(seq, seq), check_vma=False)
```

```python
import functools

import jax
import jax.numpy as jnp
from jax import lax
from jax.experimental import pallas as pl
from jax.experimental.pallas import tpu as pltpu
from jax.sharding import PartitionSpec as P

F32 = jnp.float32
BF16 = jnp.bfloat16
WIDE = 256
CHUNK = 16


def shifted(array, axis, by):
    peers = lax.axis_size(axis)
    pairs = [(i, i + by) for i in range(peers) if 0 <= i + by < peers]
    return lax.ppermute(array, axis, pairs)


def iota(shape, dim):
    return lax.broadcasted_iota(jnp.int32, shape, dim)


def dot(a, b):
    return jnp.dot(a, b, preferred_element_type=F32)


def same_group(width, dtype):
    rows, cols = iota((WIDE, WIDE), 0), iota((WIDE, WIDE), 1)
    return jnp.where(rows // width == cols // width, 1.0, 0.0).astype(F32).astype(dtype)


def spread(compact, mask):
    copies = WIDE // compact.shape[0]
    return jnp.concatenate([compact] * copies, axis=0) * mask


def split(array):
    upper = array.astype(BF16)
    return upper, (array - upper.astype(F32)).astype(BF16)


def one_minus_exp(x):
    series = 1.0 - x / 7.0
    for n in (6.0, 5.0, 4.0, 3.0, 2.0):
        series = 1.0 - x / n * series
    return jnp.where(x < 0.25, x * series, 1.0 - jnp.exp(-x))


def expand_groups(per_group, first_group, width, precision=None):
    groups = per_group.shape[1]
    pick = iota((groups, WIDE), 1) // width + first_group == iota((groups, WIDE), 0)
    return jnp.dot(per_group, pick.astype(F32).astype(per_group.dtype), precision=precision, preferred_element_type=F32)


def pipelined(steps, *stages):
    for turn in range(steps + len(stages) - 1):
        for lag, stage in enumerate(stages):
            if 0 <= turn - lag < steps:
                i = turn - lag
                stage(i, slice(i * WIDE, (i + 1) * WIDE))


def rates_along(rates, width):
    on_diagonal = iota(rates.shape, 0) == iota(rates.shape, 1) % width
    return jnp.sum(jnp.where(on_diagonal, rates, 0.0), axis=0, keepdims=True)


def pole_sums(ends, u, fold_ref, poles):
    every = dot(ends, u)
    parts = []
    lanes = 128
    for at in range(0, WIDE, lanes):
        own = every[at : at + lanes, at : at + lanes] * fold_ref[at : at + lanes, at : at + lanes]
        parts.append(functools.reduce(jnp.add, [own[p : p + poles] for p in range(0, lanes, poles)]))
    return jnp.concatenate(parts, axis=1)


def local_kernel(
    tail_ref, taps_ref, rate_ref, residue_ref, q_hbm, k_hbm, v_hbm, kli_hbm,
    mr_ref, part_ref, ulate_ref, late_ref, first_ref, taptab_ref, ends_ref, decay_ref, q_ref, kli_ref,
    mr_early_ref, u_early_ref, early_ref, rates_ref, residues_ref,
    k_ref, v_ref, mask_ref, fold_ref, acc_ref, in_sem,
):
    rows, channels = k_hbm.shape
    groups, tap_count = taps_ref.shape
    steps = channels // WIDE
    width = channels // groups
    wide_groups = WIDE // width
    poles = rate_ref.shape[0]
    half = tap_count

    pairs = (
        (k_hbm.at[:half], k_ref), (v_hbm.at[:half], v_ref), (q_hbm, q_ref), (kli_hbm, kli_ref),
    )
    copies = [pltpu.make_async_copy(a, b, in_sem.at[n]) for n, (a, b) in enumerate(pairs)]
    for copy in copies:
        copy.start()

    mask_ref[...] = same_group(width, BF16)
    fold_ref[...] = same_group(width, F32)

    def tables(i, at):
        lane_item = iota((tap_count + width, WIDE), 1) % width
        own = slice(i * wide_groups, (i + 1) * wide_groups)
        pick = (iota((wide_groups, WIDE), 1) // width == iota((wide_groups, WIDE), 0)).astype(F32).astype(BF16)
        table = lax.dot_general(taps_ref[own, :], pick, (((0,), (0,)), ((), ())), preferred_element_type=F32)
        table = jnp.concatenate([table, jnp.zeros((width, WIDE), F32)], axis=0)
        step = 1
        while step < width:
            table = jnp.where((lane_item & step) != 0, pltpu.roll(table, step, 0), table)
            step *= 2
        taptab_ref[:, at] = table.astype(BF16)
        rates = expand_groups(rate_ref[...], i * wide_groups, width, lax.Precision.HIGHEST)
        rates_ref[:, at] = rates
        residues_ref[:, at] = expand_groups(residue_ref[...], i * wide_groups, width, lax.Precision.HIGHEST)
        decay_ref[:, at] = jnp.exp(-rates * half)
        left = half - 1.0 - iota((half, WIDE), 0).astype(F32)
        ends_ref[at, :] = jnp.transpose(jnp.exp(-rates_along(rates, width) * left)).astype(BF16)

    def convolve_late(i, at):
        mask = mask_ref[...]
        acc_ref[half:, at] = jnp.zeros((rows - half, WIDE), F32)
        for first in range(half, rows, width):
            u = tail_ref[first - half : first - half + width, at]
            acc_ref[first:, at] += dot(taptab_ref[: rows - first, at], spread(u, mask))

    def convolve_early(i, at):
        mask = mask_ref[...]
        u = k_ref[:, at] * v_ref[:, at]
        acc_ref[:half, at] = jnp.zeros((half, WIDE), F32)
        for first in range(0, half, width):
            count = tap_count + width
            acc_ref[first : first + count, at] += dot(taptab_ref[:, at], spread(u[first : first + width], mask))

    def gate(i, at):
        early, late = acc_ref[:half, at], acc_ref[half:, at]
        part_ref[:, at] = early
        mr = (q_ref[half:, at].astype(F32) * late).astype(BF16)
        mr_ref[:, at] = mr
        u_late = mr * kli_ref[half:, at]
        ulate_ref[:, at] = u_late
        mr_early = (q_ref[:half, at].astype(F32) * early).astype(BF16)
        mr_early_ref[:, at] = mr_early
        u_early = mr_early * kli_ref[:half, at]
        u_early_ref[:, at] = u_early
        ends = ends_ref[at, :]
        late_state = pole_sums(ends, u_late, fold_ref, poles)
        early_state = pole_sums(ends, u_early, fold_ref, poles)
        late_ref[:, at] = late_state
        early_ref[:, at] = early_state
        first_ref[:, at] = (late_state + early_state * decay_ref[:, at]).astype(BF16)

    pipelined(steps, tables)
    pipelined(steps, convolve_late)
    for copy in copies:
        copy.wait()
    pipelined(steps, convolve_early, gate)


def near_rows(u_ref, litab_ref, near_ref, mask_ref, width):
    half = u_ref.shape[0]

    def work(i, at):
        mask = mask_ref[...]
        near_ref[:, at] = jnp.zeros((half, WIDE), F32)
        u = u_ref[:, at]
        for first in range(0, half, width):
            near_ref[first:half, at] += dot(litab_ref[: half - first, at], spread(u[first : first + width], mask))

    return work


def filter_kernel(
    rates_ref, residues_ref, u_ref, qli_hbm, litab_ref, powers_ref, scale_ref, near_ref, qli_ref, mask_ref, sem
):
    half, channels = litab_ref.shape
    poles = rates_ref.shape[0]
    width = CHUNK
    steps = channels // WIDE
    copy = pltpu.make_async_copy(qli_hbm, qli_ref, sem)
    copy.start()
    mask_ref[...] = same_group(width, BF16)

    def tables(i, at):
        mask = mask_ref[...]
        rates = rates_ref[:, at]
        scale = residues_ref[:, at] * jnp.sqrt(one_minus_exp(2.0 * rates))
        scale_ref[:, at] = scale
        item = (iota((poles, WIDE), 1) % width).astype(F32)
        times = iota((half, WIDE), 0).astype(F32)
        rate_row = rates_along(rates, width)
        power = jnp.exp(-rate_row * times)
        powers_ref[:, at] = (power * jnp.exp(-rate_row)).astype(BF16)
        power_hi, power_lo = split(power)
        lift_hi, lift_lo = split(scale * jnp.exp(rates * item))
        lift_hi, lift_lo = spread(lift_hi, mask), spread(lift_lo, mask)
        li_taps = dot(power_hi, lift_hi) + dot(power_hi, lift_lo) + dot(power_lo, lift_hi)
        causal = iota((half, WIDE), 0) >= iota((half, WIDE), 1) % width
        litab_ref[:, at] = jnp.where(causal, li_taps, 0.0).astype(BF16)

    pipelined(steps, tables, near_rows(u_ref, litab_ref, near_ref, mask_ref, width))
    copy.wait()


def rim_rows(
    rim_ref, part_ref, q_ref, kli_ref, taptab_ref, ends_ref, mr_ref, u_ref, early_ref, mask_ref, fold_ref, acc_ref
):
    half, channels = rim_ref.shape
    width = taptab_ref.shape[0] - half
    poles = early_ref.shape[0]
    mask_ref[...] = same_group(width, BF16)
    fold_ref[...] = same_group(width, F32)

    def convolve(i, at):
        mask = mask_ref[...]
        rim = rim_ref[:, at]
        acc_ref[:, at] = part_ref[:, at]
        for first in range(0, half, width):
            acc_ref[: first + width, at] += dot(taptab_ref[half - first :, at], spread(rim[first : first + width], mask))

    def gate(i, at):
        mr = (q_ref[:half, at].astype(F32) * acc_ref[:, at]).astype(BF16)
        mr_ref[:, at] = mr
        u = mr * kli_ref[:half, at]
        u_ref[:, at] = u
        early_ref[:, at] = pole_sums(ends_ref[at, :], u, fold_ref, poles)

    pipelined(channels // WIDE, convolve, gate)


def rim_kernel(place, late_ref, decay_ref, before_ref, _after, *refs):
    total_ref, mr_ref, u_ref, early_ref, *scratch = refs[6:]

    def work():
        rim_rows(*refs[:6], mr_ref, u_ref, early_ref, *scratch)
        decay = decay_ref[...]
        entered = before_ref[...].astype(F32)
        total_ref[...] = (late_ref[...] + (early_ref[...] + entered * decay) * decay).astype(BF16)

    if place is None:
        work()
    else:
        pl.when(lax.axis_index("ctx") == place)(work)


def near_kernel(places, *refs):
    sets = [refs[3 * n : 3 * n + 3] for n in range(len(places))]
    (
        rim_ref, part_ref, q_ref, kli_ref, taptab_ref, ends_ref, mr_late_ref, litab_ref,
        early_ref, near_ref, mr_hbm,
        mr_ref, u_ref, mask_ref, fold_ref, acc_ref, sem,
    ) = refs[3 * len(places) :]
    half, channels = u_ref.shape
    copies = (
        pltpu.make_async_copy(mr_late_ref, mr_hbm.at[half:], sem.at[0]),
        pltpu.make_async_copy(mr_ref, mr_hbm.at[:half], sem.at[1]),
    )
    copies[0].start()

    def take(sources):
        for source, target in zip(sources, (mr_ref, u_ref, early_ref)):
            target[...] = source[...]

    if places == (None,):
        take(sets[0])
    else:
        own = (rim_ref, part_ref, q_ref, kli_ref, taptab_ref, ends_ref, mr_ref, u_ref, early_ref, mask_ref, fold_ref, acc_ref)
        at = lax.axis_index("ctx")
        for place, sources in zip(places, sets):
            pl.when(at == place)(functools.partial(take, sources))
        pl.when(at == len(places))(lambda: rim_rows(*own))
    copies[1].start()
    mask_ref[...] = same_group(CHUNK, BF16)
    pipelined(channels // WIDE, near_rows(u_ref, litab_ref, near_ref, mask_ref, CHUNK))
    for copy in copies:
        copy.wait()


def far_kernel(adjacent, *refs):
    (
        q_ref, near_early_ref, near_late_ref, early_ref, powers_ref, decay_ref, scale_ref,
        out_hbm, out_ref, mask_ref, out_sem,
    ) = refs[-11:]
    arrived = refs[:-11]
    half, channels = powers_ref.shape
    steps = channels // WIDE

    def put(i, at):
        return pltpu.make_async_copy(out_ref.at[:, at], out_hbm.at[:, at], out_sem.at[i])

    mask_ref[...] = same_group(early_ref.shape[0], BF16)

    def work(i, at):
        mask = mask_ref[...]
        scale = scale_ref[:, at]
        decay = decay_ref[:, at]
        entering = arrived[-1][:, at].astype(F32)
        for n in range(len(arrived) - 2, -1, -1):
            if n >= adjacent - 1:
                entering = entering * (decay * decay)
            entering = entering + arrived[n][:, at].astype(F32)
        middle = entering * decay + early_ref[:, at]
        powers = powers_ref[:, at]
        for first, state, near_ref in ((0, entering, near_early_ref), (half, middle, near_late_ref)):
            far = dot(powers, spread((state * scale).astype(BF16), mask))
            gate = q_ref[first : first + half, at].astype(F32)
            out_ref[first : first + half, at] = (gate * (near_ref[:, at] + far)).astype(BF16)
        put(i, at).start()

    pipelined(steps, work)
    for i in range(steps):
        put(i, slice(i * WIDE, (i + 1) * WIDE)).wait()


def body(q_mr, k_mr, v_mr, q_li, k_li, mr_taps, li_rate, li_residue):
    rows, channels = q_mr.shape
    groups, tap_count = mr_taps.shape
    poles = li_rate.shape[1]
    width = channels // groups
    half = tap_count
    assert rows == 2 * half and poles == width == CHUNK
    steps = channels // WIDE
    params = pltpu.CompilerParams(vmem_limit_bytes=40 * 1024 * 1024)
    vmem, hbm = pl.BlockSpec(memory_space=pltpu.VMEM), pl.BlockSpec(memory_space=pl.ANY)
    in_hbm = lambda *arrays: [pltpu.with_memory_space_constraint(array, pltpu.HBM) for array in arrays]
    dma = pltpu.SemaphoreType.DMA
    mask, fold = pltpu.VMEM((WIDE, WIDE), BF16), pltpu.VMEM((WIDE, WIDE), F32)
    pole_sum, short, tall = (poles, channels), (half, channels), (rows, channels)

    def call(kernel, name, ins, outs, scratch, flops, *operands):
        return pl.pallas_call(
            kernel,
            in_specs=ins,
            out_specs=[hbm if isinstance(out, jax.ShapeDtypeStruct) else vmem for out in outs],
            out_shape=outs,
            scratch_shapes=scratch,
            cost_estimate=pl.CostEstimate(flops=flops, bytes_accessed=flops // 1000, transcendentals=0),
            compiler_params=params,
            name=name,
        )(*operands)

    tail = k_mr[half:] * v_mr[half:]
    peers = lax.axis_size("ctx")
    send = lambda array, *pairs: lax.ppermute(array, "ctx", pairs)
    by_place = peers == 4
    if by_place:
        rims = [send(tail, (at, at + 1)) for at in range(3)]
    else:
        rims = [shifted(tail, "ctx", 1)]

    mr_late, part, u_late, late, first, taptab, ends, decay, q, kli, *without_rim, rates, residues = call(
        local_kernel,
        "local_rows",
        [vmem] * 4 + [hbm] * 4,
        [
            pltpu.VMEM(short, BF16),
            pltpu.VMEM(short, F32),
            pltpu.VMEM(short, BF16),
            pltpu.VMEM(pole_sum, F32),
            pltpu.VMEM(pole_sum, BF16),
            pltpu.VMEM((half + width, channels), BF16),
            pltpu.VMEM((channels, half), BF16),
            pltpu.VMEM(pole_sum, F32),
            pltpu.VMEM(tall, BF16),
            pltpu.VMEM(tall, BF16),
            pltpu.VMEM(short, BF16),
            pltpu.VMEM(short, BF16),
            pltpu.VMEM(pole_sum, F32),
            pltpu.VMEM(pole_sum, F32),
            pltpu.VMEM(pole_sum, F32),
        ],
        [
            pltpu.VMEM(short, BF16),
            pltpu.VMEM(short, BF16),
            mask,
            fold,
            pltpu.VMEM(tall, F32),
            dma((4,)),
        ],
        4 * 10**9,
        tail, mr_taps, li_rate.T, li_residue.T,
        *in_hbm(q_mr, k_mr, v_mr, k_li),
    )

    zeros = jnp.zeros(pole_sum, BF16)
    before = send(first, (0, 1)) if by_place else zeros

    litab, powers, scale, near_late, qli = call(
        filter_kernel,
        "filter_tables",
        [vmem] * 3 + [hbm],
        [
            pltpu.VMEM(short, BF16),
            pltpu.VMEM(short, BF16),
            pltpu.VMEM(pole_sum, F32),
            pltpu.VMEM(short, F32),
            pltpu.VMEM(tall, BF16),
        ],
        [mask, dma(())],
        10**7,
        rates, residues, u_late, *in_hbm(q_li),
    )

    own = (part, q, kli, taptab, ends)

    def with_rim(place, rim, entered, after):
        return call(
            functools.partial(rim_kernel, place),
            "rim_rows",
            [vmem] * 10,
            [
                pltpu.VMEM(pole_sum, BF16),
                pltpu.VMEM(short, BF16),
                pltpu.VMEM(short, BF16),
                pltpu.VMEM(pole_sum, F32),
            ],
            [mask, fold, pltpu.VMEM(short, F32)],
            10**7,
            late, decay, entered, after, rim, *own,
        )

    if by_place:
        total_1, *rim_1 = with_rim(1, rims[0], before, scale)
        two_before = send(total_1, (1, 3))
        one_before = send(total_1, (1, 2))
        total_2, *rim_2 = with_rim(2, rims[1], zeros, total_1)
        entered = before.astype(F32) + one_before.astype(F32) + two_before.astype(F32) * (decay * decay)
        arrived = [entered, send(total_2, (2, 3))]
        early_rows, places = (*without_rim, *rim_1, *rim_2), (0, 1, 2)
    else:
        total, *early_rows = with_rim(None, rims[0], zeros, scale)
        places = (None,)
        reach = min(3, max(peers - 1, 1))
        arrived = [shifted(total, "ctx", by) for by in range(1, reach + 1)]
        while reach < peers - 1:
            window = arrived[-1].astype(F32)
            for piece in arrived[-2::-1]:
                window = window * jnp.exp(-rates * rows) + piece.astype(F32)
            merged = window
            for times in (1, 2, 3):
                if times * reach < peers:
                    moved = shifted(window, "ctx", times * reach)
                    merged = merged + moved * jnp.exp(-rates * (rows * reach * times))
            arrived = [merged]
            reach *= 4

    early, near_early, mr_out = call(
        functools.partial(near_kernel, places),
        "near_part",
        [vmem] * (len(early_rows) + 8),
        [pltpu.VMEM(pole_sum, F32), pltpu.VMEM(short, F32), jax.ShapeDtypeStruct(tall, BF16)],
        [pltpu.VMEM(short, BF16), pltpu.VMEM(short, BF16), mask, fold, pltpu.VMEM(short, F32), dma((2,))],
        10**6,
        *early_rows, rims[-1], *own, mr_late, litab,
    )

    (li_out,) = call(
        functools.partial(far_kernel, 2 if by_place else 1),
        "far_rows",
        [vmem] * (len(arrived) + 7),
        [jax.ShapeDtypeStruct(tall, BF16)],
        [pltpu.VMEM(tall, BF16), mask, dma((steps,))],
        10**9,
        *arrived, qli, near_early, near_late, early, powers, decay, scale,
    )
    return (mr_out, li_out)


def solution(mesh):
    seq = P(("rep", "ctx"), "tp")
    in_specs = (seq, seq, seq, seq, seq, P("tp", None), P("tp", None), P("tp", None))
    return jax.shard_map(body, mesh=mesh, in_specs=in_specs, out_specs=(seq, seq), check_vma=False)
```

```python
import functools

import jax
import jax.numpy as jnp
from jax import lax
from jax.experimental import pallas as pl
from jax.experimental.pallas import tpu as pltpu
from jax.sharding import PartitionSpec as P

F32 = jnp.float32
BF16 = jnp.bfloat16
WIDE = 256
CHUNK = 16


def shifted(array, axis, by):
    peers = lax.axis_size(axis)
    pairs = [(i, i + by) for i in range(peers) if 0 <= i + by < peers]
    return lax.ppermute(array, axis, pairs)


def iota(shape, dim):
    return lax.broadcasted_iota(jnp.int32, shape, dim)


def dot(a, b):
    return jnp.dot(a, b, preferred_element_type=F32)


def same_group(width, dtype):
    rows, cols = iota((WIDE, WIDE), 0), iota((WIDE, WIDE), 1)
    return jnp.where(rows // width == cols // width, 1.0, 0.0).astype(F32).astype(dtype)


def spread(compact, mask):
    copies = WIDE // compact.shape[0]
    return jnp.concatenate([compact] * copies, axis=0) * mask


def split(array):
    upper = array.astype(BF16)
    return upper, (array - upper.astype(F32)).astype(BF16)


def one_minus_exp(x):
    series = 1.0 - x / 7.0
    for n in (6.0, 5.0, 4.0, 3.0, 2.0):
        series = 1.0 - x / n * series
    return jnp.where(x < 0.25, x * series, 1.0 - jnp.exp(-x))


def expand_groups(per_group, first_group, width, precision=None):
    groups = per_group.shape[1]
    pick = iota((groups, WIDE), 1) // width + first_group == iota((groups, WIDE), 0)
    return jnp.dot(per_group, pick.astype(F32).astype(per_group.dtype), precision=precision, preferred_element_type=F32)


def pipelined(steps, *stages):
    for turn in range(steps + len(stages) - 1):
        for lag, stage in enumerate(stages):
            if 0 <= turn - lag < steps:
                i = turn - lag
                stage(i, slice(i * WIDE, (i + 1) * WIDE))


def rates_along(rates, width):
    on_diagonal = iota(rates.shape, 0) == iota(rates.shape, 1) % width
    return jnp.sum(jnp.where(on_diagonal, rates, 0.0), axis=0, keepdims=True)


def pole_sums(ends, u, fold_ref, poles):
    every = dot(ends, u)
    parts = []
    lanes = 128
    for at in range(0, WIDE, lanes):
        own = every[at : at + lanes, at : at + lanes] * fold_ref[at : at + lanes, at : at + lanes]
        parts.append(functools.reduce(jnp.add, [own[p : p + poles] for p in range(0, lanes, poles)]))
    return jnp.concatenate(parts, axis=1)


def local_kernel(
    tail_ref, taps_ref, rate_ref, residue_ref, q_hbm, k_hbm, v_hbm, kli_hbm,
    mr_ref, part_ref, ulate_ref, late_ref, first_ref, taptab_ref, ends_ref, decay_ref, q_ref, kli_ref,
    mr_early_ref, u_early_ref, early_ref, rates_ref, residues_ref,
    k_ref, v_ref, mask_ref, fold_ref, acc_ref, in_sem,
):
    rows, channels = k_hbm.shape
    groups, tap_count = taps_ref.shape
    steps = channels // WIDE
    width = channels // groups
    wide_groups = WIDE // width
    poles = rate_ref.shape[0]
    half = tap_count

    pairs = (
        (k_hbm.at[:half], k_ref), (v_hbm.at[:half], v_ref), (q_hbm, q_ref), (kli_hbm, kli_ref),
    )
    copies = [pltpu.make_async_copy(a, b, in_sem.at[n]) for n, (a, b) in enumerate(pairs)]
    for copy in copies:
        copy.start()

    mask_ref[...] = same_group(width, BF16)
    fold_ref[...] = same_group(width, F32)

    def tables(i, at):
        lane_item = iota((tap_count + width, WIDE), 1) % width
        own = slice(i * wide_groups, (i + 1) * wide_groups)
        pick = (iota((wide_groups, WIDE), 1) // width == iota((wide_groups, WIDE), 0)).astype(F32).astype(BF16)
        table = lax.dot_general(taps_ref[own, :], pick, (((0,), (0,)), ((), ())), preferred_element_type=F32)
        table = jnp.concatenate([table, jnp.zeros((width, WIDE), F32)], axis=0)
        step = 1
        while step < width:
            table = jnp.where((lane_item & step) != 0, pltpu.roll(table, step, 0), table)
            step *= 2
        taptab_ref[:, at] = table.astype(BF16)
        rates = expand_groups(rate_ref[...], i * wide_groups, width, lax.Precision.HIGHEST)
        rates_ref[:, at] = rates
        residues_ref[:, at] = expand_groups(residue_ref[...], i * wide_groups, width, lax.Precision.HIGHEST)
        decay_ref[:, at] = jnp.exp(-rates * half)
        left = half - 1.0 - iota((half, WIDE), 0).astype(F32)
        ends_ref[at, :] = jnp.transpose(jnp.exp(-rates_along(rates, width) * left)).astype(BF16)

    def convolve_late(i, at):
        mask = mask_ref[...]
        acc_ref[half:, at] = jnp.zeros((rows - half, WIDE), F32)
        for first in range(half, rows, width):
            u = tail_ref[first - half : first - half + width, at]
            acc_ref[first:, at] += dot(taptab_ref[: rows - first, at], spread(u, mask))

    def convolve_early(i, at):
        mask = mask_ref[...]
        u = k_ref[:, at] * v_ref[:, at]
        acc_ref[:half, at] = jnp.zeros((half, WIDE), F32)
        for first in range(0, half, width):
            count = tap_count + width
            acc_ref[first : first + count, at] += dot(taptab_ref[:, at], spread(u[first : first + width], mask))

    def gate(i, at):
        early, late = acc_ref[:half, at], acc_ref[half:, at]
        part_ref[:, at] = early
        mr = (q_ref[half:, at].astype(F32) * late).astype(BF16)
        mr_ref[:, at] = mr
        u_late = mr * kli_ref[half:, at]
        ulate_ref[:, at] = u_late
        mr_early = (q_ref[:half, at].astype(F32) * early).astype(BF16)
        mr_early_ref[:, at] = mr_early
        u_early = mr_early * kli_ref[:half, at]
        u_early_ref[:, at] = u_early
        ends = ends_ref[at, :]
        late_state = pole_sums(ends, u_late, fold_ref, poles)
        early_state = pole_sums(ends, u_early, fold_ref, poles)
        late_ref[:, at] = late_state
        early_ref[:, at] = early_state
        first_ref[:, at] = (late_state + early_state * decay_ref[:, at]).astype(BF16)

    pipelined(steps, tables)
    pipelined(steps, convolve_late)
    for copy in copies:
        copy.wait()
    pipelined(steps, convolve_early, gate)


def near_rows(u_ref, litab_ref, near_ref, mask_ref, width):
    half = u_ref.shape[0]

    def work(i, at):
        mask = mask_ref[...]
        near_ref[:, at] = jnp.zeros((half, WIDE), F32)
        u = u_ref[:, at]
        for first in range(0, half, width):
            near_ref[first:half, at] += dot(litab_ref[: half - first, at], spread(u[first : first + width], mask))

    return work


def filter_kernel(
    rates_ref, residues_ref, u_ref, qli_hbm, litab_ref, powers_ref, scale_ref, near_ref, qli_ref, mask_ref, sem
):
    half, channels = litab_ref.shape
    poles = rates_ref.shape[0]
    width = CHUNK
    steps = channels // WIDE
    copy = pltpu.make_async_copy(qli_hbm, qli_ref, sem)
    copy.start()
    mask_ref[...] = same_group(width, BF16)

    def tables(i, at):
        mask = mask_ref[...]
        rates = rates_ref[:, at]
        scale = residues_ref[:, at] * jnp.sqrt(one_minus_exp(2.0 * rates))
        scale_ref[:, at] = scale
        item = (iota((poles, WIDE), 1) % width).astype(F32)
        times = iota((half, WIDE), 0).astype(F32)
        rate_row = rates_along(rates, width)
        power = jnp.exp(-rate_row * times)
        powers_ref[:, at] = (power * jnp.exp(-rate_row)).astype(BF16)
        power_hi, power_lo = split(power)
        lift_hi, lift_lo = split(scale * jnp.exp(rates * item))
        lift_hi, lift_lo = spread(lift_hi, mask), spread(lift_lo, mask)
        li_taps = dot(power_hi, lift_hi) + dot(power_hi, lift_lo) + dot(power_lo, lift_hi)
        causal = iota((half, WIDE), 0) >= iota((half, WIDE), 1) % width
        litab_ref[:, at] = jnp.where(causal, li_taps, 0.0).astype(BF16)

    pipelined(steps, tables, near_rows(u_ref, litab_ref, near_ref, mask_ref, width))
    copy.wait()


def rim_rows(
    rim_ref, part_ref, q_ref, kli_ref, taptab_ref, ends_ref, mr_ref, u_ref, early_ref, mask_ref, fold_ref, acc_ref
):
    half, channels = rim_ref.shape
    width = taptab_ref.shape[0] - half
    poles = early_ref.shape[0]
    mask_ref[...] = same_group(width, BF16)
    fold_ref[...] = same_group(width, F32)

    def convolve(i, at):
        mask = mask_ref[...]
        rim = rim_ref[:, at]
        acc_ref[:, at] = part_ref[:, at]
        for first in range(0, half, width):
            acc_ref[: first + width, at] += dot(taptab_ref[half - first :, at], spread(rim[first : first + width], mask))

    def gate(i, at):
        mr = (q_ref[:half, at].astype(F32) * acc_ref[:, at]).astype(BF16)
        mr_ref[:, at] = mr
        u = mr * kli_ref[:half, at]
        u_ref[:, at] = u
        early_ref[:, at] = pole_sums(ends_ref[at, :], u, fold_ref, poles)

    pipelined(channels // WIDE, convolve, gate)


def rim_kernel(place, late_ref, decay_ref, _after, *refs):
    total_ref, mr_ref, u_ref, early_ref, *scratch = refs[6:]

    def work():
        rim_rows(*refs[:6], mr_ref, u_ref, early_ref, *scratch)
        total_ref[...] = (late_ref[...] + early_ref[...] * decay_ref[...]).astype(total_ref.dtype)

    if place is None:
        work()
    else:
        pl.when(lax.axis_index("ctx") == place)(work)


def joined_kernel(own_ref, before_ref, decay_ref, total_ref):
    decay = decay_ref[...]
    total_ref[...] = (own_ref[...] + before_ref[...].astype(F32) * (decay * decay)).astype(BF16)


def near_kernel(places, *refs):
    sets = [refs[3 * n : 3 * n + 3] for n in range(len(places))]
    (
        rim_ref, part_ref, q_ref, kli_ref, taptab_ref, ends_ref, mr_late_ref, litab_ref,
        early_ref, near_ref, mr_hbm,
        mr_ref, u_ref, mask_ref, fold_ref, acc_ref, sem,
    ) = refs[3 * len(places) :]
    half, channels = u_ref.shape
    copies = (
        pltpu.make_async_copy(mr_late_ref, mr_hbm.at[half:], sem.at[0]),
        pltpu.make_async_copy(mr_ref, mr_hbm.at[:half], sem.at[1]),
    )
    copies[0].start()

    def take(sources):
        for source, target in zip(sources, (mr_ref, u_ref, early_ref)):
            target[...] = source[...]

    if places == (None,):
        take(sets[0])
    else:
        own = (rim_ref, part_ref, q_ref, kli_ref, taptab_ref, ends_ref, mr_ref, u_ref, early_ref, mask_ref, fold_ref, acc_ref)
        at = lax.axis_index("ctx")
        for place, sources in zip(places, sets):
            pl.when(at == place)(functools.partial(take, sources))
        pl.when(at == len(places))(lambda: rim_rows(*own))
    copies[1].start()
    mask_ref[...] = same_group(CHUNK, BF16)
    pipelined(channels // WIDE, near_rows(u_ref, litab_ref, near_ref, mask_ref, CHUNK))
    for copy in copies:
        copy.wait()


def far_kernel(adjacent, *refs):
    (
        q_ref, near_early_ref, near_late_ref, early_ref, powers_ref, decay_ref, scale_ref,
        out_hbm, out_ref, mask_ref, out_sem,
    ) = refs[-11:]
    arrived = refs[:-11]
    half, channels = powers_ref.shape
    steps = channels // WIDE

    def put(i, at):
        return pltpu.make_async_copy(out_ref.at[:, at], out_hbm.at[:, at], out_sem.at[i])

    mask_ref[...] = same_group(early_ref.shape[0], BF16)

    def work(i, at):
        mask = mask_ref[...]
        scale = scale_ref[:, at]
        decay = decay_ref[:, at]
        entering = arrived[-1][:, at].astype(F32)
        for n in range(len(arrived) - 2, -1, -1):
            if n >= adjacent - 1:
                entering = entering * (decay * decay)
            entering = entering + arrived[n][:, at].astype(F32)
        middle = entering * decay + early_ref[:, at]
        powers = powers_ref[:, at]
        for first, state, near_ref in ((0, entering, near_early_ref), (half, middle, near_late_ref)):
            far = dot(powers, spread((state * scale).astype(BF16), mask))
            gate = q_ref[first : first + half, at].astype(F32)
            out_ref[first : first + half, at] = (gate * (near_ref[:, at] + far)).astype(BF16)
        put(i, at).start()

    pipelined(steps, work)
    for i in range(steps):
        put(i, slice(i * WIDE, (i + 1) * WIDE)).wait()


def body(q_mr, k_mr, v_mr, q_li, k_li, mr_taps, li_rate, li_residue):
    rows, channels = q_mr.shape
    groups, tap_count = mr_taps.shape
    poles = li_rate.shape[1]
    width = channels // groups
    half = tap_count
    assert rows == 2 * half and poles == width == CHUNK
    steps = channels // WIDE
    params = pltpu.CompilerParams(vmem_limit_bytes=40 * 1024 * 1024)
    vmem, hbm = pl.BlockSpec(memory_space=pltpu.VMEM), pl.BlockSpec(memory_space=pl.ANY)
    in_hbm = lambda *arrays: [pltpu.with_memory_space_constraint(array, pltpu.HBM) for array in arrays]
    dma = pltpu.SemaphoreType.DMA
    mask, fold = pltpu.VMEM((WIDE, WIDE), BF16), pltpu.VMEM((WIDE, WIDE), F32)
    pole_sum, short, tall = (poles, channels), (half, channels), (rows, channels)

    def call(kernel, name, ins, outs, scratch, flops, *operands):
        return pl.pallas_call(
            kernel,
            in_specs=ins,
            out_specs=[hbm if isinstance(out, jax.ShapeDtypeStruct) else vmem for out in outs],
            out_shape=outs,
            scratch_shapes=scratch,
            cost_estimate=pl.CostEstimate(flops=flops, bytes_accessed=flops // 1000, transcendentals=0),
            compiler_params=params,
            name=name,
        )(*operands)

    tail = k_mr[half:] * v_mr[half:]
    peers = lax.axis_size("ctx")
    send = lambda array, *pairs: lax.ppermute(array, "ctx", pairs)
    by_place = peers == 4
    if by_place:
        rims = [send(tail, (at, at + 1)) for at in range(3)]
    else:
        rims = [shifted(tail, "ctx", 1)]

    mr_late, part, u_late, late, first, taptab, ends, decay, q, kli, *without_rim, rates, residues = call(
        local_kernel,
        "local_rows",
        [vmem] * 4 + [hbm] * 4,
        [
            pltpu.VMEM(short, BF16),
            pltpu.VMEM(short, F32),
            pltpu.VMEM(short, BF16),
            pltpu.VMEM(pole_sum, F32),
            pltpu.VMEM(pole_sum, BF16),
            pltpu.VMEM((half + width, channels), BF16),
            pltpu.VMEM((channels, half), BF16),
            pltpu.VMEM(pole_sum, F32),
            pltpu.VMEM(tall, BF16),
            pltpu.VMEM(tall, BF16),
            pltpu.VMEM(short, BF16),
            pltpu.VMEM(short, BF16),
            pltpu.VMEM(pole_sum, F32),
            pltpu.VMEM(pole_sum, F32),
            pltpu.VMEM(pole_sum, F32),
        ],
        [
            pltpu.VMEM(short, BF16),
            pltpu.VMEM(short, BF16),
            mask,
            fold,
            pltpu.VMEM(tall, F32),
            dma((4,)),
        ],
        4 * 10**9,
        tail, mr_taps, li_rate.T, li_residue.T,
        *in_hbm(q_mr, k_mr, v_mr, k_li),
    )

    before = send(first, (0, 1)) if by_place else None

    litab, powers, scale, near_late, qli = call(
        filter_kernel,
        "filter_tables",
        [vmem] * 3 + [hbm],
        [
            pltpu.VMEM(short, BF16),
            pltpu.VMEM(short, BF16),
            pltpu.VMEM(pole_sum, F32),
            pltpu.VMEM(short, F32),
            pltpu.VMEM(tall, BF16),
        ],
        [mask, dma(())],
        10**6,
        rates, residues, u_late, *in_hbm(q_li),
    )

    own = (part, q, kli, taptab, ends)

    def with_rim(place, rim, after, dtype):
        return call(
            functools.partial(rim_kernel, place),
            "rim_rows",
            [vmem] * 9,
            [
                pltpu.VMEM(pole_sum, dtype),
                pltpu.VMEM(short, BF16),
                pltpu.VMEM(short, BF16),
                pltpu.VMEM(pole_sum, F32),
            ],
            [mask, fold, pltpu.VMEM(short, F32)],
            10**6,
            late, decay, after, rim, *own,
        )

    if by_place:
        total_1, *rim_1 = with_rim(1, rims[0], scale, F32)
        (total_1,) = call(
            joined_kernel,
            "joined_sums",
            [vmem] * 3,
            [pltpu.VMEM(pole_sum, BF16)],
            [],
            10**6,
            total_1, before, decay,
        )
        two_before = send(total_1, (1, 3))
        one_before = send(total_1, (1, 2))
        total_2, *rim_2 = with_rim(2, rims[1], total_1, BF16)
        entered = before.astype(F32) + one_before.astype(F32) + two_before.astype(F32) * (decay * decay)
        arrived = [entered, send(total_2, (2, 3))]
        early_rows, places = (*without_rim, *rim_1, *rim_2), (0, 1, 2)
    else:
        total, *early_rows = with_rim(None, rims[0], scale, BF16)
        places = (None,)
        reach = min(3, max(peers - 1, 1))
        arrived = [shifted(total, "ctx", by) for by in range(1, reach + 1)]
        while reach < peers - 1:
            window = arrived[-1].astype(F32)
            for piece in arrived[-2::-1]:
                window = window * jnp.exp(-rates * rows) + piece.astype(F32)
            merged = window
            for times in (1, 2, 3):
                if times * reach < peers:
                    moved = shifted(window, "ctx", times * reach)
                    merged = merged + moved * jnp.exp(-rates * (rows * reach * times))
            arrived = [merged]
            reach *= 4

    early, near_early, mr_out = call(
        functools.partial(near_kernel, places),
        "near_part",
        [vmem] * (len(early_rows) + 8),
        [pltpu.VMEM(pole_sum, F32), pltpu.VMEM(short, F32), jax.ShapeDtypeStruct(tall, BF16)],
        [pltpu.VMEM(short, BF16), pltpu.VMEM(short, BF16), mask, fold, pltpu.VMEM(short, F32), dma((2,))],
        10**6,
        *early_rows, rims[-1], *own, mr_late, litab,
    )

    (li_out,) = call(
        functools.partial(far_kernel, 2 if by_place else 1),
        "far_rows",
        [vmem] * (len(arrived) + 7),
        [jax.ShapeDtypeStruct(tall, BF16)],
        [pltpu.VMEM(tall, BF16), mask, dma((steps,))],
        10**9,
        *arrived, qli, near_early, near_late, early, powers, decay, scale,
    )
    return (mr_out, li_out)


def solution(mesh):
    seq = P(("rep", "ctx"), "tp")
    in_specs = (seq, seq, seq, seq, seq, P("tp", None), P("tp", None), P("tp", None))
    return jax.shard_map(body, mesh=mesh, in_specs=in_specs, out_specs=(seq, seq), check_vma=False)
```

```python
import functools

import jax
import jax.numpy as jnp
from jax import lax
from jax.experimental import pallas as pl
from jax.experimental.pallas import tpu as pltpu
from jax.sharding import PartitionSpec as P

F32 = jnp.float32
BF16 = jnp.bfloat16
WIDE = 256
CHUNK = 16


def shifted(array, axis, by):
    peers = lax.axis_size(axis)
    pairs = [(i, i + by) for i in range(peers) if 0 <= i + by < peers]
    return lax.ppermute(array, axis, pairs)


def iota(shape, dim):
    return lax.broadcasted_iota(jnp.int32, shape, dim)


def dot(a, b):
    return jnp.dot(a, b, preferred_element_type=F32)


def same_group(width, dtype):
    rows, cols = iota((WIDE, WIDE), 0), iota((WIDE, WIDE), 1)
    return jnp.where(rows // width == cols // width, 1.0, 0.0).astype(F32).astype(dtype)


def spread(compact, mask):
    copies = WIDE // compact.shape[0]
    return jnp.concatenate([compact] * copies, axis=0) * mask


def split(array):
    upper = array.astype(BF16)
    return upper, (array - upper.astype(F32)).astype(BF16)


def one_minus_exp(x):
    series = 1.0 - x / 7.0
    for n in (6.0, 5.0, 4.0, 3.0, 2.0):
        series = 1.0 - x / n * series
    return jnp.where(x < 0.25, x * series, 1.0 - jnp.exp(-x))


def expand_groups(per_group, first_group, width, precision=None):
    groups = per_group.shape[1]
    pick = iota((groups, WIDE), 1) // width + first_group == iota((groups, WIDE), 0)
    return jnp.dot(per_group, pick.astype(F32).astype(per_group.dtype), precision=precision, preferred_element_type=F32)


def pipelined(steps, *stages, lag=1):
    for turn in range(steps + lag * (len(stages) - 1)):
        for n, stage in enumerate(stages):
            i = turn - lag * n
            if 0 <= i < steps:
                stage(i, slice(i * WIDE, (i + 1) * WIDE))


def rates_along(rates, width):
    on_diagonal = iota(rates.shape, 0) == iota(rates.shape, 1) % width
    return jnp.sum(jnp.where(on_diagonal, rates, 0.0), axis=0, keepdims=True)


def pole_sums(ends, u, fold_ref, poles):
    every = dot(ends, u)
    parts = []
    lanes = 128
    for at in range(0, WIDE, lanes):
        own = every[at : at + lanes, at : at + lanes] * fold_ref[at : at + lanes, at : at + lanes]
        parts.append(functools.reduce(jnp.add, [own[p : p + poles] for p in range(0, lanes, poles)]))
    return jnp.concatenate(parts, axis=1)


def local_kernel(
    tail_ref, taps_ref, rate_ref, residue_ref, q_hbm, k_hbm, v_hbm, kli_hbm,
    mr_ref, part_ref, ulate_ref, late_ref, first_ref, taptab_ref, ends_ref, decay_ref, q_ref, kli_ref,
    mr_early_ref, u_early_ref, early_ref, rates_ref, residues_ref,
    k_ref, v_ref, mask_ref, fold_ref, acc_ref, in_sem,
):
    rows, channels = k_hbm.shape
    groups, tap_count = taps_ref.shape
    steps = channels // WIDE
    width = channels // groups
    wide_groups = WIDE // width
    poles = rate_ref.shape[0]
    half = tap_count

    pairs = (
        (k_hbm.at[:half], k_ref), (v_hbm.at[:half], v_ref), (q_hbm, q_ref), (kli_hbm, kli_ref),
    )
    copies = [pltpu.make_async_copy(a, b, in_sem.at[n]) for n, (a, b) in enumerate(pairs)]
    for copy in copies:
        copy.start()

    mask_ref[...] = same_group(width, BF16)
    fold_ref[...] = same_group(width, F32)

    def tables(i, at):
        lane_item = iota((tap_count + width, WIDE), 1) % width
        own = slice(i * wide_groups, (i + 1) * wide_groups)
        pick = (iota((wide_groups, WIDE), 1) // width == iota((wide_groups, WIDE), 0)).astype(F32).astype(BF16)
        table = lax.dot_general(taps_ref[own, :], pick, (((0,), (0,)), ((), ())), preferred_element_type=F32)
        table = jnp.concatenate([table, jnp.zeros((width, WIDE), F32)], axis=0)
        step = 1
        while step < width:
            table = jnp.where((lane_item & step) != 0, pltpu.roll(table, step, 0), table)
            step *= 2
        taptab_ref[:, at] = table.astype(BF16)
        rates = expand_groups(rate_ref[...], i * wide_groups, width, lax.Precision.HIGHEST)
        rates_ref[:, at] = rates
        residues_ref[:, at] = expand_groups(residue_ref[...], i * wide_groups, width, lax.Precision.HIGHEST)
        decay_ref[:, at] = jnp.exp(-rates * half)
        left = half - 1.0 - iota((half, WIDE), 0).astype(F32)
        ends_ref[at, :] = jnp.transpose(jnp.exp(-rates_along(rates, width) * left)).astype(BF16)

    def convolve_late(i, at):
        mask = mask_ref[...]
        acc_ref[half:, at] = jnp.zeros((rows - half, WIDE), F32)
        for first in range(half, rows, width):
            u = tail_ref[first - half : first - half + width, at]
            acc_ref[first:, at] += dot(taptab_ref[: rows - first, at], spread(u, mask))

    def convolve_early(i, at):
        mask = mask_ref[...]
        u = k_ref[:, at] * v_ref[:, at]
        acc_ref[:half, at] = jnp.zeros((half, WIDE), F32)
        for first in range(0, half, width):
            count = tap_count + width
            acc_ref[first : first + count, at] += dot(taptab_ref[:, at], spread(u[first : first + width], mask))

    def gate(i, at):
        early, late = acc_ref[:half, at], acc_ref[half:, at]
        part_ref[:, at] = early
        mr = (q_ref[half:, at].astype(F32) * late).astype(BF16)
        mr_ref[:, at] = mr
        u_late = mr * kli_ref[half:, at]
        ulate_ref[:, at] = u_late
        mr_early = (q_ref[:half, at].astype(F32) * early).astype(BF16)
        mr_early_ref[:, at] = mr_early
        u_early = mr_early * kli_ref[:half, at]
        u_early_ref[:, at] = u_early
        ends = ends_ref[at, :]
        late_state = pole_sums(ends, u_late, fold_ref, poles)
        early_state = pole_sums(ends, u_early, fold_ref, poles)
        late_ref[:, at] = late_state
        early_ref[:, at] = early_state
        first_ref[:, at] = (late_state + early_state * decay_ref[:, at]).astype(BF16)

    pipelined(steps, tables)
    pipelined(steps, convolve_late)
    for copy in copies:
        copy.wait()
    pipelined(steps, convolve_early, gate, lag=3)


def near_rows(u_ref, litab_ref, near_ref, mask_ref, width):
    half = u_ref.shape[0]

    def work(i, at):
        mask = mask_ref[...]
        near_ref[:, at] = jnp.zeros((half, WIDE), F32)
        u = u_ref[:, at]
        for first in range(0, half, width):
            near_ref[first:half, at] += dot(litab_ref[: half - first, at], spread(u[first : first + width], mask))

    return work


def filter_kernel(
    rates_ref, residues_ref, u_ref, qli_hbm, litab_ref, powers_ref, scale_ref, near_ref, qli_ref, mask_ref, sem
):
    half, channels = litab_ref.shape
    poles = rates_ref.shape[0]
    width = CHUNK
    steps = channels // WIDE
    copy = pltpu.make_async_copy(qli_hbm, qli_ref, sem)
    copy.start()
    mask_ref[...] = same_group(width, BF16)

    def tables(i, at):
        mask = mask_ref[...]
        rates = rates_ref[:, at]
        scale = residues_ref[:, at] * jnp.sqrt(one_minus_exp(2.0 * rates))
        scale_ref[:, at] = scale
        item = (iota((poles, WIDE), 1) % width).astype(F32)
        times = iota((half, WIDE), 0).astype(F32)
        rate_row = rates_along(rates, width)
        power = jnp.exp(-rate_row * times)
        powers_ref[:, at] = (power * jnp.exp(-rate_row)).astype(BF16)
        power_hi, power_lo = split(power)
        lift_hi, lift_lo = split(scale * jnp.exp(rates * item))
        lift_hi, lift_lo = spread(lift_hi, mask), spread(lift_lo, mask)
        li_taps = dot(power_hi, lift_hi) + dot(power_hi, lift_lo) + dot(power_lo, lift_hi)
        causal = iota((half, WIDE), 0) >= iota((half, WIDE), 1) % width
        litab_ref[:, at] = jnp.where(causal, li_taps, 0.0).astype(BF16)

    pipelined(steps, tables, near_rows(u_ref, litab_ref, near_ref, mask_ref, width))
    copy.wait()


def rim_rows(
    rim_ref, part_ref, q_ref, kli_ref, taptab_ref, ends_ref, mr_ref, u_ref, early_ref, mask_ref, fold_ref, acc_ref
):
    half, channels = rim_ref.shape
    width = taptab_ref.shape[0] - half
    poles = early_ref.shape[0]
    mask_ref[...] = same_group(width, BF16)
    fold_ref[...] = same_group(width, F32)

    def convolve(i, at):
        mask = mask_ref[...]
        rim = rim_ref[:, at]
        acc_ref[:, at] = part_ref[:, at]
        for first in range(half - width, -1, -width):
            acc_ref[: first + width, at] += dot(taptab_ref[half - first :, at], spread(rim[first : first + width], mask))

    def gate(i, at):
        mr = (q_ref[:half, at].astype(F32) * acc_ref[:, at]).astype(BF16)
        mr_ref[:, at] = mr
        u = mr * kli_ref[:half, at]
        u_ref[:, at] = u
        early_ref[:, at] = pole_sums(ends_ref[at, :], u, fold_ref, poles)

    pipelined(channels // WIDE, convolve, gate, lag=4)


def rim_kernel(place, late_ref, decay_ref, _after, *refs):
    total_ref, mr_ref, u_ref, early_ref, *scratch = refs[6:]

    def work():
        rim_rows(*refs[:6], mr_ref, u_ref, early_ref, *scratch)
        total_ref[...] = (late_ref[...] + early_ref[...] * decay_ref[...]).astype(total_ref.dtype)

    if place is None:
        work()
    else:
        pl.when(lax.axis_index("ctx") == place)(work)


def joined_kernel(own_ref, before_ref, decay_ref, total_ref):
    decay = decay_ref[...]
    total_ref[...] = (own_ref[...] + before_ref[...].astype(F32) * (decay * decay)).astype(BF16)


def near_kernel(places, *refs):
    sets = [refs[3 * n : 3 * n + 3] for n in range(len(places))]
    (
        rim_ref, part_ref, q_ref, kli_ref, taptab_ref, ends_ref, mr_late_ref, litab_ref,
        early_ref, near_ref, mr_hbm,
        mr_ref, u_ref, mask_ref, fold_ref, acc_ref, sem,
    ) = refs[3 * len(places) :]
    half, channels = u_ref.shape
    copies = (
        pltpu.make_async_copy(mr_late_ref, mr_hbm.at[half:], sem.at[0]),
        pltpu.make_async_copy(mr_ref, mr_hbm.at[:half], sem.at[1]),
    )
    copies[0].start()

    def take(sources):
        for source, target in zip(sources, (mr_ref, u_ref, early_ref)):
            target[...] = source[...]

    if places == (None,):
        take(sets[0])
    else:
        own = (rim_ref, part_ref, q_ref, kli_ref, taptab_ref, ends_ref, mr_ref, u_ref, early_ref, mask_ref, fold_ref, acc_ref)
        at = lax.axis_index("ctx")
        for place, sources in zip(places, sets):
            pl.when(at == place)(functools.partial(take, sources))
        pl.when(at == len(places))(lambda: rim_rows(*own))
    copies[1].start()
    mask_ref[...] = same_group(CHUNK, BF16)
    pipelined(channels // WIDE, near_rows(u_ref, litab_ref, near_ref, mask_ref, CHUNK))
    for copy in copies:
        copy.wait()


def far_kernel(adjacent, *refs):
    (
        q_ref, near_early_ref, near_late_ref, early_ref, powers_ref, decay_ref, scale_ref,
        out_hbm, out_ref, mask_ref, out_sem,
    ) = refs[-11:]
    arrived = refs[:-11]
    half, channels = powers_ref.shape
    steps = channels // WIDE

    def put(i, at):
        return pltpu.make_async_copy(out_ref.at[:, at], out_hbm.at[:, at], out_sem.at[i])

    mask_ref[...] = same_group(early_ref.shape[0], BF16)

    def work(i, at):
        mask = mask_ref[...]
        scale = scale_ref[:, at]
        decay = decay_ref[:, at]
        entering = arrived[-1][:, at].astype(F32)
        for n in range(len(arrived) - 2, -1, -1):
            if n >= adjacent - 1:
                entering = entering * (decay * decay)
            entering = entering + arrived[n][:, at].astype(F32)
        middle = entering * decay + early_ref[:, at]
        powers = powers_ref[:, at]
        for first, state, near_ref in ((0, entering, near_early_ref), (half, middle, near_late_ref)):
            far = dot(powers, spread((state * scale).astype(BF16), mask))
            gate = q_ref[first : first + half, at].astype(F32)
            out_ref[first : first + half, at] = (gate * (near_ref[:, at] + far)).astype(BF16)
        put(i, at).start()

    pipelined(steps, work)
    for i in range(steps):
        put(i, slice(i * WIDE, (i + 1) * WIDE)).wait()


def body(q_mr, k_mr, v_mr, q_li, k_li, mr_taps, li_rate, li_residue):
    rows, channels = q_mr.shape
    groups, tap_count = mr_taps.shape
    poles = li_rate.shape[1]
    width = channels // groups
    half = tap_count
    assert rows == 2 * half and poles == width == CHUNK
    steps = channels // WIDE
    params = pltpu.CompilerParams(vmem_limit_bytes=40 * 1024 * 1024)
    vmem, hbm = pl.BlockSpec(memory_space=pltpu.VMEM), pl.BlockSpec(memory_space=pl.ANY)
    in_hbm = lambda *arrays: [pltpu.with_memory_space_constraint(array, pltpu.HBM) for array in arrays]
    dma = pltpu.SemaphoreType.DMA
    mask, fold = pltpu.VMEM((WIDE, WIDE), BF16), pltpu.VMEM((WIDE, WIDE), F32)
    pole_sum, short, tall = (poles, channels), (half, channels), (rows, channels)

    def call(kernel, name, ins, outs, scratch, flops, *operands):
        return pl.pallas_call(
            kernel,
            in_specs=ins,
            out_specs=[hbm if isinstance(out, jax.ShapeDtypeStruct) else vmem for out in outs],
            out_shape=outs,
            scratch_shapes=scratch,
            cost_estimate=pl.CostEstimate(flops=flops, bytes_accessed=flops // 1000, transcendentals=0),
            compiler_params=params,
            name=name,
        )(*operands)

    tail = k_mr[half:] * v_mr[half:]
    peers = lax.axis_size("ctx")
    send = lambda array, *pairs: lax.ppermute(array, "ctx", pairs)
    by_place = peers == 4
    if by_place:
        rims = [send(tail, (at, at + 1)) for at in range(3)]
    else:
        rims = [shifted(tail, "ctx", 1)]

    mr_late, part, u_late, late, first, taptab, ends, decay, q, kli, *without_rim, rates, residues = call(
        local_kernel,
        "local_rows",
        [vmem] * 4 + [hbm] * 4,
        [
            pltpu.VMEM(short, BF16),
            pltpu.VMEM(short, F32),
            pltpu.VMEM(short, BF16),
            pltpu.VMEM(pole_sum, F32),
            pltpu.VMEM(pole_sum, BF16),
            pltpu.VMEM((half + width, channels), BF16),
            pltpu.VMEM((channels, half), BF16),
            pltpu.VMEM(pole_sum, F32),
            pltpu.VMEM(tall, BF16),
            pltpu.VMEM(tall, BF16),
            pltpu.VMEM(short, BF16),
            pltpu.VMEM(short, BF16),
            pltpu.VMEM(pole_sum, F32),
            pltpu.VMEM(pole_sum, F32),
            pltpu.VMEM(pole_sum, F32),
        ],
        [
            pltpu.VMEM(short, BF16),
            pltpu.VMEM(short, BF16),
            mask,
            fold,
            pltpu.VMEM(tall, F32),
            dma((4,)),
        ],
        4 * 10**9,
        tail, mr_taps, li_rate.T, li_residue.T,
        *in_hbm(q_mr, k_mr, v_mr, k_li),
    )

    before = send(first, (0, 1)) if by_place else None

    litab, powers, scale, near_late, qli = call(
        filter_kernel,
        "filter_tables",
        [vmem] * 3 + [hbm],
        [
            pltpu.VMEM(short, BF16),
            pltpu.VMEM(short, BF16),
            pltpu.VMEM(pole_sum, F32),
            pltpu.VMEM(short, F32),
            pltpu.VMEM(tall, BF16),
        ],
        [mask, dma(())],
        10**6,
        rates, residues, u_late, *in_hbm(q_li),
    )

    own = (part, q, kli, taptab, ends)

    def with_rim(place, rim, after, dtype):
        return call(
            functools.partial(rim_kernel, place),
            "rim_rows",
            [vmem] * 9,
            [
                pltpu.VMEM(pole_sum, dtype),
                pltpu.VMEM(short, BF16),
                pltpu.VMEM(short, BF16),
                pltpu.VMEM(pole_sum, F32),
            ],
            [mask, fold, pltpu.VMEM(short, F32)],
            10**6,
            late, decay, after, rim, *own,
        )

    if by_place:
        total_1, *rim_1 = with_rim(1, rims[0], scale, F32)
        (total_1,) = call(
            joined_kernel,
            "joined_sums",
            [vmem] * 3,
            [pltpu.VMEM(pole_sum, BF16)],
            [],
            10**6,
            total_1, before, decay,
        )
        two_before = send(total_1, (1, 3))
        one_before = send(total_1, (1, 2))
        total_2, *rim_2 = with_rim(2, rims[1], total_1, BF16)
        entered = before.astype(F32) + one_before.astype(F32) + two_before.astype(F32) * (decay * decay)
        arrived = [entered, send(total_2, (2, 3))]
        early_rows, places = (*without_rim, *rim_1, *rim_2), (0, 1, 2)
    else:
        total, *early_rows = with_rim(None, rims[0], scale, BF16)
        places = (None,)
        reach = min(3, max(peers - 1, 1))
        arrived = [shifted(total, "ctx", by) for by in range(1, reach + 1)]
        while reach < peers - 1:
            window = arrived[-1].astype(F32)
            for piece in arrived[-2::-1]:
                window = window * jnp.exp(-rates * rows) + piece.astype(F32)
            merged = window
            for times in (1, 2, 3):
                if times * reach < peers:
                    moved = shifted(window, "ctx", times * reach)
                    merged = merged + moved * jnp.exp(-rates * (rows * reach * times))
            arrived = [merged]
            reach *= 4

    early, near_early, mr_out = call(
        functools.partial(near_kernel, places),
        "near_part",
        [vmem] * (len(early_rows) + 8),
        [pltpu.VMEM(pole_sum, F32), pltpu.VMEM(short, F32), jax.ShapeDtypeStruct(tall, BF16)],
        [pltpu.VMEM(short, BF16), pltpu.VMEM(short, BF16), mask, fold, pltpu.VMEM(short, F32), dma((2,))],
        10**6,
        *early_rows, rims[-1], *own, mr_late, litab,
    )

    (li_out,) = call(
        functools.partial(far_kernel, 2 if by_place else 1),
        "far_rows",
        [vmem] * (len(arrived) + 7),
        [jax.ShapeDtypeStruct(tall, BF16)],
        [pltpu.VMEM(tall, BF16), mask, dma((steps,))],
        10**9,
        *arrived, qli, near_early, near_late, early, powers, decay, scale,
    )
    return (mr_out, li_out)


def solution(mesh):
    seq = P(("rep", "ctx"), "tp")
    in_specs = (seq, seq, seq, seq, seq, P("tp", None), P("tp", None), P("tp", None))
    return jax.shard_map(body, mesh=mesh, in_specs=in_specs, out_specs=(seq, seq), check_vma=False)
```

```python
import functools

import jax
import jax.numpy as jnp
from jax import lax
from jax.experimental import pallas as pl
from jax.experimental.pallas import tpu as pltpu
from jax.sharding import PartitionSpec as P

F32 = jnp.float32
BF16 = jnp.bfloat16
WIDE = 256
CHUNK = 16


def shifted(array, axis, by):
    peers = lax.axis_size(axis)
    pairs = [(i, i + by) for i in range(peers) if 0 <= i + by < peers]
    return lax.ppermute(array, axis, pairs)


def iota(shape, dim):
    return lax.broadcasted_iota(jnp.int32, shape, dim)


def dot(a, b):
    return jnp.dot(a, b, preferred_element_type=F32)


def same_group(width, dtype):
    rows, cols = iota((WIDE, WIDE), 0), iota((WIDE, WIDE), 1)
    return jnp.where(rows // width == cols // width, 1.0, 0.0).astype(F32).astype(dtype)


def spread(compact, mask):
    copies = WIDE // compact.shape[0]
    return jnp.concatenate([compact] * copies, axis=0) * mask


def split(array):
    upper = array.astype(BF16)
    return upper, (array - upper.astype(F32)).astype(BF16)


def one_minus_exp(x):
    series = 1.0 - x / 7.0
    for n in (6.0, 5.0, 4.0, 3.0, 2.0):
        series = 1.0 - x / n * series
    return jnp.where(x < 0.25, x * series, 1.0 - jnp.exp(-x))


def expand_groups(per_group, first_group, width, precision=None):
    groups = per_group.shape[1]
    pick = iota((groups, WIDE), 1) // width + first_group == iota((groups, WIDE), 0)
    return jnp.dot(per_group, pick.astype(F32).astype(per_group.dtype), precision=precision, preferred_element_type=F32)


def pipelined(steps, *stages, lag=1):
    for turn in range(steps + lag * (len(stages) - 1)):
        for n, stage in enumerate(stages):
            i = turn - lag * n
            if 0 <= i < steps:
                stage(i, slice(i * WIDE, (i + 1) * WIDE))


def rates_along(rates, width):
    on_diagonal = iota(rates.shape, 0) == iota(rates.shape, 1) % width
    return jnp.sum(jnp.where(on_diagonal, rates, 0.0), axis=0, keepdims=True)


def pole_sums(ends, u, fold_ref, poles):
    every = dot(ends, u)
    parts = []
    lanes = 128
    for at in range(0, WIDE, lanes):
        own = every[at : at + lanes, at : at + lanes] * fold_ref[at : at + lanes, at : at + lanes]
        parts.append(functools.reduce(jnp.add, [own[p : p + poles] for p in range(0, lanes, poles)]))
    return jnp.concatenate(parts, axis=1)


def local_kernel(
    tail_ref, taps_ref, rate_ref, residue_ref, q_hbm, k_hbm, v_hbm, kli_hbm,
    mr_ref, part_ref, ulate_ref, late_ref, taptab_ref, ends_ref, decay_ref, q_ref, kli_ref,
    mr_early_ref, u_early_ref, early_ref, rates_ref, residues_ref,
    k_ref, v_ref, mask_ref, fold_ref, acc_ref, in_sem,
):
    rows, channels = k_hbm.shape
    groups, tap_count = taps_ref.shape
    steps = channels // WIDE
    width = channels // groups
    wide_groups = WIDE // width
    poles = rate_ref.shape[0]
    half = tap_count

    pairs = (
        (k_hbm.at[:half], k_ref), (v_hbm.at[:half], v_ref), (q_hbm, q_ref), (kli_hbm, kli_ref),
    )
    copies = [pltpu.make_async_copy(a, b, in_sem.at[n]) for n, (a, b) in enumerate(pairs)]
    for copy in copies:
        copy.start()

    mask_ref[...] = same_group(width, BF16)
    fold_ref[...] = same_group(width, F32)

    def tables(i, at):
        lane_item = iota((tap_count + width, WIDE), 1) % width
        own = slice(i * wide_groups, (i + 1) * wide_groups)
        pick = (iota((wide_groups, WIDE), 1) // width == iota((wide_groups, WIDE), 0)).astype(F32).astype(BF16)
        table = lax.dot_general(taps_ref[own, :], pick, (((0,), (0,)), ((), ())), preferred_element_type=F32)
        table = jnp.concatenate([table, jnp.zeros((width, WIDE), F32)], axis=0)
        step = 1
        while step < width:
            table = jnp.where((lane_item & step) != 0, pltpu.roll(table, step, 0), table)
            step *= 2
        taptab_ref[:, at] = table.astype(BF16)
        rates = expand_groups(rate_ref[...], i * wide_groups, width, lax.Precision.HIGHEST)
        rates_ref[:, at] = rates
        residues_ref[:, at] = expand_groups(residue_ref[...], i * wide_groups, width, lax.Precision.HIGHEST)
        decay_ref[:, at] = jnp.exp(-rates * half)
        left = half - 1.0 - iota((half, WIDE), 0).astype(F32)
        ends_ref[at, :] = jnp.transpose(jnp.exp(-rates_along(rates, width) * left)).astype(BF16)

    def convolve_late(i, at):
        mask = mask_ref[...]
        for first in range(half, rows, width):
            u = tail_ref[first - half : first - half + width, at]
            reached = dot(taptab_ref[: rows - first, at], spread(u, mask))
            acc_ref[first:, at] = acc_ref[first:, at] + reached if first > half else reached

    def convolve_early(i, at):
        mask = mask_ref[...]
        u = k_ref[:, at] * v_ref[:, at]
        acc_ref[:half, at] = jnp.zeros((half, WIDE), F32)
        for first in range(0, half, width):
            count = tap_count + width
            acc_ref[first : first + count, at] += dot(taptab_ref[:, at], spread(u[first : first + width], mask))

    def gate(i, at):
        early, late = acc_ref[:half, at], acc_ref[half:, at]
        part_ref[:, at] = early
        mr = (q_ref[half:, at].astype(F32) * late).astype(BF16)
        mr_ref[:, at] = mr
        u_late = mr * kli_ref[half:, at]
        ulate_ref[:, at] = u_late
        mr_early = (q_ref[:half, at].astype(F32) * early).astype(BF16)
        mr_early_ref[:, at] = mr_early
        u_early = mr_early * kli_ref[:half, at]
        u_early_ref[:, at] = u_early
        ends = ends_ref[at, :]
        late_ref[:, at] = pole_sums(ends, u_late, fold_ref, poles)
        early_ref[:, at] = pole_sums(ends, u_early, fold_ref, poles)

    pipelined(steps, tables)
    pipelined(steps, convolve_late)
    for copy in copies:
        copy.wait()
    pipelined(steps, convolve_early, gate, lag=3)


def near_rows(u_ref, litab_ref, near_ref, mask_ref, width):
    half = u_ref.shape[0]

    def work(i, at):
        mask = mask_ref[...]
        u = u_ref[:, at]
        for first in range(0, half, width):
            reached = dot(litab_ref[: half - first, at], spread(u[first : first + width], mask))
            near_ref[first:half, at] = near_ref[first:half, at] + reached if first else reached

    return work


def filter_kernel(
    rates_ref, residues_ref, late_ref, early_ref, decay_ref, qli_hbm,
    first_ref, litab_ref, powers_ref, scale_ref, qli_ref,
    mask_ref, sem,
):
    half, channels = litab_ref.shape
    poles = rates_ref.shape[0]
    width = CHUNK
    steps = channels // WIDE
    copy = pltpu.make_async_copy(qli_hbm, qli_ref, sem)
    copy.start()
    first_ref[...] = (late_ref[...] + early_ref[...] * decay_ref[...]).astype(BF16)
    mask_ref[...] = same_group(width, BF16)

    def tables(i, at):
        mask = mask_ref[...]
        rates = rates_ref[:, at]
        scale = residues_ref[:, at] * jnp.sqrt(one_minus_exp(2.0 * rates))
        scale_ref[:, at] = scale
        item = (iota((poles, WIDE), 1) % width).astype(F32)
        times = iota((half, WIDE), 0).astype(F32)
        rate_row = rates_along(rates, width)
        power = jnp.exp(-rate_row * times)
        powers_ref[:, at] = (power * jnp.exp(-rate_row)).astype(BF16)
        power_hi, power_lo = split(power)
        lift_hi, lift_lo = split(scale * jnp.exp(rates * item))
        lift_hi, lift_lo = spread(lift_hi, mask), spread(lift_lo, mask)
        li_taps = dot(power_hi, lift_hi) + dot(power_hi, lift_lo) + dot(power_lo, lift_hi)
        causal = iota((half, WIDE), 0) >= iota((half, WIDE), 1) % width
        litab_ref[:, at] = jnp.where(causal, li_taps, 0.0).astype(BF16)

    pipelined(steps, tables)
    copy.wait()


def near_late_kernel(u_ref, litab_ref, near_ref, mask_ref):
    mask_ref[...] = same_group(CHUNK, BF16)
    pipelined(u_ref.shape[1] // WIDE, near_rows(u_ref, litab_ref, near_ref, mask_ref, CHUNK))


def rim_rows(
    rim_ref, part_ref, q_ref, kli_ref, taptab_ref, ends_ref, mr_ref, u_ref, early_ref, mask_ref, fold_ref, acc_ref
):
    half, channels = rim_ref.shape
    width = taptab_ref.shape[0] - half
    poles = early_ref.shape[0]
    mask_ref[...] = same_group(width, BF16)
    fold_ref[...] = same_group(width, F32)

    def convolve(i, at):
        mask = mask_ref[...]
        rim = rim_ref[:, at]
        for first in range(half - width, -1, -width):
            reached = dot(taptab_ref[half - first :, at], spread(rim[first : first + width], mask))
            before_ref = part_ref if first == half - width else acc_ref
            acc_ref[: first + width, at] = before_ref[: first + width, at] + reached

    def gate(i, at):
        mr = (q_ref[:half, at].astype(F32) * acc_ref[:, at]).astype(BF16)
        mr_ref[:, at] = mr
        u = mr * kli_ref[:half, at]
        u_ref[:, at] = u
        early_ref[:, at] = pole_sums(ends_ref[at, :], u, fold_ref, poles)

    pipelined(channels // WIDE, convolve, gate, lag=4)


def rim_kernel(place, late_ref, decay_ref, _after, *refs):
    total_ref, mr_ref, u_ref, early_ref, *scratch = refs[6:]

    def work():
        rim_rows(*refs[:6], mr_ref, u_ref, early_ref, *scratch)
        total_ref[...] = (late_ref[...] + early_ref[...] * decay_ref[...]).astype(total_ref.dtype)

    if place is None:
        work()
    else:
        pl.when(lax.axis_index("ctx") == place)(work)


def joined_kernel(own_ref, before_ref, decay_ref, total_ref):
    decay = decay_ref[...]
    total_ref[...] = (own_ref[...] + before_ref[...].astype(F32) * (decay * decay)).astype(BF16)


def near_kernel(places, *refs):
    sets = [refs[3 * n : 3 * n + 3] for n in range(len(places))]
    (
        rim_ref, part_ref, q_ref, kli_ref, taptab_ref, ends_ref, mr_late_ref, litab_ref,
        early_ref, near_ref, mr_hbm,
        mr_ref, u_ref, mask_ref, fold_ref, acc_ref, sem,
    ) = refs[3 * len(places) :]
    half, channels = u_ref.shape
    copies = (
        pltpu.make_async_copy(mr_late_ref, mr_hbm.at[half:], sem.at[0]),
        pltpu.make_async_copy(mr_ref, mr_hbm.at[:half], sem.at[1]),
    )
    copies[0].start()

    def take(sources):
        for source, target in zip(sources, (mr_ref, u_ref, early_ref)):
            target[...] = source[...]

    if places == (None,):
        take(sets[0])
    else:
        own = (rim_ref, part_ref, q_ref, kli_ref, taptab_ref, ends_ref, mr_ref, u_ref, early_ref, mask_ref, fold_ref, acc_ref)
        at = lax.axis_index("ctx")
        for place, sources in zip(places, sets):
            pl.when(at == place)(functools.partial(take, sources))
        pl.when(at == len(places))(lambda: rim_rows(*own))
    copies[1].start()
    mask_ref[...] = same_group(CHUNK, BF16)
    pipelined(channels // WIDE, near_rows(u_ref, litab_ref, near_ref, mask_ref, CHUNK))
    for copy in copies:
        copy.wait()


def far_kernel(adjacent, *refs):
    (
        q_ref, near_early_ref, near_late_ref, early_ref, powers_ref, decay_ref, scale_ref,
        out_hbm, out_ref, mask_ref, out_sem,
    ) = refs[-11:]
    arrived = refs[:-11]
    half, channels = powers_ref.shape
    steps = channels // WIDE

    def put(i, at):
        return pltpu.make_async_copy(out_ref.at[:, at], out_hbm.at[:, at], out_sem.at[i])

    mask_ref[...] = same_group(early_ref.shape[0], BF16)

    def work(i, at):
        mask = mask_ref[...]
        scale = scale_ref[:, at]
        decay = decay_ref[:, at]
        entering = arrived[-1][:, at].astype(F32)
        for n in range(len(arrived) - 2, -1, -1):
            if n >= adjacent - 1:
                entering = entering * (decay * decay)
            entering = entering + arrived[n][:, at].astype(F32)
        middle = entering * decay + early_ref[:, at]
        powers = powers_ref[:, at]
        for first, state, near_ref in ((0, entering, near_early_ref), (half, middle, near_late_ref)):
            far = dot(powers, spread((state * scale).astype(BF16), mask))
            gate = q_ref[first : first + half, at].astype(F32)
            out_ref[first : first + half, at] = (gate * (near_ref[:, at] + far)).astype(BF16)
        put(i, at).start()

    pipelined(steps, work)
    for i in range(steps):
        put(i, slice(i * WIDE, (i + 1) * WIDE)).wait()


def body(q_mr, k_mr, v_mr, q_li, k_li, mr_taps, li_rate, li_residue):
    rows, channels = q_mr.shape
    groups, tap_count = mr_taps.shape
    poles = li_rate.shape[1]
    width = channels // groups
    half = tap_count
    assert rows == 2 * half and poles == width == CHUNK
    steps = channels // WIDE
    params = pltpu.CompilerParams(vmem_limit_bytes=40 * 1024 * 1024)
    vmem, hbm = pl.BlockSpec(memory_space=pltpu.VMEM), pl.BlockSpec(memory_space=pl.ANY)
    in_hbm = lambda *arrays: [pltpu.with_memory_space_constraint(array, pltpu.HBM) for array in arrays]
    dma = pltpu.SemaphoreType.DMA
    mask, fold = pltpu.VMEM((WIDE, WIDE), BF16), pltpu.VMEM((WIDE, WIDE), F32)
    pole_sum, short, tall = (poles, channels), (half, channels), (rows, channels)

    def call(kernel, name, ins, outs, scratch, flops, *operands):
        return pl.pallas_call(
            kernel,
            in_specs=ins,
            out_specs=[hbm if isinstance(out, jax.ShapeDtypeStruct) else vmem for out in outs],
            out_shape=outs,
            scratch_shapes=scratch,
            cost_estimate=pl.CostEstimate(flops=flops, bytes_accessed=flops // 1000, transcendentals=0),
            compiler_params=params,
            name=name,
        )(*operands)

    tail = k_mr[half:] * v_mr[half:]
    peers = lax.axis_size("ctx")
    send = lambda array, *pairs: lax.ppermute(array, "ctx", pairs)
    by_place = peers == 4
    if by_place:
        rims = [send(tail, (at, at + 1)) for at in range(3)]
    else:
        rims = [shifted(tail, "ctx", 1)]

    mr_late, part, u_late, late, taptab, ends, decay, q, kli, *without_rim, rates, residues = call(
        local_kernel,
        "local_rows",
        [vmem] * 4 + [hbm] * 4,
        [
            pltpu.VMEM(short, BF16),
            pltpu.VMEM(short, F32),
            pltpu.VMEM(short, BF16),
            pltpu.VMEM(pole_sum, F32),
            pltpu.VMEM((half + width, channels), BF16),
            pltpu.VMEM((channels, half), BF16),
            pltpu.VMEM(pole_sum, F32),
            pltpu.VMEM(tall, BF16),
            pltpu.VMEM(tall, BF16),
            pltpu.VMEM(short, BF16),
            pltpu.VMEM(short, BF16),
            pltpu.VMEM(pole_sum, F32),
            pltpu.VMEM(pole_sum, F32),
            pltpu.VMEM(pole_sum, F32),
        ],
        [
            pltpu.VMEM(short, BF16),
            pltpu.VMEM(short, BF16),
            mask,
            fold,
            pltpu.VMEM(tall, F32),
            dma((4,)),
        ],
        4 * 10**9,
        tail, mr_taps, li_rate.T, li_residue.T,
        *in_hbm(q_mr, k_mr, v_mr, k_li),
    )

    first, litab, powers, scale, qli = call(
        filter_kernel,
        "filter_tables",
        [vmem] * 5 + [hbm],
        [
            pltpu.VMEM(pole_sum, BF16),
            pltpu.VMEM(short, BF16),
            pltpu.VMEM(short, BF16),
            pltpu.VMEM(pole_sum, F32),
            pltpu.VMEM(tall, BF16),
        ],
        [mask, dma(())],
        10**6,
        rates, residues, late, without_rim[2], decay, *in_hbm(q_li),
    )
    (near_late,) = call(
        near_late_kernel, "near_late", [vmem] * 2, [pltpu.VMEM(short, F32)], [mask], 10**6, u_late, litab
    )

    before = send(first, (0, 1)) if by_place else None

    own = (part, q, kli, taptab, ends)

    def with_rim(place, rim, after, dtype):
        return call(
            functools.partial(rim_kernel, place),
            "rim_rows",
            [vmem] * 9,
            [
                pltpu.VMEM(pole_sum, dtype),
                pltpu.VMEM(short, BF16),
                pltpu.VMEM(short, BF16),
                pltpu.VMEM(pole_sum, F32),
            ],
            [mask, fold, pltpu.VMEM(short, F32)],
            10**6,
            late, decay, after, rim, *own,
        )

    if by_place:
        total_1, *rim_1 = with_rim(1, rims[0], near_late, F32)
        (total_1,) = call(
            joined_kernel,
            "joined_sums",
            [vmem] * 3,
            [pltpu.VMEM(pole_sum, BF16)],
            [],
            10**6,
            total_1, before, decay,
        )
        two_before = send(total_1, (1, 3))
        one_before = send(total_1, (1, 2))
        total_2, *rim_2 = with_rim(2, rims[1], total_1, BF16)
        entered = before.astype(F32) + one_before.astype(F32) + two_before.astype(F32) * (decay * decay)
        arrived = [entered, send(total_2, (2, 3))]
        early_rows, places = (*without_rim, *rim_1, *rim_2), (0, 1, 2)
    else:
        total, *early_rows = with_rim(None, rims[0], near_late, BF16)
        places = (None,)
        reach = min(3, max(peers - 1, 1))
        arrived = [shifted(total, "ctx", by) for by in range(1, reach + 1)]
        while reach < peers - 1:
            window = arrived[-1].astype(F32)
            for piece in arrived[-2::-1]:
                window = window * jnp.exp(-rates * rows) + piece.astype(F32)
            merged = window
            for times in (1, 2, 3):
                if times * reach < peers:
                    moved = shifted(window, "ctx", times * reach)
                    merged = merged + moved * jnp.exp(-rates * (rows * reach * times))
            arrived = [merged]
            reach *= 4

    early, near_early, mr_out = call(
        functools.partial(near_kernel, places),
        "near_part",
        [vmem] * (len(early_rows) + 8),
        [pltpu.VMEM(pole_sum, F32), pltpu.VMEM(short, F32), jax.ShapeDtypeStruct(tall, BF16)],
        [pltpu.VMEM(short, BF16), pltpu.VMEM(short, BF16), mask, fold, pltpu.VMEM(short, F32), dma((2,))],
        10**6,
        *early_rows, rims[-1], *own, mr_late, litab,
    )

    (li_out,) = call(
        functools.partial(far_kernel, 2 if by_place else 1),
        "far_rows",
        [vmem] * (len(arrived) + 7),
        [jax.ShapeDtypeStruct(tall, BF16)],
        [pltpu.VMEM(tall, BF16), mask, dma((steps,))],
        10**9,
        *arrived, qli, near_early, near_late, early, powers, decay, scale,
    )
    return (mr_out, li_out)


def solution(mesh):
    seq = P(("rep", "ctx"), "tp")
    in_specs = (seq, seq, seq, seq, seq, P("tp", None), P("tp", None), P("tp", None))
    return jax.shard_map(body, mesh=mesh, in_specs=in_specs, out_specs=(seq, seq), check_vma=False)
```

```python
import functools

import jax
import jax.numpy as jnp
from jax import lax
from jax.experimental import pallas as pl
from jax.experimental.pallas import tpu as pltpu
from jax.sharding import PartitionSpec as P

F32 = jnp.float32
BF16 = jnp.bfloat16
WIDE = 256
CHUNK = 16


def shifted(array, axis, by):
    peers = lax.axis_size(axis)
    pairs = [(i, i + by) for i in range(peers) if 0 <= i + by < peers]
    return lax.ppermute(array, axis, pairs)


def iota(shape, dim):
    return lax.broadcasted_iota(jnp.int32, shape, dim)


def dot(a, b):
    return jnp.dot(a, b, preferred_element_type=F32)


def same_group(width, dtype):
    rows, cols = iota((WIDE, WIDE), 0), iota((WIDE, WIDE), 1)
    return jnp.where(rows // width == cols // width, 1.0, 0.0).astype(F32).astype(dtype)


def spread(compact, mask):
    copies = WIDE // compact.shape[0]
    return jnp.concatenate([compact] * copies, axis=0) * mask


def split(array):
    upper = array.astype(BF16)
    return upper, (array - upper.astype(F32)).astype(BF16)


def one_minus_exp(x):
    series = 1.0 - x / 7.0
    for n in (6.0, 5.0, 4.0, 3.0, 2.0):
        series = 1.0 - x / n * series
    return jnp.where(x < 0.25, x * series, 1.0 - jnp.exp(-x))


def expand_groups(per_group, first_group, width, precision=None):
    groups = per_group.shape[1]
    pick = iota((groups, WIDE), 1) // width + first_group == iota((groups, WIDE), 0)
    return jnp.dot(per_group, pick.astype(F32).astype(per_group.dtype), precision=precision, preferred_element_type=F32)


def pipelined(steps, *stages, lag=1):
    for turn in range(steps + lag * (len(stages) - 1)):
        for n, stage in enumerate(stages):
            i = turn - lag * n
            if 0 <= i < steps:
                stage(i, slice(i * WIDE, (i + 1) * WIDE))


def rates_along(rates, width):
    on_diagonal = iota(rates.shape, 0) == iota(rates.shape, 1) % width
    return jnp.sum(jnp.where(on_diagonal, rates, 0.0), axis=0, keepdims=True)


def pole_sums(ends, u, fold_ref, poles):
    every = dot(ends, u)
    parts = []
    lanes = 128
    for at in range(0, WIDE, lanes):
        own = every[at : at + lanes, at : at + lanes] * fold_ref[at : at + lanes, at : at + lanes]
        parts.append(functools.reduce(jnp.add, [own[p : p + poles] for p in range(0, lanes, poles)]))
    return jnp.concatenate(parts, axis=1)


def last_products(k_hbm, v_hbm, tail_ref, k_ref, v_ref, sem):
    half, channels = tail_ref.shape
    last = pl.ds(k_hbm.shape[0] - half, half)
    pieces = (slice(0, channels // 2), slice(channels // 2, channels))
    copies = [
        (
            pltpu.make_async_copy(k_hbm.at[last, at], k_ref.at[:, at], sem.at[0, n]),
            pltpu.make_async_copy(v_hbm.at[last, at], v_ref.at[:, at], sem.at[1, n]),
        )
        for n, at in enumerate(pieces)
    ]
    for pair in copies:
        for copy in pair:
            copy.start()
    for pair, at in zip(copies, pieces):
        for copy in pair:
            copy.wait()
        tail_ref[:, at] = k_ref[:, at] * v_ref[:, at]


def tail_kernel(place, _after, *refs):
    pl.when(lax.axis_index("ctx") == place)(lambda: last_products(*refs))


def local_kernel(count, *refs):
    tails, refs = refs[:count], refs[count:]
    if count > 1:
        *refs, tail_ref, tail_sem = refs
        k_hbm, v_hbm = refs[4:6]
        k_ref, v_ref = refs[-6:-4]
        at = lax.axis_index("ctx")
        for place, ref in enumerate(tails):

            @pl.when(at == place)
            def _():
                tail_ref[...] = ref[...]

        pl.when(at == count)(lambda: last_products(k_hbm, v_hbm, tail_ref, k_ref, v_ref, tail_sem))
    else:
        (tail_ref,) = tails
    local_rows(tail_ref, *refs)


def local_rows(
    tail_ref, taps_ref, rate_ref, residue_ref, q_hbm, k_hbm, v_hbm, kli_hbm,
    mr_ref, part_ref, ulate_ref, late_ref, taptab_ref, ends_ref, decay_ref, q_ref, kli_ref,
    mr_early_ref, u_early_ref, early_ref, rates_ref, residues_ref,
    k_ref, v_ref, mask_ref, fold_ref, acc_ref, in_sem,
):
    rows, channels = k_hbm.shape
    groups, tap_count = taps_ref.shape
    steps = channels // WIDE
    width = channels // groups
    wide_groups = WIDE // width
    poles = rate_ref.shape[0]
    half = tap_count

    pairs = (
        (k_hbm.at[:half], k_ref), (v_hbm.at[:half], v_ref), (q_hbm, q_ref), (kli_hbm, kli_ref),
    )
    copies = [pltpu.make_async_copy(a, b, in_sem.at[n]) for n, (a, b) in enumerate(pairs)]
    for copy in copies:
        copy.start()

    mask_ref[...] = same_group(width, BF16)
    fold_ref[...] = same_group(width, F32)

    def tables(i, at):
        lane_item = iota((tap_count + width, WIDE), 1) % width
        own = slice(i * wide_groups, (i + 1) * wide_groups)
        pick = (iota((wide_groups, WIDE), 1) // width == iota((wide_groups, WIDE), 0)).astype(F32).astype(BF16)
        table = lax.dot_general(taps_ref[own, :], pick, (((0,), (0,)), ((), ())), preferred_element_type=F32)
        table = jnp.concatenate([table, jnp.zeros((width, WIDE), F32)], axis=0)
        step = 1
        while step < width:
            table = jnp.where((lane_item & step) != 0, pltpu.roll(table, step, 0), table)
            step *= 2
        taptab_ref[:, at] = table.astype(BF16)
        rates = expand_groups(rate_ref[...], i * wide_groups, width, lax.Precision.HIGHEST)
        rates_ref[:, at] = rates
        residues_ref[:, at] = expand_groups(residue_ref[...], i * wide_groups, width, lax.Precision.HIGHEST)
        decay_ref[:, at] = jnp.exp(-rates * half)
        left = half - 1.0 - iota((half, WIDE), 0).astype(F32)
        ends_ref[at, :] = jnp.transpose(jnp.exp(-rates_along(rates, width) * left)).astype(BF16)

    def convolve_late(i, at):
        mask = mask_ref[...]
        for first in range(half, rows, width):
            u = tail_ref[first - half : first - half + width, at]
            reached = dot(taptab_ref[: rows - first, at], spread(u, mask))
            acc_ref[first:, at] = acc_ref[first:, at] + reached if first > half else reached

    def convolve_early(i, at):
        mask = mask_ref[...]
        u = k_ref[:, at] * v_ref[:, at]
        acc_ref[:half, at] = jnp.zeros((half, WIDE), F32)
        for first in range(0, half, width):
            count = tap_count + width
            acc_ref[first : first + count, at] += dot(taptab_ref[:, at], spread(u[first : first + width], mask))

    def gate(i, at):
        early, late = acc_ref[:half, at], acc_ref[half:, at]
        part_ref[:, at] = early
        mr = (q_ref[half:, at].astype(F32) * late).astype(BF16)
        mr_ref[:, at] = mr
        u_late = mr * kli_ref[half:, at]
        ulate_ref[:, at] = u_late
        mr_early = (q_ref[:half, at].astype(F32) * early).astype(BF16)
        mr_early_ref[:, at] = mr_early
        u_early = mr_early * kli_ref[:half, at]
        u_early_ref[:, at] = u_early
        ends = ends_ref[at, :]
        late_ref[:, at] = pole_sums(ends, u_late, fold_ref, poles)
        early_ref[:, at] = pole_sums(ends, u_early, fold_ref, poles)

    pipelined(steps, tables)
    pipelined(steps, convolve_late)
    for copy in copies:
        copy.wait()
    pipelined(steps, convolve_early, gate, lag=3)


def near_rows(u_ref, litab_ref, near_ref, mask_ref, width):
    half = u_ref.shape[0]

    def work(i, at):
        mask = mask_ref[...]
        u = u_ref[:, at]
        for first in range(0, half, width):
            reached = dot(litab_ref[: half - first, at], spread(u[first : first + width], mask))
            near_ref[first:half, at] = near_ref[first:half, at] + reached if first else reached

    return work


def filter_kernel(
    rates_ref, residues_ref, late_ref, early_ref, decay_ref, qli_hbm,
    first_ref, litab_ref, powers_ref, scale_ref, qli_ref,
    mask_ref, sem,
):
    half, channels = litab_ref.shape
    poles = rates_ref.shape[0]
    width = CHUNK
    steps = channels // WIDE
    copy = pltpu.make_async_copy(qli_hbm, qli_ref, sem)
    copy.start()
    first_ref[...] = (late_ref[...] + early_ref[...] * decay_ref[...]).astype(BF16)
    mask_ref[...] = same_group(width, BF16)

    def tables(i, at):
        mask = mask_ref[...]
        rates = rates_ref[:, at]
        scale = residues_ref[:, at] * jnp.sqrt(one_minus_exp(2.0 * rates))
        scale_ref[:, at] = scale
        item = (iota((poles, WIDE), 1) % width).astype(F32)
        times = iota((half, WIDE), 0).astype(F32)
        rate_row = rates_along(rates, width)
        power = jnp.exp(-rate_row * times)
        powers_ref[:, at] = (power * jnp.exp(-rate_row)).astype(BF16)
        power_hi, power_lo = split(power)
        lift_hi, lift_lo = split(scale * jnp.exp(rates * item))
        lift_hi, lift_lo = spread(lift_hi, mask), spread(lift_lo, mask)
        li_taps = dot(power_hi, lift_hi) + dot(power_hi, lift_lo) + dot(power_lo, lift_hi)
        causal = iota((half, WIDE), 0) >= iota((half, WIDE), 1) % width
        litab_ref[:, at] = jnp.where(causal, li_taps, 0.0).astype(BF16)

    pipelined(steps, tables)
    copy.wait()


def near_late_kernel(u_ref, litab_ref, near_ref, mask_ref):
    mask_ref[...] = same_group(CHUNK, BF16)
    pipelined(u_ref.shape[1] // WIDE, near_rows(u_ref, litab_ref, near_ref, mask_ref, CHUNK))


def rim_rows(
    rim_ref, part_ref, q_ref, kli_ref, taptab_ref, ends_ref, mr_ref, u_ref, early_ref, mask_ref, fold_ref, acc_ref
):
    half, channels = rim_ref.shape
    width = taptab_ref.shape[0] - half
    poles = early_ref.shape[0]
    mask_ref[...] = same_group(width, BF16)
    fold_ref[...] = same_group(width, F32)

    def convolve(i, at):
        mask = mask_ref[...]
        rim = rim_ref[:, at]
        for first in range(half - width, -1, -width):
            reached = dot(taptab_ref[half - first :, at], spread(rim[first : first + width], mask))
            before_ref = part_ref if first == half - width else acc_ref
            acc_ref[: first + width, at] = before_ref[: first + width, at] + reached

    def gate(i, at):
        mr = (q_ref[:half, at].astype(F32) * acc_ref[:, at]).astype(BF16)
        mr_ref[:, at] = mr
        u = mr * kli_ref[:half, at]
        u_ref[:, at] = u
        early_ref[:, at] = pole_sums(ends_ref[at, :], u, fold_ref, poles)

    pipelined(channels // WIDE, convolve, gate, lag=4)


def rim_kernel(place, late_ref, decay_ref, _after, *refs):
    total_ref, mr_ref, u_ref, early_ref, *scratch = refs[6:]

    def work():
        rim_rows(*refs[:6], mr_ref, u_ref, early_ref, *scratch)
        total_ref[...] = (late_ref[...] + early_ref[...] * decay_ref[...]).astype(total_ref.dtype)

    if place is None:
        work()
    else:
        pl.when(lax.axis_index("ctx") == place)(work)


def joined_kernel(own_ref, before_ref, decay_ref, total_ref):
    decay = decay_ref[...]
    total_ref[...] = (own_ref[...] + before_ref[...].astype(F32) * (decay * decay)).astype(BF16)


def near_kernel(places, *refs):
    sets = [refs[3 * n : 3 * n + 3] for n in range(len(places))]
    (
        rim_ref, part_ref, q_ref, kli_ref, taptab_ref, ends_ref, mr_late_ref, litab_ref,
        early_ref, near_ref, mr_hbm,
        mr_ref, u_ref, mask_ref, fold_ref, acc_ref, sem,
    ) = refs[3 * len(places) :]
    half, channels = u_ref.shape
    copies = (
        pltpu.make_async_copy(mr_late_ref, mr_hbm.at[half:], sem.at[0]),
        pltpu.make_async_copy(mr_ref, mr_hbm.at[:half], sem.at[1]),
    )
    copies[0].start()

    def take(sources):
        for source, target in zip(sources, (mr_ref, u_ref, early_ref)):
            target[...] = source[...]

    if places == (None,):
        take(sets[0])
    else:
        own = (rim_ref, part_ref, q_ref, kli_ref, taptab_ref, ends_ref, mr_ref, u_ref, early_ref, mask_ref, fold_ref, acc_ref)
        at = lax.axis_index("ctx")
        for place, sources in zip(places, sets):
            pl.when(at == place)(functools.partial(take, sources))
        pl.when(at == len(places))(lambda: rim_rows(*own))
    copies[1].start()
    mask_ref[...] = same_group(CHUNK, BF16)
    pipelined(channels // WIDE, near_rows(u_ref, litab_ref, near_ref, mask_ref, CHUNK))
    for copy in copies:
        copy.wait()


def far_kernel(adjacent, *refs):
    (
        q_ref, near_early_ref, near_late_ref, early_ref, powers_ref, decay_ref, scale_ref,
        out_hbm, out_ref, mask_ref, out_sem,
    ) = refs[-11:]
    arrived = refs[:-11]
    half, channels = powers_ref.shape
    steps = channels // WIDE

    def put(i, at):
        return pltpu.make_async_copy(out_ref.at[:, at], out_hbm.at[:, at], out_sem.at[i])

    mask_ref[...] = same_group(early_ref.shape[0], BF16)

    def work(i, at):
        mask = mask_ref[...]
        scale = scale_ref[:, at]
        decay = decay_ref[:, at]
        entering = arrived[-1][:, at].astype(F32)
        for n in range(len(arrived) - 2, -1, -1):
            if n >= adjacent - 1:
                entering = entering * (decay * decay)
            entering = entering + arrived[n][:, at].astype(F32)
        middle = entering * decay + early_ref[:, at]
        powers = powers_ref[:, at]
        for first, state, near_ref in ((0, entering, near_early_ref), (half, middle, near_late_ref)):
            far = dot(powers, spread((state * scale).astype(BF16), mask))
            gate = q_ref[first : first + half, at].astype(F32)
            out_ref[first : first + half, at] = (gate * (near_ref[:, at] + far)).astype(BF16)
        put(i, at).start()

    pipelined(steps, work)
    for i in range(steps):
        put(i, slice(i * WIDE, (i + 1) * WIDE)).wait()


def body(q_mr, k_mr, v_mr, q_li, k_li, mr_taps, li_rate, li_residue):
    rows, channels = q_mr.shape
    groups, tap_count = mr_taps.shape
    poles = li_rate.shape[1]
    width = channels // groups
    half = tap_count
    assert rows == 2 * half and poles == width == CHUNK
    steps = channels // WIDE
    params = pltpu.CompilerParams(vmem_limit_bytes=40 * 1024 * 1024)
    vmem, hbm = pl.BlockSpec(memory_space=pltpu.VMEM), pl.BlockSpec(memory_space=pl.ANY)
    in_hbm = lambda *arrays: [pltpu.with_memory_space_constraint(array, pltpu.HBM) for array in arrays]
    dma = pltpu.SemaphoreType.DMA
    mask, fold = pltpu.VMEM((WIDE, WIDE), BF16), pltpu.VMEM((WIDE, WIDE), F32)
    pole_sum, short, tall = (poles, channels), (half, channels), (rows, channels)

    def call(kernel, name, ins, outs, scratch, flops, *operands):
        return pl.pallas_call(
            kernel,
            in_specs=ins,
            out_specs=[hbm if isinstance(out, jax.ShapeDtypeStruct) else vmem for out in outs],
            out_shape=outs,
            scratch_shapes=scratch,
            cost_estimate=pl.CostEstimate(flops=flops, bytes_accessed=flops // 1000, transcendentals=0),
            compiler_params=params,
            name=name,
        )(*operands)

    peers = lax.axis_size("ctx")
    send = lambda array, *pairs: lax.ppermute(array, "ctx", pairs)
    by_place = peers == 4
    if by_place:
        tails = []
        for place in range(3):
            tails += call(
                functools.partial(tail_kernel, place),
                "tail_rows",
                [vmem if tails else hbm] + [hbm] * 2,
                [pltpu.VMEM(short, BF16)],
                [pltpu.VMEM(short, BF16), pltpu.VMEM(short, BF16), dma((2, 2))],
                10**6,
                tails[-1] if tails else in_hbm(k_mr)[0], *in_hbm(k_mr, v_mr),
            )
        rims = [send(tail, (at, at + 1)) for at, tail in enumerate(tails)]
    else:
        tail = k_mr[half:] * v_mr[half:]
        tails = [tail]
        rims = [shifted(tail, "ctx", 1)]

    mr_late, part, u_late, late, taptab, ends, decay, q, kli, *without_rim, rates, residues = call(
        functools.partial(local_kernel, len(tails)),
        "local_rows",
        [vmem] * (len(tails) + 3) + [hbm] * 4,
        [
            pltpu.VMEM(short, BF16),
            pltpu.VMEM(short, F32),
            pltpu.VMEM(short, BF16),
            pltpu.VMEM(pole_sum, F32),
            pltpu.VMEM((half + width, channels), BF16),
            pltpu.VMEM((channels, half), BF16),
            pltpu.VMEM(pole_sum, F32),
            pltpu.VMEM(tall, BF16),
            pltpu.VMEM(tall, BF16),
            pltpu.VMEM(short, BF16),
            pltpu.VMEM(short, BF16),
            pltpu.VMEM(pole_sum, F32),
            pltpu.VMEM(pole_sum, F32),
            pltpu.VMEM(pole_sum, F32),
        ],
        [
            pltpu.VMEM(short, BF16),
            pltpu.VMEM(short, BF16),
            mask,
            fold,
            pltpu.VMEM(tall, F32),
            dma((4,)),
            *[pltpu.VMEM(short, BF16), dma((2, 2))] * (len(tails) > 1),
        ],
        4 * 10**9,
        *tails, mr_taps, li_rate.T, li_residue.T,
        *in_hbm(q_mr, k_mr, v_mr, k_li),
    )

    first, litab, powers, scale, qli = call(
        filter_kernel,
        "filter_tables",
        [vmem] * 5 + [hbm],
        [
            pltpu.VMEM(pole_sum, BF16),
            pltpu.VMEM(short, BF16),
            pltpu.VMEM(short, BF16),
            pltpu.VMEM(pole_sum, F32),
            pltpu.VMEM(tall, BF16),
        ],
        [mask, dma(())],
        10**6,
        rates, residues, late, without_rim[2], decay, *in_hbm(q_li),
    )
    (near_late,) = call(
        near_late_kernel, "near_late", [vmem] * 2, [pltpu.VMEM(short, F32)], [mask], 10**6, u_late, litab
    )

    before = send(first, (0, 1)) if by_place else None

    own = (part, q, kli, taptab, ends)

    def with_rim(place, rim, after, dtype):
        return call(
            functools.partial(rim_kernel, place),
            "rim_rows",
            [vmem] * 9,
            [
                pltpu.VMEM(pole_sum, dtype),
                pltpu.VMEM(short, BF16),
                pltpu.VMEM(short, BF16),
                pltpu.VMEM(pole_sum, F32),
            ],
            [mask, fold, pltpu.VMEM(short, F32)],
            10**6,
            late, decay, after, rim, *own,
        )

    if by_place:
        total_1, *rim_1 = with_rim(1, rims[0], near_late, F32)
        (total_1,) = call(
            joined_kernel,
            "joined_sums",
            [vmem] * 3,
            [pltpu.VMEM(pole_sum, BF16)],
            [],
            10**6,
            total_1, before, decay,
        )
        two_before = send(total_1, (1, 3))
        one_before = send(total_1, (1, 2))
        total_2, *rim_2 = with_rim(2, rims[1], total_1, BF16)
        entered = before.astype(F32) + one_before.astype(F32) + two_before.astype(F32) * (decay * decay)
        arrived = [entered, send(total_2, (2, 3))]
        early_rows, places = (*without_rim, *rim_1, *rim_2), (0, 1, 2)
    else:
        total, *early_rows = with_rim(None, rims[0], near_late, BF16)
        places = (None,)
        reach = min(3, max(peers - 1, 1))
        arrived = [shifted(total, "ctx", by) for by in range(1, reach + 1)]
        while reach < peers - 1:
            window = arrived[-1].astype(F32)
            for piece in arrived[-2::-1]:
                window = window * jnp.exp(-rates * rows) + piece.astype(F32)
            merged = window
            for times in (1, 2, 3):
                if times * reach < peers:
                    moved = shifted(window, "ctx", times * reach)
                    merged = merged + moved * jnp.exp(-rates * (rows * reach * times))
            arrived = [merged]
            reach *= 4

    early, near_early, mr_out = call(
        functools.partial(near_kernel, places),
        "near_part",
        [vmem] * (len(early_rows) + 8),
        [pltpu.VMEM(pole_sum, F32), pltpu.VMEM(short, F32), jax.ShapeDtypeStruct(tall, BF16)],
        [pltpu.VMEM(short, BF16), pltpu.VMEM(short, BF16), mask, fold, pltpu.VMEM(short, F32), dma((2,))],
        10**6,
        *early_rows, rims[-1], *own, mr_late, litab,
    )

    (li_out,) = call(
        functools.partial(far_kernel, 2 if by_place else 1),
        "far_rows",
        [vmem] * (len(arrived) + 7),
        [jax.ShapeDtypeStruct(tall, BF16)],
        [pltpu.VMEM(tall, BF16), mask, dma((steps,))],
        10**9,
        *arrived, qli, near_early, near_late, early, powers, decay, scale,
    )
    return (mr_out, li_out)


def solution(mesh):
    seq = P(("rep", "ctx"), "tp")
    in_specs = (seq, seq, seq, seq, seq, P("tp", None), P("tp", None), P("tp", None))
    return jax.shard_map(body, mesh=mesh, in_specs=in_specs, out_specs=(seq, seq), check_vma=False)
```

```python
import functools

import jax
import jax.numpy as jnp
from jax import lax
from jax.experimental import pallas as pl
from jax.experimental.pallas import tpu as pltpu
from jax.sharding import PartitionSpec as P

F32 = jnp.float32
BF16 = jnp.bfloat16
WIDE = 256
CHUNK = 16


def shifted(array, axis, by):
    peers = lax.axis_size(axis)
    pairs = [(i, i + by) for i in range(peers) if 0 <= i + by < peers]
    return lax.ppermute(array, axis, pairs)


def iota(shape, dim):
    return lax.broadcasted_iota(jnp.int32, shape, dim)


def dot(a, b):
    return jnp.dot(a, b, preferred_element_type=F32)


def same_group(width, dtype):
    rows, cols = iota((WIDE, WIDE), 0), iota((WIDE, WIDE), 1)
    return jnp.where(rows // width == cols // width, 1.0, 0.0).astype(F32).astype(dtype)


def spread(compact, mask):
    copies = WIDE // compact.shape[0]
    return jnp.concatenate([compact] * copies, axis=0) * mask


def split(array):
    upper = array.astype(BF16)
    return upper, (array - upper.astype(F32)).astype(BF16)


def one_minus_exp(x):
    series = 1.0 - x / 7.0
    for n in (6.0, 5.0, 4.0, 3.0, 2.0):
        series = 1.0 - x / n * series
    return jnp.where(x < 0.25, x * series, 1.0 - jnp.exp(-x))


def expand_groups(per_group, first_group, width, precision=None):
    groups = per_group.shape[1]
    pick = iota((groups, WIDE), 1) // width + first_group == iota((groups, WIDE), 0)
    return jnp.dot(per_group, pick.astype(F32).astype(per_group.dtype), precision=precision, preferred_element_type=F32)


def pipelined(steps, *stages, lag=1):
    for turn in range(steps + lag * (len(stages) - 1)):
        for n, stage in enumerate(stages):
            i = turn - lag * n
            if 0 <= i < steps:
                stage(i, slice(i * WIDE, (i + 1) * WIDE))


def rates_along(rates, width):
    on_diagonal = iota(rates.shape, 0) == iota(rates.shape, 1) % width
    return jnp.sum(jnp.where(on_diagonal, rates, 0.0), axis=0, keepdims=True)


def pole_sums(ends, u, fold_ref, poles):
    every = dot(ends, u)
    parts = []
    lanes = 128
    for at in range(0, WIDE, lanes):
        own = every[at : at + lanes, at : at + lanes] * fold_ref[at : at + lanes, at : at + lanes]
        parts.append(functools.reduce(jnp.add, [own[p : p + poles] for p in range(0, lanes, poles)]))
    return jnp.concatenate(parts, axis=1)


def last_products(k_hbm, v_hbm, tail_ref, k_ref, v_ref, sem):
    half, channels = tail_ref.shape
    last = pl.ds(k_hbm.shape[0] - half, half)
    pieces = (slice(0, channels // 2), slice(channels // 2, channels))
    copies = [
        (
            pltpu.make_async_copy(k_hbm.at[last, at], k_ref.at[:, at], sem.at[0, n]),
            pltpu.make_async_copy(v_hbm.at[last, at], v_ref.at[:, at], sem.at[1, n]),
        )
        for n, at in enumerate(pieces)
    ]
    for pair in copies:
        for copy in pair:
            copy.start()
    for pair, at in zip(copies, pieces):
        for copy in pair:
            copy.wait()
        tail_ref[:, at] = k_ref[:, at] * v_ref[:, at]


def tail_kernel(place, _after, *refs):
    pl.when(lax.axis_index("ctx") == place)(lambda: last_products(*refs))


def local_kernel(count, *refs):
    tails, refs = refs[:count], refs[count:]
    if count > 1:
        *refs, tail_ref, tail_sem = refs
        k_hbm, v_hbm = refs[4:6]
        k_ref, v_ref = refs[-6:-4]
        at = lax.axis_index("ctx")
        for place, ref in enumerate(tails):

            @pl.when(at == place)
            def _():
                tail_ref[...] = ref[...]

        pl.when(at == count)(lambda: last_products(k_hbm, v_hbm, tail_ref, k_ref, v_ref, tail_sem))
    else:
        (tail_ref,) = tails
    local_rows(tail_ref, *refs)


def local_rows(
    tail_ref, taps_ref, rate_ref, residue_ref, q_hbm, k_hbm, v_hbm, kli_hbm,
    mr_ref, part_ref, ulate_ref, late_ref, taptab_ref, ends_ref, decay_ref, q_ref, kli_ref,
    mr_early_ref, u_early_ref, early_ref, rates_ref, residues_ref,
    k_ref, v_ref, mask_ref, fold_ref, acc_ref, in_sem,
):
    rows, channels = k_hbm.shape
    groups, tap_count = taps_ref.shape
    steps = channels // WIDE
    width = channels // groups
    wide_groups = WIDE // width
    poles = rate_ref.shape[0]
    half = tap_count

    pairs = (
        (k_hbm.at[:half], k_ref), (v_hbm.at[:half], v_ref), (q_hbm, q_ref), (kli_hbm, kli_ref),
    )
    copies = [pltpu.make_async_copy(a, b, in_sem.at[n]) for n, (a, b) in enumerate(pairs)]
    for copy in copies:
        copy.start()

    mask_ref[...] = same_group(width, BF16)
    fold_ref[...] = same_group(width, F32)

    def tables(i, at):
        lane_item = iota((tap_count + width, WIDE), 1) % width
        own = slice(i * wide_groups, (i + 1) * wide_groups)
        pick = (iota((wide_groups, WIDE), 1) // width == iota((wide_groups, WIDE), 0)).astype(F32).astype(BF16)
        table = lax.dot_general(taps_ref[own, :], pick, (((0,), (0,)), ((), ())), preferred_element_type=F32)
        table = jnp.concatenate([table, jnp.zeros((width, WIDE), F32)], axis=0)
        step = 1
        while step < width:
            table = jnp.where((lane_item & step) != 0, pltpu.roll(table, step, 0), table)
            step *= 2
        taptab_ref[:, at] = table.astype(BF16)
        rates = expand_groups(rate_ref[...], i * wide_groups, width, lax.Precision.HIGHEST)
        rates_ref[:, at] = rates
        residues_ref[:, at] = expand_groups(residue_ref[...], i * wide_groups, width, lax.Precision.HIGHEST)
        decay_ref[:, at] = jnp.exp(-rates * half)
        left = half - 1.0 - iota((half, WIDE), 0).astype(F32)
        ends_ref[at, :] = jnp.transpose(jnp.exp(-rates_along(rates, width) * left)).astype(BF16)

    def convolve_late(i, at):
        mask = mask_ref[...]
        for first in range(half, rows, width):
            u = tail_ref[first - half : first - half + width, at]
            reached = dot(taptab_ref[: rows - first, at], spread(u, mask))
            acc_ref[first:, at] = acc_ref[first:, at] + reached if first > half else reached

    def convolve_early(i, at):
        mask = mask_ref[...]
        u = k_ref[:, at] * v_ref[:, at]
        acc_ref[:half, at] = jnp.zeros((half, WIDE), F32)
        for first in range(0, half, width):
            count = tap_count + width
            acc_ref[first : first + count, at] += dot(taptab_ref[:, at], spread(u[first : first + width], mask))

    def gate(i, at):
        early, late = acc_ref[:half, at], acc_ref[half:, at]
        part_ref[:, at] = early
        mr = (q_ref[half:, at].astype(F32) * late).astype(BF16)
        mr_ref[:, at] = mr
        u_late = mr * kli_ref[half:, at]
        ulate_ref[:, at] = u_late
        mr_early = (q_ref[:half, at].astype(F32) * early).astype(BF16)
        mr_early_ref[:, at] = mr_early
        u_early = mr_early * kli_ref[:half, at]
        u_early_ref[:, at] = u_early
        ends = ends_ref[at, :]
        late_ref[:, at] = pole_sums(ends, u_late, fold_ref, poles)
        early_ref[:, at] = pole_sums(ends, u_early, fold_ref, poles)

    pipelined(steps, tables)
    pipelined(steps, convolve_late)
    for copy in copies:
        copy.wait()
    pipelined(steps, convolve_early, gate, lag=3)


def near_rows(u_ref, litab_ref, near_ref, mask_ref, width):
    half = u_ref.shape[0]

    def work(i, at):
        mask = mask_ref[...]
        u = u_ref[:, at]
        for first in range(0, half, width):
            reached = dot(litab_ref[: half - first, at], spread(u[first : first + width], mask))
            near_ref[first:half, at] = near_ref[first:half, at] + reached if first else reached

    return work


def filter_kernel(
    rates_ref, residues_ref, late_ref, early_ref, decay_ref, qli_hbm,
    first_ref, litab_ref, powers_ref, scale_ref, qli_ref,
    mask_ref, sem,
):
    half, channels = litab_ref.shape
    poles = rates_ref.shape[0]
    width = CHUNK
    steps = channels // WIDE
    copy = pltpu.make_async_copy(qli_hbm, qli_ref, sem)
    copy.start()
    first_ref[...] = (late_ref[...] + early_ref[...] * decay_ref[...]).astype(BF16)
    mask_ref[...] = same_group(width, BF16)

    def tables(i, at):
        mask = mask_ref[...]
        rates = rates_ref[:, at]
        scale = residues_ref[:, at] * jnp.sqrt(one_minus_exp(2.0 * rates))
        scale_ref[:, at] = scale
        item = (iota((poles, WIDE), 1) % width).astype(F32)
        times = iota((half, WIDE), 0).astype(F32)
        rate_row = rates_along(rates, width)
        power = jnp.exp(-rate_row * times)
        powers_ref[:, at] = (power * jnp.exp(-rate_row)).astype(BF16)
        power_hi, power_lo = split(power)
        lift_hi, lift_lo = split(scale * jnp.exp(rates * item))
        lift_hi, lift_lo = spread(lift_hi, mask), spread(lift_lo, mask)
        li_taps = dot(power_hi, lift_hi) + dot(power_hi, lift_lo) + dot(power_lo, lift_hi)
        causal = iota((half, WIDE), 0) >= iota((half, WIDE), 1) % width
        litab_ref[:, at] = jnp.where(causal, li_taps, 0.0).astype(BF16)

    pipelined(steps, tables)
    copy.wait()


def near_late_kernel(u_ref, litab_ref, near_ref, mask_ref):
    mask_ref[...] = same_group(CHUNK, BF16)
    pipelined(u_ref.shape[1] // WIDE, near_rows(u_ref, litab_ref, near_ref, mask_ref, CHUNK))


def rim_rows(
    rim_ref, part_ref, q_ref, kli_ref, taptab_ref, ends_ref, mr_ref, u_ref, early_ref, mask_ref, fold_ref, acc_ref
):
    half, channels = rim_ref.shape
    width = taptab_ref.shape[0] - half
    poles = early_ref.shape[0]
    mask_ref[...] = same_group(width, BF16)
    fold_ref[...] = same_group(width, F32)

    def convolve(i, at):
        mask = mask_ref[...]
        rim = rim_ref[:, at]
        tables, chunks = [], []
        for first in range(0, half, width):
            table = taptab_ref[half - first :, at]
            tables.append(jnp.concatenate([table, jnp.zeros((half - table.shape[0], WIDE), BF16)], axis=0) if table.shape[0] < half else table)
            chunks.append(spread(rim[first : first + width], mask))
        acc_ref[:, at] = part_ref[:, at] + dot(jnp.concatenate(tables, axis=1), jnp.concatenate(chunks, axis=0))

    def gate(i, at):
        mr = (q_ref[:half, at].astype(F32) * acc_ref[:, at]).astype(BF16)
        mr_ref[:, at] = mr
        u = mr * kli_ref[:half, at]
        u_ref[:, at] = u
        early_ref[:, at] = pole_sums(ends_ref[at, :], u, fold_ref, poles)

    pipelined(channels // WIDE, convolve, gate, lag=6)


def rim_kernel(place, late_ref, decay_ref, _after, *refs):
    total_ref, mr_ref, u_ref, early_ref, *scratch = refs[6:]

    def work():
        rim_rows(*refs[:6], mr_ref, u_ref, early_ref, *scratch)
        total_ref[...] = (late_ref[...] + early_ref[...] * decay_ref[...]).astype(total_ref.dtype)

    if place is None:
        work()
    else:
        pl.when(lax.axis_index("ctx") == place)(work)


def joined_kernel(own_ref, before_ref, decay_ref, total_ref):
    decay = decay_ref[...]
    total_ref[...] = (own_ref[...] + before_ref[...].astype(F32) * (decay * decay)).astype(BF16)


def near_kernel(places, *refs):
    sets = [refs[3 * n : 3 * n + 3] for n in range(len(places))]
    (
        rim_ref, part_ref, q_ref, kli_ref, taptab_ref, ends_ref, mr_late_ref, litab_ref,
        early_ref, near_ref, mr_hbm,
        mr_ref, u_ref, mask_ref, fold_ref, acc_ref, sem,
    ) = refs[3 * len(places) :]
    half, channels = u_ref.shape
    copies = (
        pltpu.make_async_copy(mr_late_ref, mr_hbm.at[half:], sem.at[0]),
        pltpu.make_async_copy(mr_ref, mr_hbm.at[:half], sem.at[1]),
    )
    copies[0].start()

    def take(sources):
        for source, target in zip(sources, (mr_ref, u_ref, early_ref)):
            target[...] = source[...]

    if places == (None,):
        take(sets[0])
    else:
        own = (rim_ref, part_ref, q_ref, kli_ref, taptab_ref, ends_ref, mr_ref, u_ref, early_ref, mask_ref, fold_ref, acc_ref)
        at = lax.axis_index("ctx")
        for place, sources in zip(places, sets):
            pl.when(at == place)(functools.partial(take, sources))
        pl.when(at == len(places))(lambda: rim_rows(*own))
    copies[1].start()
    mask_ref[...] = same_group(CHUNK, BF16)
    pipelined(channels // WIDE, near_rows(u_ref, litab_ref, near_ref, mask_ref, CHUNK))
    for copy in copies:
        copy.wait()


def far_kernel(adjacent, *refs):
    (
        q_ref, near_early_ref, near_late_ref, early_ref, powers_ref, decay_ref, scale_ref,
        out_hbm, out_ref, mask_ref, out_sem,
    ) = refs[-11:]
    arrived = refs[:-11]
    half, channels = powers_ref.shape
    steps = channels // WIDE

    def put(i, at):
        return pltpu.make_async_copy(out_ref.at[:, at], out_hbm.at[:, at], out_sem.at[i])

    mask_ref[...] = same_group(early_ref.shape[0], BF16)

    def work(i, at):
        mask = mask_ref[...]
        scale = scale_ref[:, at]
        decay = decay_ref[:, at]
        entering = arrived[-1][:, at].astype(F32)
        for n in range(len(arrived) - 2, -1, -1):
            if n >= adjacent - 1:
                entering = entering * (decay * decay)
            entering = entering + arrived[n][:, at].astype(F32)
        middle = entering * decay + early_ref[:, at]
        powers = powers_ref[:, at]
        for first, state, near_ref in ((0, entering, near_early_ref), (half, middle, near_late_ref)):
            far = dot(powers, spread((state * scale).astype(BF16), mask))
            gate = q_ref[first : first + half, at].astype(F32)
            out_ref[first : first + half, at] = (gate * (near_ref[:, at] + far)).astype(BF16)
        put(i, at).start()

    pipelined(steps, work)
    for i in range(steps):
        put(i, slice(i * WIDE, (i + 1) * WIDE)).wait()


def body(q_mr, k_mr, v_mr, q_li, k_li, mr_taps, li_rate, li_residue):
    rows, channels = q_mr.shape
    groups, tap_count = mr_taps.shape
    poles = li_rate.shape[1]
    width = channels // groups
    half = tap_count
    assert rows == 2 * half and poles == width == CHUNK
    steps = channels // WIDE
    params = pltpu.CompilerParams(vmem_limit_bytes=40 * 1024 * 1024)
    vmem, hbm = pl.BlockSpec(memory_space=pltpu.VMEM), pl.BlockSpec(memory_space=pl.ANY)
    in_hbm = lambda *arrays: [pltpu.with_memory_space_constraint(array, pltpu.HBM) for array in arrays]
    dma = pltpu.SemaphoreType.DMA
    mask, fold = pltpu.VMEM((WIDE, WIDE), BF16), pltpu.VMEM((WIDE, WIDE), F32)
    pole_sum, short, tall = (poles, channels), (half, channels), (rows, channels)

    def call(kernel, name, ins, outs, scratch, flops, *operands):
        return pl.pallas_call(
            kernel,
            in_specs=ins,
            out_specs=[hbm if isinstance(out, jax.ShapeDtypeStruct) else vmem for out in outs],
            out_shape=outs,
            scratch_shapes=scratch,
            cost_estimate=pl.CostEstimate(flops=flops, bytes_accessed=flops // 1000, transcendentals=0),
            compiler_params=params,
            name=name,
        )(*operands)

    peers = lax.axis_size("ctx")
    send = lambda array, *pairs: lax.ppermute(array, "ctx", pairs)
    by_place = peers == 4
    if by_place:
        tails = []
        for place in range(3):
            tails += call(
                functools.partial(tail_kernel, place),
                "tail_rows",
                [vmem if tails else hbm] + [hbm] * 2,
                [pltpu.VMEM(short, BF16)],
                [pltpu.VMEM(short, BF16), pltpu.VMEM(short, BF16), dma((2, 2))],
                10**6,
                tails[-1] if tails else in_hbm(k_mr)[0], *in_hbm(k_mr, v_mr),
            )
        rims = [send(tail, (at, at + 1)) for at, tail in enumerate(tails)]
    else:
        tail = k_mr[half:] * v_mr[half:]
        tails = [tail]
        rims = [shifted(tail, "ctx", 1)]

    mr_late, part, u_late, late, taptab, ends, decay, q, kli, *without_rim, rates, residues = call(
        functools.partial(local_kernel, len(tails)),
        "local_rows",
        [vmem] * (len(tails) + 3) + [hbm] * 4,
        [
            pltpu.VMEM(short, BF16),
            pltpu.VMEM(short, F32),
            pltpu.VMEM(short, BF16),
            pltpu.VMEM(pole_sum, F32),
            pltpu.VMEM((half + width, channels), BF16),
            pltpu.VMEM((channels, half), BF16),
            pltpu.VMEM(pole_sum, F32),
            pltpu.VMEM(tall, BF16),
            pltpu.VMEM(tall, BF16),
            pltpu.VMEM(short, BF16),
            pltpu.VMEM(short, BF16),
            pltpu.VMEM(pole_sum, F32),
            pltpu.VMEM(pole_sum, F32),
            pltpu.VMEM(pole_sum, F32),
        ],
        [
            pltpu.VMEM(short, BF16),
            pltpu.VMEM(short, BF16),
            mask,
            fold,
            pltpu.VMEM(tall, F32),
            dma((4,)),
            *[pltpu.VMEM(short, BF16), dma((2, 2))] * (len(tails) > 1),
        ],
        4 * 10**9,
        *tails, mr_taps, li_rate.T, li_residue.T,
        *in_hbm(q_mr, k_mr, v_mr, k_li),
    )

    first, litab, powers, scale, qli = call(
        filter_kernel,
        "filter_tables",
        [vmem] * 5 + [hbm],
        [
            pltpu.VMEM(pole_sum, BF16),
            pltpu.VMEM(short, BF16),
            pltpu.VMEM(short, BF16),
            pltpu.VMEM(pole_sum, F32),
            pltpu.VMEM(tall, BF16),
        ],
        [mask, dma(())],
        10**6,
        rates, residues, late, without_rim[2], decay, *in_hbm(q_li),
    )
    (near_late,) = call(
        near_late_kernel, "near_late", [vmem] * 2, [pltpu.VMEM(short, F32)], [mask], 10**6, u_late, litab
    )

    before = send(first, (0, 1)) if by_place else None

    own = (part, q, kli, taptab, ends)

    def with_rim(place, rim, after, dtype):
        return call(
            functools.partial(rim_kernel, place),
            "rim_rows",
            [vmem] * 9,
            [
                pltpu.VMEM(pole_sum, dtype),
                pltpu.VMEM(short, BF16),
                pltpu.VMEM(short, BF16),
                pltpu.VMEM(pole_sum, F32),
            ],
            [mask, fold, pltpu.VMEM(short, F32)],
            10**6,
            late, decay, after, rim, *own,
        )

    if by_place:
        total_1, *rim_1 = with_rim(1, rims[0], near_late, F32)
        (total_1,) = call(
            joined_kernel,
            "joined_sums",
            [vmem] * 3,
            [pltpu.VMEM(pole_sum, BF16)],
            [],
            10**6,
            total_1, before, decay,
        )
        one_before = send(total_1, (1, 2))
        two_before = send(total_1, (1, 3))
        total_2, *rim_2 = with_rim(2, rims[1], total_1, BF16)
        entered = two_before.astype(F32) * (decay * decay) + one_before.astype(F32) + before.astype(F32)
        arrived = [entered, send(total_2, (2, 3))]
        early_rows, places = (*without_rim, *rim_1, *rim_2), (0, 1, 2)
    else:
        total, *early_rows = with_rim(None, rims[0], near_late, BF16)
        places = (None,)
        reach = min(3, max(peers - 1, 1))
        arrived = [shifted(total, "ctx", by) for by in range(1, reach + 1)]
        while reach < peers - 1:
            window = arrived[-1].astype(F32)
            for piece in arrived[-2::-1]:
                window = window * jnp.exp(-rates * rows) + piece.astype(F32)
            merged = window
            for times in (1, 2, 3):
                if times * reach < peers:
                    moved = shifted(window, "ctx", times * reach)
                    merged = merged + moved * jnp.exp(-rates * (rows * reach * times))
            arrived = [merged]
            reach *= 4

    early, near_early, mr_out = call(
        functools.partial(near_kernel, places),
        "near_part",
        [vmem] * (len(early_rows) + 8),
        [pltpu.VMEM(pole_sum, F32), pltpu.VMEM(short, F32), jax.ShapeDtypeStruct(tall, BF16)],
        [pltpu.VMEM(short, BF16), pltpu.VMEM(short, BF16), mask, fold, pltpu.VMEM(short, F32), dma((2,))],
        10**6,
        *early_rows, rims[-1], *own, mr_late, litab,
    )

    (li_out,) = call(
        functools.partial(far_kernel, 2 if by_place else 1),
        "far_rows",
        [vmem] * (len(arrived) + 7),
        [jax.ShapeDtypeStruct(tall, BF16)],
        [pltpu.VMEM(tall, BF16), mask, dma((steps,))],
        10**9,
        *arrived, qli, near_early, near_late, early, powers, decay, scale,
    )
    return (mr_out, li_out)


def solution(mesh):
    seq = P(("rep", "ctx"), "tp")
    in_specs = (seq, seq, seq, seq, seq, P("tp", None), P("tp", None), P("tp", None))
    return jax.shard_map(body, mesh=mesh, in_specs=in_specs, out_specs=(seq, seq), check_vma=False)
```

```python
import functools

import jax
import jax.numpy as jnp
from jax import lax
from jax.experimental import pallas as pl
from jax.experimental.pallas import tpu as pltpu
from jax.sharding import PartitionSpec as P

F32 = jnp.float32
BF16 = jnp.bfloat16
WIDE = 256
CHUNK = 16


def shifted(array, axis, by):
    peers = lax.axis_size(axis)
    pairs = [(i, i + by) for i in range(peers) if 0 <= i + by < peers]
    return lax.ppermute(array, axis, pairs)


def iota(shape, dim):
    return lax.broadcasted_iota(jnp.int32, shape, dim)


def dot(a, b):
    return jnp.dot(a, b, preferred_element_type=F32)


def same_group(width, dtype):
    rows, cols = iota((WIDE, WIDE), 0), iota((WIDE, WIDE), 1)
    return jnp.where(rows // width == cols // width, 1.0, 0.0).astype(F32).astype(dtype)


def spread(compact, mask):
    copies = WIDE // compact.shape[0]
    return jnp.concatenate([compact] * copies, axis=0) * mask


def split(array):
    upper = array.astype(BF16)
    return upper, (array - upper.astype(F32)).astype(BF16)


def one_minus_exp(x):
    series = 1.0 - x / 7.0
    for n in (6.0, 5.0, 4.0, 3.0, 2.0):
        series = 1.0 - x / n * series
    return jnp.where(x < 0.25, x * series, 1.0 - jnp.exp(-x))


def expand_groups(per_group, first_group, width, precision=None):
    groups = per_group.shape[1]
    pick = iota((groups, WIDE), 1) // width + first_group == iota((groups, WIDE), 0)
    return jnp.dot(per_group, pick.astype(F32).astype(per_group.dtype), precision=precision, preferred_element_type=F32)


def pipelined(steps, *stages, lag=1):
    for turn in range(steps + lag * (len(stages) - 1)):
        for n, stage in enumerate(stages):
            i = turn - lag * n
            if 0 <= i < steps:
                stage(i, slice(i * WIDE, (i + 1) * WIDE))


def rates_along(rates, width):
    on_diagonal = iota(rates.shape, 0) == iota(rates.shape, 1) % width
    return jnp.sum(jnp.where(on_diagonal, rates, 0.0), axis=0, keepdims=True)


def pole_sums(ends, u, fold_ref, poles):
    every = dot(ends, u)
    parts = []
    lanes = 128
    for at in range(0, WIDE, lanes):
        own = every[at : at + lanes, at : at + lanes] * fold_ref[at : at + lanes, at : at + lanes]
        parts.append(functools.reduce(jnp.add, [own[p : p + poles] for p in range(0, lanes, poles)]))
    return jnp.concatenate(parts, axis=1)


def last_products(k_hbm, v_hbm, tail_ref, k_ref, v_ref, sem):
    half, channels = tail_ref.shape
    last = pl.ds(k_hbm.shape[0] - half, half)
    pieces = (slice(0, channels // 2), slice(channels // 2, channels))
    copies = [
        (
            pltpu.make_async_copy(k_hbm.at[last, at], k_ref.at[:, at], sem.at[0, n]),
            pltpu.make_async_copy(v_hbm.at[last, at], v_ref.at[:, at], sem.at[1, n]),
        )
        for n, at in enumerate(pieces)
    ]
    for pair in copies:
        for copy in pair:
            copy.start()
    for pair, at in zip(copies, pieces):
        for copy in pair:
            copy.wait()
        tail_ref[:, at] = k_ref[:, at] * v_ref[:, at]


def tail_kernel(place, _after, *refs):
    pl.when(lax.axis_index("ctx") == place)(lambda: last_products(*refs))


def local_kernel(count, *refs):
    tails, refs = refs[:count], refs[count:]
    if count > 1:
        *refs, tail_ref, tail_sem = refs
        k_hbm, v_hbm = refs[4:6]
        k_ref, v_ref = refs[-6:-4]
        at = lax.axis_index("ctx")
        for place, ref in enumerate(tails):

            @pl.when(at == place)
            def _():
                tail_ref[...] = ref[...]

        pl.when(at == count)(lambda: last_products(k_hbm, v_hbm, tail_ref, k_ref, v_ref, tail_sem))
    else:
        (tail_ref,) = tails
    local_rows(tail_ref, *refs)


def local_rows(
    tail_ref, taps_ref, rate_ref, residue_ref, q_hbm, k_hbm, v_hbm, kli_hbm,
    mr_ref, part_ref, ulate_ref, late_ref, taptab_ref, ends_ref, decay_ref, q_ref, kli_ref,
    mr_early_ref, u_early_ref, early_ref, rates_ref, residues_ref,
    k_ref, v_ref, mask_ref, fold_ref, acc_ref, in_sem,
):
    rows, channels = k_hbm.shape
    groups, tap_count = taps_ref.shape
    steps = channels // WIDE
    width = channels // groups
    wide_groups = WIDE // width
    poles = rate_ref.shape[0]
    half = tap_count

    pairs = (
        (k_hbm.at[:half], k_ref), (v_hbm.at[:half], v_ref), (q_hbm, q_ref), (kli_hbm, kli_ref),
    )
    copies = [pltpu.make_async_copy(a, b, in_sem.at[n]) for n, (a, b) in enumerate(pairs)]
    for copy in copies:
        copy.start()

    mask_ref[...] = same_group(width, BF16)
    fold_ref[...] = same_group(width, F32)

    def tables(i, at):
        lane_item = iota((tap_count + width, WIDE), 1) % width
        own = slice(i * wide_groups, (i + 1) * wide_groups)
        pick = (iota((wide_groups, WIDE), 1) // width == iota((wide_groups, WIDE), 0)).astype(F32).astype(BF16)
        table = lax.dot_general(taps_ref[own, :], pick, (((0,), (0,)), ((), ())), preferred_element_type=F32)
        table = jnp.concatenate([table, jnp.zeros((width, WIDE), F32)], axis=0)
        step = 1
        while step < width:
            table = jnp.where((lane_item & step) != 0, pltpu.roll(table, step, 0), table)
            step *= 2
        taptab_ref[:, at] = table.astype(BF16)
        rates = expand_groups(rate_ref[...], i * wide_groups, width, lax.Precision.HIGHEST)
        rates_ref[:, at] = rates
        residues_ref[:, at] = expand_groups(residue_ref[...], i * wide_groups, width, lax.Precision.HIGHEST)
        decay_ref[:, at] = jnp.exp(-rates * half)
        left = half - 1.0 - iota((half, WIDE), 0).astype(F32)
        ends_ref[at, :] = jnp.transpose(jnp.exp(-rates_along(rates, width) * left)).astype(BF16)

    def convolve_late(i, at):
        mask = mask_ref[...]
        for first in range(half, rows, width):
            u = tail_ref[first - half : first - half + width, at]
            reached = dot(taptab_ref[: rows - first, at], spread(u, mask))
            acc_ref[first:, at] = acc_ref[first:, at] + reached if first > half else reached

    def convolve_early(i, at):
        mask = mask_ref[...]
        u = k_ref[:, at] * v_ref[:, at]
        acc_ref[:half, at] = jnp.zeros((half, WIDE), F32)
        for first in range(0, half, width):
            count = tap_count + width
            acc_ref[first : first + count, at] += dot(taptab_ref[:, at], spread(u[first : first + width], mask))

    def gate(i, at):
        early, late = acc_ref[:half, at], acc_ref[half:, at]
        part_ref[:, at] = early
        mr = (q_ref[half:, at].astype(F32) * late).astype(BF16)
        mr_ref[:, at] = mr
        u_late = mr * kli_ref[half:, at]
        ulate_ref[:, at] = u_late
        mr_early = (q_ref[:half, at].astype(F32) * early).astype(BF16)
        mr_early_ref[:, at] = mr_early
        u_early = mr_early * kli_ref[:half, at]
        u_early_ref[:, at] = u_early
        ends = ends_ref[at, :]
        late_ref[:, at] = pole_sums(ends, u_late, fold_ref, poles)
        early_ref[:, at] = pole_sums(ends, u_early, fold_ref, poles)

    pipelined(steps, tables)
    pipelined(steps, convolve_late)
    for copy in copies:
        copy.wait()
    pipelined(steps, convolve_early, gate, lag=6)


def near_rows(u_ref, litab_ref, near_ref, mask_ref, width):
    half = u_ref.shape[0]

    def work(i, at):
        mask = mask_ref[...]
        u = u_ref[:, at]
        for first in range(0, half, width):
            reached = dot(litab_ref[: half - first, at], spread(u[first : first + width], mask))
            near_ref[first:half, at] = near_ref[first:half, at] + reached if first else reached

    return work


def filter_kernel(
    rates_ref, residues_ref, late_ref, early_ref, decay_ref, qli_hbm,
    first_ref, litab_ref, powers_ref, scale_ref, qli_ref,
    mask_ref, sem,
):
    half, channels = litab_ref.shape
    poles = rates_ref.shape[0]
    width = CHUNK
    steps = channels // WIDE
    copy = pltpu.make_async_copy(qli_hbm, qli_ref, sem)
    copy.start()
    first_ref[...] = (late_ref[...] + early_ref[...] * decay_ref[...]).astype(BF16)
    mask_ref[...] = same_group(width, BF16)

    def tables(i, at):
        mask = mask_ref[...]
        rates = rates_ref[:, at]
        scale = residues_ref[:, at] * jnp.sqrt(one_minus_exp(2.0 * rates))
        scale_ref[:, at] = scale
        item = (iota((poles, WIDE), 1) % width).astype(F32)
        times = iota((half, WIDE), 0).astype(F32)
        rate_row = rates_along(rates, width)
        power = jnp.exp(-rate_row * times)
        powers_ref[:, at] = (power * jnp.exp(-rate_row)).astype(BF16)
        power_hi, power_lo = split(power)
        lift_hi, lift_lo = split(scale * jnp.exp(rates * item))
        lift_hi, lift_lo = spread(lift_hi, mask), spread(lift_lo, mask)
        li_taps = dot(power_hi, lift_hi) + dot(power_hi, lift_lo) + dot(power_lo, lift_hi)
        causal = iota((half, WIDE), 0) >= iota((half, WIDE), 1) % width
        litab_ref[:, at] = jnp.where(causal, li_taps, 0.0).astype(BF16)

    pipelined(steps, tables)
    copy.wait()


def near_late_kernel(u_ref, litab_ref, near_ref, mask_ref):
    mask_ref[...] = same_group(CHUNK, BF16)
    pipelined(u_ref.shape[1] // WIDE, near_rows(u_ref, litab_ref, near_ref, mask_ref, CHUNK))


def rim_rows(
    rim_ref, part_ref, q_ref, kli_ref, taptab_ref, ends_ref, mr_ref, u_ref, early_ref, mask_ref, fold_ref, acc_ref
):
    half, channels = rim_ref.shape
    width = taptab_ref.shape[0] - half
    poles = early_ref.shape[0]
    mask_ref[...] = same_group(width, BF16)
    fold_ref[...] = same_group(width, F32)

    def convolve(i, at):
        mask = mask_ref[...]
        rim = rim_ref[:, at]
        for first in range(half - width, -1, -width):
            reached = dot(taptab_ref[half - first :, at], spread(rim[first : first + width], mask))
            before_ref = part_ref if first == half - width else acc_ref
            acc_ref[: first + width, at] = before_ref[: first + width, at] + reached

    def gate(i, at):
        mr = (q_ref[:half, at].astype(F32) * acc_ref[:, at]).astype(BF16)
        mr_ref[:, at] = mr
        u = mr * kli_ref[:half, at]
        u_ref[:, at] = u
        early_ref[:, at] = pole_sums(ends_ref[at, :], u, fold_ref, poles)

    pipelined(channels // WIDE, convolve, gate, lag=6)


def rim_kernel(place, late_ref, decay_ref, _after, *refs):
    total_ref, mr_ref, u_ref, early_ref, *scratch = refs[6:]

    def work():
        rim_rows(*refs[:6], mr_ref, u_ref, early_ref, *scratch)
        total_ref[...] = (late_ref[...] + early_ref[...] * decay_ref[...]).astype(total_ref.dtype)

    if place is None:
        work()
    else:
        pl.when(lax.axis_index("ctx") == place)(work)


def joined_kernel(own_ref, before_ref, decay_ref, total_ref):
    decay = decay_ref[...]
    total_ref[...] = (own_ref[...] + before_ref[...].astype(F32) * (decay * decay)).astype(BF16)


def near_kernel(places, *refs):
    sets = [refs[3 * n : 3 * n + 3] for n in range(len(places))]
    (
        rim_ref, part_ref, q_ref, kli_ref, taptab_ref, ends_ref, mr_late_ref, litab_ref,
        early_ref, near_ref, mr_hbm,
        mr_ref, u_ref, mask_ref, fold_ref, acc_ref, sem,
    ) = refs[3 * len(places) :]
    half, channels = u_ref.shape
    copies = (
        pltpu.make_async_copy(mr_late_ref, mr_hbm.at[half:], sem.at[0]),
        pltpu.make_async_copy(mr_ref, mr_hbm.at[:half], sem.at[1]),
    )
    copies[0].start()

    def take(sources):
        for source, target in zip(sources, (mr_ref, u_ref, early_ref)):
            target[...] = source[...]

    if places == (None,):
        take(sets[0])
    else:
        own = (rim_ref, part_ref, q_ref, kli_ref, taptab_ref, ends_ref, mr_ref, u_ref, early_ref, mask_ref, fold_ref, acc_ref)
        at = lax.axis_index("ctx")
        for place, sources in zip(places, sets):
            pl.when(at == place)(functools.partial(take, sources))
        pl.when(at == len(places))(lambda: rim_rows(*own))
    copies[1].start()
    mask_ref[...] = same_group(CHUNK, BF16)
    pipelined(channels // WIDE, near_rows(u_ref, litab_ref, near_ref, mask_ref, CHUNK))
    for copy in copies:
        copy.wait()


def far_kernel(adjacent, *refs):
    (
        q_ref, near_early_ref, near_late_ref, early_ref, powers_ref, decay_ref, scale_ref,
        out_hbm, out_ref, mask_ref, out_sem,
    ) = refs[-11:]
    arrived = refs[:-11]
    half, channels = powers_ref.shape
    steps = channels // WIDE

    def put(i, at):
        return pltpu.make_async_copy(out_ref.at[:, at], out_hbm.at[:, at], out_sem.at[i])

    mask_ref[...] = same_group(early_ref.shape[0], BF16)

    def work(i, at):
        mask = mask_ref[...]
        scale = scale_ref[:, at]
        decay = decay_ref[:, at]
        entering = arrived[-1][:, at].astype(F32)
        for n in range(len(arrived) - 2, -1, -1):
            if n >= adjacent - 1:
                entering = entering * (decay * decay)
            entering = entering + arrived[n][:, at].astype(F32)
        middle = entering * decay + early_ref[:, at]
        powers = powers_ref[:, at]
        for first, state, near_ref in ((0, entering, near_early_ref), (half, middle, near_late_ref)):
            far = dot(powers, spread((state * scale).astype(BF16), mask))
            gate = q_ref[first : first + half, at].astype(F32)
            out_ref[first : first + half, at] = (gate * (near_ref[:, at] + far)).astype(BF16)
        put(i, at).start()

    pipelined(steps, work)
    for i in range(steps):
        put(i, slice(i * WIDE, (i + 1) * WIDE)).wait()


def body(q_mr, k_mr, v_mr, q_li, k_li, mr_taps, li_rate, li_residue):
    rows, channels = q_mr.shape
    groups, tap_count = mr_taps.shape
    poles = li_rate.shape[1]
    width = channels // groups
    half = tap_count
    assert rows == 2 * half and poles == width == CHUNK
    steps = channels // WIDE
    params = pltpu.CompilerParams(vmem_limit_bytes=40 * 1024 * 1024)
    vmem, hbm = pl.BlockSpec(memory_space=pltpu.VMEM), pl.BlockSpec(memory_space=pl.ANY)
    in_hbm = lambda *arrays: [pltpu.with_memory_space_constraint(array, pltpu.HBM) for array in arrays]
    dma = pltpu.SemaphoreType.DMA
    mask, fold = pltpu.VMEM((WIDE, WIDE), BF16), pltpu.VMEM((WIDE, WIDE), F32)
    pole_sum, short, tall = (poles, channels), (half, channels), (rows, channels)

    def call(kernel, name, ins, outs, scratch, flops, *operands):
        return pl.pallas_call(
            kernel,
            in_specs=ins,
            out_specs=[hbm if isinstance(out, jax.ShapeDtypeStruct) else vmem for out in outs],
            out_shape=outs,
            scratch_shapes=scratch,
            cost_estimate=pl.CostEstimate(flops=flops, bytes_accessed=flops // 1000, transcendentals=0),
            compiler_params=params,
            name=name,
        )(*operands)

    peers = lax.axis_size("ctx")
    send = lambda array, *pairs: lax.ppermute(array, "ctx", pairs)
    by_place = peers == 4
    if by_place:
        tails = []
        for place in range(3):
            tails += call(
                functools.partial(tail_kernel, place),
                "tail_rows",
                [vmem if tails else hbm] + [hbm] * 2,
                [pltpu.VMEM(short, BF16)],
                [pltpu.VMEM(short, BF16), pltpu.VMEM(short, BF16), dma((2, 2))],
                10**6,
                tails[-1] if tails else in_hbm(k_mr)[0], *in_hbm(k_mr, v_mr),
            )
        rims = [send(tail, (at, at + 1)) for at, tail in enumerate(tails)]
    else:
        tail = k_mr[half:] * v_mr[half:]
        tails = [tail]
        rims = [shifted(tail, "ctx", 1)]

    mr_late, part, u_late, late, taptab, ends, decay, q, kli, *without_rim, rates, residues = call(
        functools.partial(local_kernel, len(tails)),
        "local_rows",
        [vmem] * (len(tails) + 3) + [hbm] * 4,
        [
            pltpu.VMEM(short, BF16),
            pltpu.VMEM(short, F32),
            pltpu.VMEM(short, BF16),
            pltpu.VMEM(pole_sum, F32),
            pltpu.VMEM((half + width, channels), BF16),
            pltpu.VMEM((channels, half), BF16),
            pltpu.VMEM(pole_sum, F32),
            pltpu.VMEM(tall, BF16),
            pltpu.VMEM(tall, BF16),
            pltpu.VMEM(short, BF16),
            pltpu.VMEM(short, BF16),
            pltpu.VMEM(pole_sum, F32),
            pltpu.VMEM(pole_sum, F32),
            pltpu.VMEM(pole_sum, F32),
        ],
        [
            pltpu.VMEM(short, BF16),
            pltpu.VMEM(short, BF16),
            mask,
            fold,
            pltpu.VMEM(tall, F32),
            dma((4,)),
            *[pltpu.VMEM(short, BF16), dma((2, 2))] * (len(tails) > 1),
        ],
        4 * 10**9,
        *tails, mr_taps, li_rate.T, li_residue.T,
        *in_hbm(q_mr, k_mr, v_mr, k_li),
    )

    first, litab, powers, scale, qli = call(
        filter_kernel,
        "filter_tables",
        [vmem] * 5 + [hbm],
        [
            pltpu.VMEM(pole_sum, BF16),
            pltpu.VMEM(short, BF16),
            pltpu.VMEM(short, BF16),
            pltpu.VMEM(pole_sum, F32),
            pltpu.VMEM(tall, BF16),
        ],
        [mask, dma(())],
        10**6,
        rates, residues, late, without_rim[2], decay, *in_hbm(q_li),
    )
    (near_late,) = call(
        near_late_kernel, "near_late", [vmem] * 2, [pltpu.VMEM(short, F32)], [mask], 10**6, u_late, litab
    )

    before = send(first, (0, 1)) if by_place else None

    own = (part, q, kli, taptab, ends)

    def with_rim(place, rim, after, dtype):
        return call(
            functools.partial(rim_kernel, place),
            "rim_rows",
            [vmem] * 9,
            [
                pltpu.VMEM(pole_sum, dtype),
                pltpu.VMEM(short, BF16),
                pltpu.VMEM(short, BF16),
                pltpu.VMEM(pole_sum, F32),
            ],
            [mask, fold, pltpu.VMEM(short, F32)],
            10**6,
            late, decay, after, rim, *own,
        )

    if by_place:
        total_1, *rim_1 = with_rim(1, rims[0], near_late, F32)
        (total_1,) = call(
            joined_kernel,
            "joined_sums",
            [vmem] * 3,
            [pltpu.VMEM(pole_sum, BF16)],
            [],
            10**6,
            total_1, before, decay,
        )
        two_before = send(total_1, (1, 3))
        one_before = send(total_1, (1, 2))
        total_2, *rim_2 = with_rim(2, rims[1], total_1, BF16)
        entered = before.astype(F32) + one_before.astype(F32) + two_before.astype(F32) * (decay * decay)
        arrived = [entered, send(total_2, (2, 3))]
        early_rows, places = (*without_rim, *rim_1, *rim_2), (0, 1, 2)
    else:
        total, *early_rows = with_rim(None, rims[0], near_late, BF16)
        places = (None,)
        reach = min(3, max(peers - 1, 1))
        arrived = [shifted(total, "ctx", by) for by in range(1, reach + 1)]
        while reach < peers - 1:
            window = arrived[-1].astype(F32)
            for piece in arrived[-2::-1]:
                window = window * jnp.exp(-rates * rows) + piece.astype(F32)
            merged = window
            for times in (1, 2, 3):
                if times * reach < peers:
                    moved = shifted(window, "ctx", times * reach)
                    merged = merged + moved * jnp.exp(-rates * (rows * reach * times))
            arrived = [merged]
            reach *= 4

    early, near_early, mr_out = call(
        functools.partial(near_kernel, places),
        "near_part",
        [vmem] * (len(early_rows) + 8),
        [pltpu.VMEM(pole_sum, F32), pltpu.VMEM(short, F32), jax.ShapeDtypeStruct(tall, BF16)],
        [pltpu.VMEM(short, BF16), pltpu.VMEM(short, BF16), mask, fold, pltpu.VMEM(short, F32), dma((2,))],
        10**6,
        *early_rows, rims[-1], *own, mr_late, litab,
    )

    (li_out,) = call(
        functools.partial(far_kernel, 2 if by_place else 1),
        "far_rows",
        [vmem] * (len(arrived) + 7),
        [jax.ShapeDtypeStruct(tall, BF16)],
        [pltpu.VMEM(tall, BF16), mask, dma((steps,))],
        10**9,
        *arrived, qli, near_early, near_late, early, powers, decay, scale,
    )
    return (mr_out, li_out)


def solution(mesh):
    seq = P(("rep", "ctx"), "tp")
    in_specs = (seq, seq, seq, seq, seq, P("tp", None), P("tp", None), P("tp", None))
    return jax.shard_map(body, mesh=mesh, in_specs=in_specs, out_specs=(seq, seq), check_vma=False)
```
